32 devices in a mesh: wide: 8 (over z, y), narrow: 4 (over x, core).
Axes of the slice: x: 2, y: 2, z: 4, core: 2. Of those that a mesh axis runs over, the one named last changes fastest.
Arguments:
- char_ids: int32 [4096, 50], P(('wide', 'narrow')), may hold values from 0 to 261
- char_mask: int32 [4096, 50], P(('wide', 'narrow')), may hold values 0 or 1
- position_ids: int32 [4096], P(('wide', 'narrow')), may hold values from 0 to 511
- type_ids: int32 [4096], P(('wide', 'narrow')), may hold values from 0 to 1
- key_mask: int32 [8, 512], P('wide'), may hold values from 0 to 1, as said below
- char_table: bfloat16 [262, 16], replicated, may hold values from -6 to 6
- conv_weight: bfloat16 [112, 2048], P(None, ('wide', 'narrow')), may hold values from -0.5 to 0.5
- conv_bias: bfloat16 [2048], P(('wide', 'narrow')), may hold values from -3 to 3
- highway_weight: bfloat16 [2, 2048, 4096], P(None, None, ('wide', 'narrow')), may hold values from -0.125 to 0.125
- highway_bias: bfloat16 [2, 4096], P(None, ('wide', 'narrow')), may hold values from -3 to 3
- proj_weight: bfloat16 [2048, 768], P(None, ('wide', 'narrow')), may hold values from -0.125 to 0.125
- proj_bias: bfloat16 [768], P(('wide', 'narrow')), may hold values from -3 to 3
- position_table: bfloat16 [512, 768], P(None, ('wide', 'narrow')), may hold values from -3 to 3
- type_table: bfloat16 [2, 768], P(None, ('wide', 'narrow')), may hold values from -3 to 3
- embed_gain: bfloat16 [768], P(('wide', 'narrow')), may hold values from 0.5 to 1.5
- embed_shift: bfloat16 [768], P(('wide', 'narrow')), may hold values from -2 to 2
- qkv_weight: bfloat16 [3, 768, 768], P(None, None, 'narrow'), may hold values from -0.21875 to 0.21875
- qv_bias: bfloat16 [2, 768], P(None, 'narrow'), may hold values from -3 to 3
- out_weight: bfloat16 [768, 768], P('narrow'), may hold values from -0.875 to 0.875
- out_bias: bfloat16 [768], replicated, may hold values from -3 to 3
- ln1_gain: bfloat16 [768], replicated, may hold values from 0.5 to 1.5
- ln1_shift: bfloat16 [768], replicated, may hold values from -2 to 2
- up_weight: bfloat16 [768, 3072], P(None, 'narrow'), may hold values from -0.21875 to 0.21875
- up_bias: bfloat16 [3072], P('narrow'), may hold values from -3 to 3
- down_weight: bfloat16 [3072, 768], P('narrow'), may hold values from -0.109375 to 0.109375
- down_bias: bfloat16 [768], replicated, may hold values from -3 to 3
- ln2_gain: bfloat16 [768], replicated, may hold values from 0.5 to 1.5
- ln2_shift: bfloat16 [768], replicated, may hold values from -2 to 2
- cotangent: float32 [4096, 768], P(('wide', 'narrow')), may hold values from -6 to 6
Outputs:
- layer_out: float32 [4096, 768], P(('wide', 'narrow'))
- char_table_grad: float32 [262, 16], replicated
- conv_weight_grad: float32 [112, 2048], P(None, ('wide', 'narrow'))
- conv_bias_grad: float32 [2048], P(('wide', 'narrow'))
- highway_weight_grad: float32 [2, 2048, 4096], P(None, None, ('wide', 'narrow'))
- highway_bias_grad: float32 [2, 4096], P(None, ('wide', 'narrow'))
- proj_weight_grad: float32 [2048, 768], P(None, ('wide', 'narrow'))
- proj_bias_grad: float32 [768], P(('wide', 'narrow'))
- position_table_grad: float32 [512, 768], P(None, ('wide', 'narrow'))
- type_table_grad: float32 [2, 768], P(None, ('wide', 'narrow'))
- embed_gain_grad: float32 [768], P(('wide', 'narrow'))
- embed_shift_grad: float32 [768], P(('wide', 'narrow'))
- qkv_weight_grad: float32 [3, 768, 768], P(None, None, 'narrow')
- qv_bias_grad: float32 [2, 768], P(None, 'narrow')
- out_weight_grad: float32 [768, 768], P('narrow')
- out_bias_grad: float32 [768], replicated
- ln1_gain_grad: float32 [768], replicated
- ln1_shift_grad: float32 [768], replicated
- up_weight_grad: float32 [768, 3072], P(None, 'narrow')
- up_bias_grad: float32 [3072], P('narrow')
- down_weight_grad: float32 [3072, 768], P('narrow')
- down_bias_grad: float32 [768], replicated
- ln2_gain_grad: float32 [768], replicated
- ln2_shift_grad: float32 [768], replicated
The draws below stay inside these ranges and needn't reach their ends.
Inputs may be any that keep to these rules, and one draw needn't show every extreme that they name: `key_mask`: the ones of each sequence form a prefix that covers half of its 512 words or more.
All inputs are finite; a program needn't handle non-finite values. No bound on the sum of `char_mask` on one device may be relied on, other than what follows from the above.
Results may differ from the reference program's by a relative error of at most 0.02.
Values may be sent and summed in bfloat16 or wider, within the bound.
No kernel may reach another device: no remote copies, remote signals or barrier semaphores. Data moves between devices by JAX's collectives and lax.ppermute only.
A program may use at most 320 MiB of HBM per device.

```python
import math
import jax
import jax.numpy as jnp
import numpy as np
from jax import lax

D = 768
HEADS = 12
HEAD_DIM = 64
FF = 3072
CHAR_VOCAB = 262
CHAR_DIM = 16
FILTERS = 2048
WORD_CHARS = 50
LEN = 512
TAPS = 7
SEQS = 1
SEQUENCES = 8
TOKENS = 4096
N_WIDE = 8


def draw_key_mask(key, part):
    key = jax.random.fold_in(key, 11)
    lengths = jax.random.randint(key, (SEQUENCES, 1), LEN // 2, LEN + 1)
    return (jnp.arange(LEN)[None, :] < lengths).astype(jnp.int32)


def plant(values, key, smallest, high):
    shape = values.shape
    index_at = [jax.random.randint(jax.random.fold_in(key, axis), (), 0, shape[axis]) for axis in range(len(shape))]
    values = values.at[tuple(index_at)].set(smallest)
    longest = shape.index(max(shape))
    index_at[longest] = (index_at[longest] + 1) % shape[longest]
    return values.at[tuple(index_at)].set(high)


def block_levels(own_key, shape, cuts, least, largest):
    def one(position, blocks):
        draws = jax.random.uniform(jax.random.fold_in(jax.random.fold_in(own_key, 6), position), (blocks,), jnp.float32, least / len(cuts), largest / len(cuts))
        return jnp.repeat(jnp.exp(draws), shape[position] // blocks).reshape((-1,) + (1,) * (len(shape) - position - 1))

    level = one(*cuts[0])
    for cut in cuts[1:]:
        level = level * one(*cut)
    return level


def cumulative_ranks(amount, slope):
    portions = [(1 << 20) // math.isqrt(standing ** slope) + 1 for standing in range(1, amount + 1)]
    deviation = 1 + sum(portions) // (1 << 30)
    return np.cumsum(np.array([max(1, weight // deviation) for weight in portions]))


def ranked(key, extent, number_of, lean):
    listing = cumulative_ranks(number_of, lean)
    ticket = jax.random.randint(jax.random.fold_in(key, 1), extent, 0, int(listing[number_of - 1]))
    grade = jnp.searchsorted(jnp.asarray(listing, jnp.int32), ticket, side="right")
    return jax.random.permutation(jax.random.fold_in(key, 2), number_of)[grade].astype(jnp.int32)


def scatter_about(own_key, shape, deviation, limit, cuts=(), kind=jnp.bfloat16):
    loudness = block_levels(own_key, shape, cuts, -0.22, 0.18) if cuts else 1.0
    values = jax.random.normal(own_key, shape, jnp.float32) * deviation * loudness
    return jnp.minimum(jnp.maximum(values, -limit), limit).astype(kind)


def setup_inputs(seed: int = 0) -> dict:
    key_list = jax.random.split(jax.random.key(seed), 30)
    return {
        "char_ids": plant(ranked(key_list[0], (TOKENS, WORD_CHARS), CHAR_VOCAB, 2), jax.random.fold_in(key_list[0], 3), 0, CHAR_VOCAB - 1).astype(jnp.int32),
        "char_mask": plant((jax.random.randint(key_list[1], (TOKENS, WORD_CHARS), 0, 4) < 3).astype(jnp.int32), jax.random.fold_in(key_list[1], 1), 0, 1),
        "position_ids": plant(jax.random.randint(key_list[2], (TOKENS,), 0, LEN), jax.random.fold_in(key_list[2], 1), 0, LEN - 1).astype(jnp.int32),
        "type_ids": plant(jax.random.randint(key_list[3], (TOKENS,), 0, 2), jax.random.fold_in(key_list[3], 1), 0, 1).astype(jnp.int32),
        "key_mask": draw_key_mask(jax.random.fold_in(key_list[29], 71), 0),
        "char_table": scatter_about(key_list[5], (CHAR_VOCAB, CHAR_DIM), 1.0, 6.0),
        "conv_weight": scatter_about(key_list[6], (TAPS * CHAR_DIM, FILTERS), (TAPS * CHAR_DIM) ** -0.5, 0.5, ((1, 32),)),
        "conv_bias": scatter_about(key_list[7], (FILTERS,), 0.5, 3.0, ((0, 32),)),
        "highway_weight": scatter_about(key_list[8], (2, FILTERS, 2 * FILTERS), FILTERS ** -0.5, 0.125, ((2, 32),)),
        "highway_bias": scatter_about(key_list[9], (2, 2 * FILTERS), 0.5, 3.0, ((1, 32),)),
        "proj_weight": scatter_about(key_list[10], (FILTERS, D), FILTERS ** -0.5, 0.125, ((1, 32),)),
        "proj_bias": scatter_about(key_list[11], (D,), 0.5, 3.0, ((0, 32),)),
        "position_table": scatter_about(key_list[12], (LEN, D), 0.5, 3.0, ((1, 32),)),
        "type_table": scatter_about(key_list[13], (2, D), 0.5, 3.0, ((1, 32),)),
        "embed_gain": jnp.clip(1.0 + 0.1 * jax.random.normal(key_list[14], (D,), jnp.float32), 0.5, 1.5).astype(jnp.bfloat16),
        "embed_shift": scatter_about(key_list[15], (D,), 0.3, 2.0, ((0, 32),)),
        "qkv_weight": scatter_about(key_list[16], (3, D, D), D ** -0.5, 0.21875, ((2, 4),)),
        "qv_bias": scatter_about(key_list[17], (2, D), 0.5, 3.0, ((1, 4),)),
        "out_weight": scatter_about(key_list[18], (D, D), (D // 16) ** -0.5, 0.875, ((0, 4),)),
        "out_bias": scatter_about(key_list[19], (D,), 0.5, 3.0),
        "ln1_gain": jnp.clip(1.0 + 0.1 * jax.random.normal(key_list[20], (D,), jnp.float32), 0.5, 1.5).astype(jnp.bfloat16),
        "ln1_shift": scatter_about(key_list[21], (D,), 0.3, 2.0),
        "up_weight": scatter_about(key_list[22], (D, FF), D ** -0.5, 0.21875, ((1, 4),)),
        "up_bias": scatter_about(key_list[23], (FF,), 0.5, 3.0, ((0, 4),)),
        "down_weight": scatter_about(key_list[24], (FF, D), FF ** -0.5, 0.109375, ((0, 4),)),
        "down_bias": scatter_about(key_list[25], (D,), 0.5, 3.0),
        "ln2_gain": jnp.clip(1.0 + 0.1 * jax.random.normal(key_list[26], (D,), jnp.float32), 0.5, 1.5).astype(jnp.bfloat16),
        "ln2_shift": scatter_about(key_list[27], (D,), 0.3, 2.0),
        "cotangent": scatter_about(key_list[28], (TOKENS, D), 1.0, 6.0, ((0, 32),), jnp.float32),
    }


HIGHEST = lax.Precision.HIGHEST
EPSILON = 1e-05
NEG_FILL = -1000000000.0

@jax.custom_vjp
def low(v):
    return lax.optimization_barrier(v.astype(jnp.bfloat16)).astype(jnp.float32)

@jax.custom_vjp
def low_back(v):
    return v

def low_keep(v):
    return (low(v), None)

def low_pass(kept, grad):
    return (grad,)

def back_keep(v):
    return (v, None)

def back_low(kept, grad):
    return (low(grad),)
low.defvjp(low_keep, low_pass)
low_back.defvjp(back_keep, back_low)

def matmul(left, right):
    return jnp.dot(left, right, precision=HIGHEST, preferred_element_type=jnp.float32)

def layer_norm(values, gain, shift):
    centre = values - lax.optimization_barrier(jnp.mean(values, axis=-1, keepdims=True))
    spread = lax.optimization_barrier(jnp.mean(centre * centre, axis=-1, keepdims=True))
    return centre * lax.rsqrt(spread + EPSILON) * gain + shift

def smooth_gelu(values):
    return jax.nn.gelu(values, approximate=False)

def filter_widths(filter_total):
    index = jnp.arange(filter_total)
    widths = jnp.ones((filter_total,), jnp.int32)
    for level in range(6):
        widths = widths + (index >= filter_total * 2 ** level // 64).astype(jnp.int32)
    return widths

def tap_mask(widths):
    tap_index = jnp.arange(TAPS * CHAR_DIM) // CHAR_DIM
    return tap_index[:, None] < widths[None, :]

def pool_masks(word_mask, widths):
    letters = word_mask.shape[1]
    place = jnp.arange(letters)
    usable = (word_mask == 1) | (place[None, :] == 0)
    valid_mask = usable[:, :, None] & (place[None, :, None] <= letters - widths[None, None, :])
    valid_count = lax.optimization_barrier(jnp.sum(valid_mask.astype(jnp.float32), axis=1))
    return (valid_mask, valid_count)

def char_block(word_ids, word_mask, table, conv_masked, conv_shift, widths):
    letters = word_ids.shape[1]
    embedded = table[word_ids]
    padded = jnp.pad(embedded, ((0, 0), (0, TAPS), (0, 0)))
    columns = jnp.concatenate([padded[:, offset:offset + letters] for offset in range(TAPS)], axis=-1)
    conv_out = low_back(jnp.einsum('bcx,xf->bcf', columns, conv_masked, precision=HIGHEST))
    valid_mask, valid_count = pool_masks(word_mask, widths)
    pooled = jax.nn.logsumexp(conv_out, axis=1, where=valid_mask) - jnp.log(valid_count) + conv_shift
    return smooth_gelu(pooled)

def embed_group(weights, word_ids, word_mask, place_ids, kind_ids):
    table, conv_weight, conv_bias, highway_weight, highway_bias, proj_weight, proj_bias, position_table, type_table, embed_gain, embed_shift = weights[:11]
    widths = filter_widths(FILTERS)
    conv_masked = conv_weight * tap_mask(widths).astype(jnp.float32)
    word_total = word_ids.shape[0]
    block_words = 128 if word_total % 128 == 0 else word_total
    block_count = word_total // block_words
    mapper = jax.checkpoint(lambda block_pair: char_block(block_pair[0], block_pair[1], table, conv_masked, conv_bias, widths))
    features = lax.map(mapper, (word_ids.reshape(block_count, block_words, WORD_CHARS), word_mask.reshape(block_count, block_words, WORD_CHARS)))
    hidden = features.reshape(word_total, FILTERS)
    for layer_index in range(2):
        mixture = low_back(matmul(low(hidden), highway_weight[layer_index]) + highway_bias[layer_index])
        nonlinear = smooth_gelu(mixture[:, :FILTERS])
        opening = jax.nn.sigmoid(mixture[:, FILTERS:])
        hidden = opening * hidden + (1.0 - opening) * nonlinear
    projected = low_back(matmul(low(hidden), proj_weight) + proj_bias)
    summed = projected + position_table[place_ids] + type_table[kind_ids]
    return layer_norm(summed, embed_gain, embed_shift)

def encoder_group(weights, first_state, keep_mask):
    qkv_weight, qv_bias, out_weight, out_bias, ln1_gain, ln1_shift, up_weight, up_bias, down_weight, down_bias, ln2_gain, ln2_shift = weights[11:]
    group_rows = first_state.shape[0]
    seq_shape = (SEQS, LEN, HEADS, HEAD_DIM)
    rows_low = low(first_state)
    query_heads = low(low_back(matmul(rows_low, qkv_weight[0]) + qv_bias[0])).reshape(seq_shape)
    key_heads = low(low_back(matmul(rows_low, qkv_weight[1]))).reshape(seq_shape)
    value_heads = low(low_back(matmul(rows_low, qkv_weight[2]) + qv_bias[1])).reshape(seq_shape)
    scores = jnp.einsum('sqhd,skhd->shqk', query_heads, key_heads, precision=HIGHEST) * HEAD_DIM ** (-0.5)
    scores = low_back(jnp.where(keep_mask[:, None, None, :] == 1, scores, NEG_FILL))
    attn_weights = low(jax.nn.softmax(scores, axis=-1))
    context = low(low_back(jnp.einsum('shqk,skhd->sqhd', attn_weights, value_heads, precision=HIGHEST)))
    context = context.reshape(group_rows, D)
    attn_branch = low_back(matmul(context, out_weight) + out_bias)
    second_state = layer_norm(first_state + attn_branch, ln1_gain, ln1_shift)
    up_value = low_back(matmul(low(second_state), up_weight) + up_bias)
    activated = low(smooth_gelu(up_value))
    ffn_branch = low_back(matmul(activated, down_weight) + down_bias)
    return layer_norm(second_state + ffn_branch, ln2_gain, ln2_shift)

def reference(char_ids, char_mask, position_ids, type_ids, key_mask, char_table, conv_weight, conv_bias, highway_weight, highway_bias, proj_weight, proj_bias, position_table, type_table, embed_gain, embed_shift, qkv_weight, qv_bias, out_weight, out_bias, ln1_gain, ln1_shift, up_weight, up_bias, down_weight, down_bias, ln2_gain, ln2_shift, cotangent):
    weights_all = tuple((item.astype(jnp.float32) for item in (char_table, conv_weight, conv_bias, highway_weight, highway_bias, proj_weight, proj_bias, position_table, type_table, embed_gain, embed_shift, qkv_weight, qv_bias, out_weight, out_bias, ln1_gain, ln1_shift, up_weight, up_bias, down_weight, down_bias, ln2_gain, ln2_shift)))
    group_size = SEQS * LEN
    group_inputs = (char_ids.reshape(N_WIDE, group_size, WORD_CHARS), char_mask.reshape(N_WIDE, group_size, WORD_CHARS), position_ids.reshape(N_WIDE, group_size), type_ids.reshape(N_WIDE, group_size), key_mask.reshape(N_WIDE, SEQS, LEN), cotangent.astype(jnp.float32).reshape(N_WIDE, group_size, D))

    def group_step(running, one_group):
        word_ids, word_mask, place_ids, kind_ids, keep_mask, grad_out = one_group

        def forward(*weights):
            first_state = embed_group(weights, word_ids, word_mask, place_ids, kind_ids)
            return encoder_group(weights, first_state, keep_mask)
        group_out, pull_back = jax.vjp(forward, *weights_all)
        gradients = pull_back(grad_out)
        return (tuple((total_part + new_part for total_part, new_part in zip(running, gradients))), group_out)
    start_sums = tuple((jnp.zeros(item.shape, jnp.float32) for item in weights_all))
    summed_grads, outputs = lax.scan(group_step, start_sums, group_inputs)
    return (outputs.reshape(TOKENS, D), summed_grads[0], summed_grads[1], summed_grads[2], summed_grads[3], summed_grads[4], summed_grads[5], summed_grads[6], summed_grads[7], summed_grads[8], summed_grads[9], summed_grads[10], summed_grads[11], summed_grads[12], summed_grads[13], summed_grads[14], summed_grads[15], summed_grads[16], summed_grads[17], summed_grads[18], summed_grads[19], summed_grads[20], summed_grads[21], summed_grads[22])
```

```python
import functools

import jax
import jax.numpy as jnp
from jax import lax
from jax.experimental import pallas as pl
from jax.experimental.pallas import tpu as pltpu
from jax.sharding import PartitionSpec as P

HEAD_DIM = 64
EPSILON = 1e-05
NEG_FILL = -1000000000.0
SHUT = -1e30
LANES = 128


def layer_norm(values, gain, shift):
    centre = values - jnp.mean(values, axis=-1, keepdims=True)
    spread = jnp.mean(centre * centre, axis=-1, keepdims=True)
    return centre * lax.rsqrt(spread + EPSILON) * gain + shift


def smooth_gelu(values):
    return jax.nn.gelu(values, approximate=False)


def low(values):
    return values.astype(jnp.bfloat16)


def full(values):
    return values.astype(jnp.float32)


def filter_widths(filter_total):
    index = jnp.arange(filter_total)
    widths = jnp.ones((filter_total,), jnp.int32)
    for level in range(6):
        widths = widths + (index >= filter_total * 2**level // 64).astype(jnp.int32)
    return widths


def highway_mix(hidden, mixture):
    width_half = hidden.shape[1]
    nonlinear = smooth_gelu(mixture[:, :width_half])
    opening = jax.nn.sigmoid(mixture[:, width_half:])
    return opening * hidden + (1.0 - opening) * nonlinear


def swap(block, axis, bit):
    size = lax.axis_size(axis)
    return lax.ppermute(block, axis, [(i, i ^ (1 << bit)) for i in range(size)])


def my_bit(axis, bit):
    return (lax.axis_index(axis) >> bit) & 1


def bits_of(axis):
    return [(axis, bit) for bit in range(lax.axis_size(axis).bit_length() - 1)]


def spread(block, bits):
    shape = block.shape
    held = block[None]
    for axis, bit in bits:
        other = swap(held, axis, bit)
        high = my_bit(axis, bit) == 1
        held = jnp.stack([jnp.where(high, other, held), jnp.where(high, held, other)], axis=1)
        held = held.reshape((-1,) + shape)
    return held


def fold(parts, bits):
    shape = parts.shape[1:]
    for axis, bit in bits:
        pairs = parts.reshape((-1, 2) + shape)
        mine = my_bit(axis, bit)
        kept = lax.dynamic_index_in_dim(pairs, mine, 1, keepdims=False)
        sent = low(lax.dynamic_index_in_dim(pairs, 1 - mine, 1, keepdims=False))
        parts = full(kept) + full(swap(sent, axis, bit))
    return parts[0]


def total(value, bits):
    for axis, bit in bits:
        value = value + swap(value, axis, bit)
    return value


def dot_nt(left, right):
    return lax.dot_general(left, right, (((1,), (1,)), ((), ())), preferred_element_type=jnp.float32)


def pool_kernel(cols_ref, filt_ref, lse_ref, *, group):
    letters = cols_ref.shape[0]
    filt = filt_ref[...]
    peak = None
    for first in range(0, letters, group):
        scores = [dot_nt(cols_ref[p], filt) for p in range(first, min(first + group, letters))]
        top = functools.reduce(jnp.maximum, scores)
        if peak is None:
            peak = top
            mass = functools.reduce(jnp.add, [jnp.exp(s - peak) for s in scores])
        else:
            later = jnp.maximum(peak, top)
            fresh = functools.reduce(jnp.add, [jnp.exp(s - later) for s in scores])
            mass = mass * jnp.exp(peak - later) + fresh
            peak = later
    lse_ref[...] = peak + jnp.log(mass)


def pool_forward(columns, filt_rows, block=256):
    letters, words, depth = columns.shape
    filters = filt_rows.shape[0]
    return pl.pallas_call(
        functools.partial(pool_kernel, group=5),
        grid=(filters // block,),
        in_specs=[
            pl.BlockSpec(columns.shape, lambda i: (0, 0, 0)),
            pl.BlockSpec((block, depth), lambda i: (i, 0)),
        ],
        out_specs=pl.BlockSpec((words, block), lambda i: (0, i)),
        out_shape=jax.ShapeDtypeStruct((words, filters), jnp.float32),
        compiler_params=pltpu.CompilerParams(vmem_limit_bytes=48 * 2**20),
        cost_estimate=pl.CostEstimate(
            flops=2 * letters * words * depth * filters,
            bytes_accessed=4 * words * filters,
            transcendentals=letters * words * filters,
        ),
        name="pool_forward",
    )(columns, filt_rows)


def back_kernel(
    cols_ref, cols_t_ref, hot_ref, filt_ref, lse_ref, grad_ref, dw_ref, table_ref, gcol_ref, *, depth, taps
):
    letters, words, lanes = cols_ref.shape
    step = pl.program_id(0)
    filt = filt_ref[...]
    lse = lse_ref[...]
    grad = grad_ref[...]

    @pl.when(step == 0)
    def _():
        gcol_ref[...] = jnp.zeros_like(gcol_ref)

    half = letters // 2
    weight_sum = jnp.zeros((lanes, filt.shape[0]), jnp.float32)
    for first, last in ((0, half), (half, letters)):
        slots = jnp.concatenate(
            [low(grad * jnp.exp(dot_nt(cols_ref[p], filt) - lse)) for p in range(first, last)], axis=0
        )
        at = slice(first * words, last * words)
        gcol_ref[at, :] += jnp.dot(slots, filt, preferred_element_type=jnp.float32)
        weight_sum += jnp.dot(cols_t_ref[:, at], slots, preferred_element_type=jnp.float32)
    dw_ref[...] = weight_sum.T

    @pl.when(step == pl.num_programs(0) - 1)
    def _():
        tap = lax.broadcasted_iota(jnp.int32, (words, lanes), 1) // depth
        table_ref[...] = jnp.zeros_like(table_ref)
        for c in range(letters):
            moved = jnp.where(tap == 0, gcol_ref[c * words : (c + 1) * words, :], 0.0)
            for t in range(1, min(taps, c + 1)):
                moved = jnp.where(tap == t, gcol_ref[(c - t) * words : (c - t + 1) * words, :], moved)
            table_ref[...] += jnp.dot(
                hot_ref[:, c * words : (c + 1) * words], low(moved), preferred_element_type=jnp.float32
            )


def pool_backward(columns, columns_t, hot, filt_rows, lse, grad, depth, taps, block=256):
    letters, words, lanes = columns.shape
    filters = filt_rows.shape[0]
    whole = lambda item: pl.BlockSpec(item.shape, lambda i: (0,) * item.ndim)
    return pl.pallas_call(
        functools.partial(back_kernel, depth=depth, taps=taps),
        grid=(filters // block,),
        in_specs=[
            whole(columns),
            whole(columns_t),
            whole(hot),
            pl.BlockSpec((block, lanes), lambda i: (i, 0)),
            pl.BlockSpec((words, block), lambda i: (0, i)),
            pl.BlockSpec((words, block), lambda i: (0, i)),
        ],
        out_specs=[
            pl.BlockSpec((block, lanes), lambda i: (i, 0)),
            pl.BlockSpec((hot.shape[0], lanes), lambda i: (0, 0)),
        ],
        out_shape=[
            jax.ShapeDtypeStruct((filters, lanes), jnp.float32),
            jax.ShapeDtypeStruct((hot.shape[0], lanes), jnp.float32),
        ],
        scratch_shapes=[pltpu.VMEM((letters * words, lanes), jnp.float32)],
        compiler_params=pltpu.CompilerParams(vmem_limit_bytes=48 * 2**20),
        cost_estimate=pl.CostEstimate(
            flops=6 * letters * words * lanes * filters,
            bytes_accessed=8 * words * filters,
            transcendentals=letters * words * filters,
        ),
        name="pool_backward",
    )(columns, columns_t, hot, filt_rows, lse, grad)


def masked_scores(query_heads, key_heads, keep_mask, score_scale):
    scores = (
        jnp.einsum("qhd,khd->hqk", query_heads, key_heads, preferred_element_type=jnp.float32)
        * score_scale
    )
    return jnp.where(keep_mask[None, None, :] == 1, scores, NEG_FILL)


def attend(query_heads, key_heads, value_heads, keep_mask, score_scale):
    scores = masked_scores(query_heads, key_heads, keep_mask, score_scale)
    row_peak = jnp.max(scores, axis=-1, keepdims=True)
    raised = jnp.exp(scores - row_peak)
    row_total = jnp.sum(raised, axis=-1, keepdims=True)
    attn_weights = (raised / row_total).astype(jnp.bfloat16)
    context = jnp.einsum(
        "hqk,khd->qhd", attn_weights, value_heads, preferred_element_type=jnp.float32
    )
    return (context.astype(jnp.bfloat16), row_peak, row_total)


def attend_back(
    query_heads, key_heads, value_heads, keep_mask, row_peak, row_total, grad_context, score_scale
):
    scores = masked_scores(query_heads, key_heads, keep_mask, score_scale)
    probs_full = jnp.exp(scores - row_peak) / row_total
    attn_weights = probs_full.astype(jnp.bfloat16)
    grad_value = jnp.einsum(
        "hqk,qhd->khd", attn_weights, grad_context, preferred_element_type=jnp.float32
    )
    grad_weights = jnp.einsum(
        "qhd,khd->hqk", grad_context, value_heads, preferred_element_type=jnp.float32
    )
    inner_sum = jnp.sum(grad_weights * probs_full, axis=-1, keepdims=True)
    grad_scores = (probs_full * (grad_weights - inner_sum)).astype(jnp.bfloat16)
    grad_query = (
        jnp.einsum("hqk,khd->qhd", grad_scores, key_heads, preferred_element_type=jnp.float32)
        * score_scale
    )
    grad_key = (
        jnp.einsum("hqk,qhd->khd", grad_scores, query_heads, preferred_element_type=jnp.float32)
        * score_scale
    )
    return (
        grad_query.astype(jnp.bfloat16),
        grad_key.astype(jnp.bfloat16),
        grad_value.astype(jnp.bfloat16),
    )


def per_device(
    char_ids,
    char_mask,
    position_ids,
    type_ids,
    key_mask,
    char_table,
    conv_weight,
    conv_bias,
    highway_weight,
    highway_bias,
    proj_weight,
    proj_bias,
    position_table,
    type_table,
    embed_gain,
    embed_shift,
    qkv_weight,
    qv_bias,
    out_weight,
    out_bias,
    ln1_gain,
    ln1_shift,
    up_weight,
    up_bias,
    down_weight,
    down_bias,
    ln2_gain,
    ln2_shift,
    cotangent,
):
    n_wide, n_narrow = lax.axis_size("wide"), lax.axis_size("narrow")
    half_wide = n_wide // 2
    me_narrow = lax.axis_index("narrow")
    wide_bits, narrow_bits = bits_of("wide"), bits_of("narrow")
    every_bit = narrow_bits + wide_bits
    falling = every_bit[::-1]
    word_total, letters = char_ids.shape
    tap_rows, own_filters = conv_weight.shape
    char_depth = char_table.shape[1]
    tap_count = tap_rows // char_depth
    filters = highway_weight.shape[1]
    own_mix = highway_weight.shape[2]
    own_width = proj_weight.shape[1]
    seq_length = position_table.shape[0]
    group = word_total * n_narrow
    own_hidden = half_wide * own_mix

    conv_block = jnp.zeros((own_filters, LANES), jnp.bfloat16)
    conv_block = conv_block.at[:, :tap_rows].set(conv_weight.T)
    conv_block = conv_block.at[:, tap_rows + tap_count].set(conv_bias)
    bias_block = jnp.pad(highway_bias, ((0, 0), (0, LANES - own_mix)))
    conv_spread = spread(jnp.concatenate([conv_block, bias_block]), falling)
    filt_rows = conv_spread[:, :own_filters].reshape(filters, LANES)
    mix_bias = conv_spread[:, own_filters:, :own_mix].reshape(n_wide, n_narrow, 2, own_mix)
    mix_bias = full(lax.dynamic_index_in_dim(mix_bias, me_narrow, 1, keepdims=False))
    mix_bias = mix_bias.transpose(1, 0, 2).reshape(2, n_wide * own_mix)
    second_rows = (
        highway_weight[1]
        .reshape(half_wide, n_narrow, own_mix, own_mix)
        .transpose(1, 0, 2, 3)
        .reshape(filters, own_mix)
    )
    mix_weights = [
        lax.all_gather(highway_weight[0], "wide", axis=1, tiled=True),
        lax.all_gather(second_rows, "wide", axis=1, tiled=True),
    ]
    vector_block = jnp.stack([proj_bias, type_table[0], type_table[1], embed_gain, embed_shift], axis=1)
    vector_block = jnp.pad(vector_block, ((0, 0), (0, LANES - vector_block.shape[1])))
    rest = spread(jnp.concatenate([proj_weight.T, position_table.T, vector_block], axis=1), falling)
    rest = rest.reshape(n_wide * n_narrow * own_width, -1)
    model_width = rest.shape[0]
    proj_rows = rest[:, :filters].reshape(model_width, half_wide, n_narrow, own_mix)
    proj_own = lax.dynamic_index_in_dim(proj_rows, me_narrow, 2, keepdims=False)
    proj_own = proj_own.reshape(model_width, own_hidden)
    position_rows = rest[:, filters : filters + seq_length]
    vectors = full(rest[:, filters + seq_length :].T)
    proj_shift, type_low, type_high, first_gain, first_shift = (vectors[i] for i in range(5))

    widths = filter_widths(filters)
    lane = jnp.arange(LANES)
    tap_keep = (lane[None, :] // char_depth) < widths[:, None]
    late = lane - tap_rows
    shut = (late == 0)[None, :] | (
        (late >= 1)[None, :] & (late < tap_count)[None, :] & (widths[:, None] > late[None, :])
    )
    is_bias = (late == tap_count)[None, :]
    filt_rows = jnp.where(
        (tap_keep & (late < 0)[None, :]) | is_bias,
        filt_rows,
        jnp.where(shut, jnp.bfloat16(SHUT), jnp.bfloat16(0.0)),
    )
    vocab = char_table.shape[0]
    vocab_rows = -(-vocab // 16) * 16
    id_row = char_ids.T.reshape(1, letters * word_total)
    hot = (jnp.arange(vocab_rows)[:, None] == id_row).astype(jnp.bfloat16)
    table_t = jnp.pad(char_table, ((0, vocab_rows - vocab), (0, 0))).T
    embedded = low(jnp.dot(table_t, hot, preferred_element_type=jnp.float32))
    embedded = jnp.pad(embedded, ((0, 0), (0, tap_count * word_total)))
    span = letters * word_total
    tap_blocks = [embedded[:, t * word_total : t * word_total + span] for t in range(tap_count)]
    place = jnp.arange(letters)
    usable = (char_mask == 1) | (place[None, :] == 0)
    unusable_row = low(~usable).T.reshape(1, span)
    late_rows = low(place[None, :] == letters - jnp.arange(1, tap_count)[:, None])
    late_rows = jnp.repeat(late_rows, word_total, axis=1)
    columns_t = jnp.concatenate(
        tap_blocks
        + [
            unusable_row,
            late_rows,
            jnp.ones((1, span), jnp.bfloat16),
            jnp.zeros((LANES - tap_rows - tap_count - 1, span), jnp.bfloat16),
        ]
    )
    columns = columns_t.T.reshape(letters, word_total, LANES)
    tally = jnp.stack(
        [jnp.sum(full(usable[:, : letters - w + 1]), axis=1) for w in range(1, tap_count + 1)], axis=1
    )
    width_hot = full(jnp.arange(1, tap_count + 1)[:, None] == widths[None, :])
    valid_count = jnp.dot(tally, width_hot)

    lse = pool_forward(columns, filt_rows)
    pooled = lse - jnp.log(valid_count)
    features = low(smooth_gelu(pooled))

    first_low = spread(features, narrow_bits[::-1]).reshape(group, filters)
    first_own = lax.dynamic_index_in_dim(
        first_low.reshape(group, half_wide, n_narrow, own_mix), me_narrow, 2, keepdims=False
    )
    hidden = full(first_own.reshape(group, own_hidden))
    low_input = first_low
    highway_saved = []
    for layer_index in range(2):
        mixture = jnp.dot(low_input, mix_weights[layer_index], preferred_element_type=jnp.float32)
        mixture = mixture + mix_bias[layer_index]
        highway_saved.append((hidden, low_input, mixture))
        hidden = highway_mix(hidden, mixture)
        if layer_index == 0:
            blocks = spread(low(hidden), narrow_bits[::-1])
            low_input = jnp.concatenate([blocks[m] for m in range(n_narrow)], axis=1)
    proj_input = low(hidden)
    projected = fold(dot_nt(proj_input, proj_own).reshape(n_narrow, word_total, model_width), narrow_bits)
    position_hot = (position_ids[:, None] == jnp.arange(seq_length)[None, :]).astype(jnp.bfloat16)
    type_rows = jnp.where(type_ids[:, None] == 1, type_high, type_low)
    summed = projected + proj_shift + dot_nt(position_hot, position_rows) + type_rows
    first_state, first_pull = jax.vjp(layer_norm, summed, first_gain, first_shift)

    gathered = lax.all_gather(low(first_state), "narrow", axis=0, tiled=True)
    group_rows = gathered.shape[0]
    qkv_out = jnp.einsum("gd,kdc->kgc", gathered, qkv_weight, preferred_element_type=jnp.float32)
    local_width = qkv_out.shape[2]
    head_count = local_width // HEAD_DIM
    seq_shape = (group_rows, head_count, HEAD_DIM)
    query_heads = low(qkv_out[0] + full(qv_bias[0])).reshape(seq_shape)
    key_heads = low(qkv_out[1]).reshape(seq_shape)
    value_heads = low(qkv_out[2] + full(qv_bias[1])).reshape(seq_shape)
    score_scale = HEAD_DIM ** (-0.5)
    keep_mask = key_mask[0]
    context, row_peak, row_total = attend(query_heads, key_heads, value_heads, keep_mask, score_scale)
    context_rows = context.reshape(group_rows, local_width)

    def by_owner(partial):
        return fold(partial.reshape(n_narrow, word_total, model_width), narrow_bits)

    attn_branch = by_owner(jnp.dot(context_rows, out_weight, preferred_element_type=jnp.float32))
    attn_branch = attn_branch + full(out_bias)
    second_state, second_pull = jax.vjp(
        layer_norm, first_state + attn_branch, full(ln1_gain), full(ln1_shift)
    )
    ffn_input = lax.all_gather(low(second_state), "narrow", axis=0, tiled=True)
    up_value = jnp.dot(ffn_input, up_weight, preferred_element_type=jnp.float32) + full(up_bias)
    activated = low(smooth_gelu(up_value))
    ffn_branch = by_owner(jnp.dot(activated, down_weight, preferred_element_type=jnp.float32))
    ffn_branch = ffn_branch + full(down_bias)
    layer_out, third_pull = jax.vjp(
        layer_norm, second_state + ffn_branch, full(ln2_gain), full(ln2_shift)
    )

    grad_third, grad_ln2_gain, grad_ln2_shift = third_pull(cotangent)
    grad_ffn = low(grad_third)
    grad_down_bias = jnp.sum(full(grad_ffn), axis=0)
    grad_ffn_rows = lax.all_gather(grad_ffn, "narrow", axis=0, tiled=True)
    grad_down_weight = jnp.einsum(
        "gf,gd->fd", activated, grad_ffn_rows, preferred_element_type=jnp.float32
    )
    grad_active = dot_nt(grad_ffn_rows, down_weight)
    grad_up = low(jax.vjp(smooth_gelu, up_value)[1](grad_active)[0])
    grad_up_bias = jnp.sum(full(grad_up), axis=0)
    grad_up_weight = jnp.einsum("gd,gf->df", ffn_input, grad_up, preferred_element_type=jnp.float32)
    grad_second = grad_third + by_owner(dot_nt(grad_up, up_weight))
    ffn_sums = lax.psum((low(grad_up_weight), low(grad_down_weight)), "wide")
    grad_first_branch, grad_ln1_gain, grad_ln1_shift = second_pull(grad_second)
    grad_attn = low(grad_first_branch)
    grad_out_bias = jnp.sum(full(grad_attn), axis=0)
    grad_attn_rows = lax.all_gather(grad_attn, "narrow", axis=0, tiled=True)
    grad_out_weight = jnp.einsum(
        "gc,gd->cd", context_rows, grad_attn_rows, preferred_element_type=jnp.float32
    )
    grad_context = low(dot_nt(grad_attn_rows, out_weight)).reshape(seq_shape)
    grad_query, grad_key, grad_value = attend_back(
        query_heads, key_heads, value_heads, keep_mask, row_peak, row_total, grad_context, score_scale
    )
    grad_joined = jnp.stack(
        [item.reshape(group_rows, local_width) for item in (grad_query, grad_key, grad_value)]
    )
    grad_qv_bias = jnp.stack(
        [jnp.sum(full(grad_joined[0]), axis=0), jnp.sum(full(grad_joined[2]), axis=0)]
    )
    grad_qkv_weight = jnp.einsum(
        "gd,kgc->kdc", gathered, grad_joined, preferred_element_type=jnp.float32
    )
    attn_sums = lax.psum((low(grad_qkv_weight), low(grad_out_weight)), "wide")
    grad_first = grad_first_branch + by_owner(
        jnp.einsum("kgc,kdc->gd", grad_joined, qkv_weight, preferred_element_type=jnp.float32)
    )
    grad_summed, grad_embed_gain, grad_embed_shift = first_pull(grad_first)

    grad_proj_low = low(grad_summed)
    grad_position = jnp.einsum(
        "td,tl->dl", grad_proj_low, position_hot, preferred_element_type=jnp.float32
    )
    is_high = type_ids[:, None] == 1
    vector_grads = jnp.stack(
        [
            jnp.sum(full(grad_proj_low), axis=0),
            jnp.sum(jnp.where(is_high, 0.0, grad_summed), axis=0),
            jnp.sum(jnp.where(is_high, grad_summed, 0.0), axis=0),
            grad_embed_gain,
            grad_embed_shift,
        ],
        axis=1,
    )
    vector_grads = jnp.pad(vector_grads, ((0, 0), (0, LANES - vector_grads.shape[1])))
    table_grads = jnp.concatenate([grad_position, vector_grads], axis=1)
    table_grads = fold(table_grads.reshape(n_wide * n_narrow, own_width, -1), every_bit)
    grad_proj_rows = lax.all_gather(grad_proj_low, "narrow", axis=0, tiled=True)
    grad_proj_weight = jnp.einsum(
        "gd,gh->dh", grad_proj_rows, proj_input, preferred_element_type=jnp.float32
    )
    grad_proj_weight = fold(
        grad_proj_weight.reshape(n_wide, n_narrow * own_width, own_hidden), wide_bits
    )
    grad_proj_weight = lax.all_to_all(
        low(grad_proj_weight).reshape(n_narrow, own_width, own_hidden), "narrow", 0, 0, tiled=True
    )
    owned_proj = full(
        grad_proj_weight.reshape(n_narrow, own_width, half_wide, own_mix)
        .transpose(2, 0, 3, 1)
        .reshape(filters, own_width)
    )
    grad_hidden = jnp.dot(grad_proj_rows, proj_own, preferred_element_type=jnp.float32)

    owned_highway = [None, None]
    mix_bias_grads = [None, None]
    for layer_index in (1, 0):
        hidden_in, low_input, mixture = highway_saved[layer_index]
        grad_direct, grad_mixture = jax.vjp(highway_mix, hidden_in, mixture)[1](grad_hidden)
        grad_mix_low = low(grad_mixture)
        mix_bias_grads[layer_index] = jnp.sum(full(grad_mix_low), axis=0)
        weight = mix_weights[layer_index]
        if layer_index == 1:
            partial = jnp.einsum(
                "tf,mcf->mtc",
                grad_mix_low,
                weight.reshape(n_narrow, own_hidden, -1),
                preferred_element_type=jnp.float32,
            )
            grad_hidden = grad_direct + fold(partial, narrow_bits)
        else:
            partial = dot_nt(grad_mix_low, weight).reshape(group, half_wide, n_narrow, own_mix)
            mine = (jnp.arange(n_narrow) == me_narrow)[None, None, :, None]
            direct = grad_direct.reshape(group, half_wide, 1, own_mix)
            partial = partial + jnp.where(mine, direct, 0.0)
            grad_features = fold(partial.reshape(n_narrow, word_total, filters), narrow_bits)
        weight_grad = jnp.einsum(
            "tk,twc->wkc",
            low_input,
            grad_mix_low.reshape(group, n_wide, own_mix),
            preferred_element_type=jnp.float32,
        )
        weight_grad = full(lax.psum_scatter(low(weight_grad), "wide", scatter_dimension=0))
        if layer_index == 1:
            weight_grad = (
                weight_grad.reshape(n_narrow, half_wide, own_mix, own_mix)
                .transpose(1, 0, 2, 3)
                .reshape(filters, own_mix)
            )
        owned_highway[layer_index] = weight_grad
    owned_highway = jnp.stack(owned_highway)

    grad_pooled = jax.vjp(smooth_gelu, pooled)[1](grad_features)[0]
    filt_grads, hot_grads = pool_backward(
        columns, columns_t, hot, filt_rows, lse, grad_pooled, char_depth, tap_count
    )
    filt_grads = jnp.where(tap_keep | is_bias, filt_grads, 0.0)
    owned_filt = fold(filt_grads.reshape(n_wide * n_narrow, own_filters, LANES), every_bit)
    owned_conv = owned_filt[:, :tap_rows].T
    owned_conv_bias = owned_filt[:, tap_rows + tap_count]
    grad_table = hot_grads[:vocab, :tap_rows].reshape(vocab, tap_count, char_depth).sum(axis=1)

    mix_bias_grads = jnp.stack(mix_bias_grads).reshape(2, n_wide, own_mix)
    wide_parts = [mix_bias_grads, grad_up_bias, grad_qv_bias]
    all_parts = [
        grad_out_bias,
        grad_ln1_gain,
        grad_ln1_shift,
        grad_down_bias,
        grad_ln2_gain,
        grad_ln2_shift,
        grad_table,
    ]

    def joined(parts):
        flat = jnp.concatenate([item.reshape(-1) for item in parts])
        return jnp.pad(flat, (0, -flat.shape[0] % LANES)).reshape(-1, LANES)

    def parted(flat, parts):
        flat, done, start = flat.reshape(-1), [], 0
        for item in parts:
            done.append(flat[start : start + item.size].reshape(item.shape))
            start += item.size
        return done

    wide_flat, all_flat = joined(wide_parts), joined(all_parts)
    flat = total(jnp.concatenate([wide_flat, all_flat]), wide_bits)
    mix_sums, sum_up_bias, sum_qv_bias = parted(flat[: wide_flat.shape[0]], wide_parts)
    owned_mix_bias = lax.dynamic_index_in_dim(mix_sums, lax.axis_index("wide"), 1, keepdims=False)
    (
        sum_out_bias,
        sum_ln1_gain,
        sum_ln1_shift,
        sum_down_bias,
        sum_ln2_gain,
        sum_ln2_shift,
        sum_table,
    ) = parted(total(flat[wide_flat.shape[0] :], narrow_bits), all_parts)
    owned_vectors = table_grads[:, seq_length : seq_length + 5].T
    return (
        layer_out,
        sum_table,
        owned_conv,
        owned_conv_bias,
        owned_highway,
        owned_mix_bias,
        owned_proj,
        owned_vectors[0],
        table_grads[:, :seq_length].T,
        owned_vectors[1:3],
        owned_vectors[3],
        owned_vectors[4],
        full(attn_sums[0]),
        sum_qv_bias,
        full(attn_sums[1]),
        sum_out_bias,
        sum_ln1_gain,
        sum_ln1_shift,
        full(ffn_sums[0]),
        sum_up_bias,
        full(ffn_sums[1]),
        sum_down_bias,
        sum_ln2_gain,
        sum_ln2_shift,
    )


def solution(mesh):
    return jax.shard_map(
        per_device,
        mesh=mesh,
        in_specs=(
            P(("wide", "narrow"), None),
            P(("wide", "narrow"), None),
            P(("wide", "narrow")),
            P(("wide", "narrow")),
            P("wide", None),
            P(),
            P(None, ("wide", "narrow")),
            P(("wide", "narrow")),
            P(None, None, ("wide", "narrow")),
            P(None, ("wide", "narrow")),
            P(None, ("wide", "narrow")),
            P(("wide", "narrow")),
            P(None, ("wide", "narrow")),
            P(None, ("wide", "narrow")),
            P(("wide", "narrow")),
            P(("wide", "narrow")),
            P(None, None, "narrow"),
            P(None, "narrow"),
            P("narrow", None),
            P(),
            P(),
            P(),
            P(None, "narrow"),
            P("narrow"),
            P("narrow", None),
            P(),
            P(),
            P(),
            P(("wide", "narrow"), None),
        ),
        out_specs=(
            P(("wide", "narrow"), None),
            P(),
            P(None, ("wide", "narrow")),
            P(("wide", "narrow")),
            P(None, None, ("wide", "narrow")),
            P(None, ("wide", "narrow")),
            P(None, ("wide", "narrow")),
            P(("wide", "narrow")),
            P(None, ("wide", "narrow")),
            P(None, ("wide", "narrow")),
            P(("wide", "narrow")),
            P(("wide", "narrow")),
            P(None, None, "narrow"),
            P(None, "narrow"),
            P("narrow", None),
            P(),
            P(),
            P(),
            P(None, "narrow"),
            P("narrow"),
            P("narrow", None),
            P(),
            P(),
            P(),
        ),
        check_vma=False,
    )
```

```python
import functools

import jax
import jax.numpy as jnp
from jax import lax
from jax.experimental import pallas as pl
from jax.experimental.pallas import tpu as pltpu
from jax.sharding import PartitionSpec as P

HEAD_DIM = 64
EPSILON = 1e-05
NEG_FILL = -1000000000.0
SHUT = -1e30
LANES = 128
LIGHT = pl.CostEstimate(flops=1000, bytes_accessed=1000, transcendentals=0)


def layer_norm(values, gain, shift):
    centre = values - jnp.mean(values, axis=-1, keepdims=True)
    spread = jnp.mean(centre * centre, axis=-1, keepdims=True)
    return centre * lax.rsqrt(spread + EPSILON) * gain + shift


def smooth_gelu(values):
    return jax.nn.gelu(values, approximate=False)


def low(values):
    return values.astype(jnp.bfloat16)


def full(values):
    return values.astype(jnp.float32)


def filter_widths(filter_total):
    index = jnp.arange(filter_total)
    widths = jnp.ones((filter_total,), jnp.int32)
    for level in range(6):
        widths = widths + (index >= filter_total * 2**level // 64).astype(jnp.int32)
    return widths


def swap(block, axis, bit):
    size = lax.axis_size(axis)
    return lax.ppermute(block, axis, [(i, i ^ (1 << bit)) for i in range(size)])


def after(value, *others):
    return lax.optimization_barrier((value,) + others)[0]


def my_bit(axis, bit):
    return (lax.axis_index(axis) >> bit) & 1


def bits_of(axis):
    return [(axis, bit) for bit in range(lax.axis_size(axis).bit_length() - 1)]


def spread(block, bits):
    shape = block.shape
    held = block[None]
    for axis, bit in bits:
        other = swap(held, axis, bit)
        high = my_bit(axis, bit) == 1
        held = jnp.stack([jnp.where(high, other, held), jnp.where(high, held, other)], axis=1)
        held = held.reshape((-1,) + shape)
    return held


def doubled(block, axis, bit, depth):
    other = swap(block, axis, bit)
    high = my_bit(axis, bit) == 1
    return jnp.stack([jnp.where(high, other, block), jnp.where(high, block, other)], axis=depth)


def halved(parts, axis, bit):
    pairs = parts.reshape((-1, 2) + parts.shape[1:])
    mine = my_bit(axis, bit)
    kept = lax.dynamic_index_in_dim(pairs, mine, 1, keepdims=False)
    sent = low(lax.dynamic_index_in_dim(pairs, 1 - mine, 1, keepdims=False))
    return full(kept) + full(swap(sent, axis, bit))


def fold(parts, bits):
    for axis, bit in bits:
        parts = halved(parts, axis, bit)
    return parts[0]


def near_parts(block, axis):
    parts = [block]
    for bit in reversed(range(lax.axis_size(axis).bit_length() - 1)):
        parts = [item for part in parts for item in (part, swap(part, axis, bit))]
    return parts


def in_order(parts, axis, dim):
    mine = lax.axis_index(axis)
    blocks = []
    for m in range(len(parts)):
        held, count = parts, len(parts)
        for bit in range(count.bit_length() - 1):
            here = ((mine >> bit) & 1) == ((m >> bit) & 1)
            held = [jnp.where(here, even, odd) for even, odd in zip(held[::2], held[1::2])]
        blocks.append(held[0])
    return jnp.concatenate(blocks, axis=dim)


def fold_near(sent, kept, axis):
    whole = full(kept) + full(swap(sent, axis, 0))
    for bit in range(1, lax.axis_size(axis).bit_length() - 1):
        pairs = whole.reshape((-1, 2) + whole.shape[1:])
        whole = pairs[:, 0] + full(swap(low(pairs[:, 1]), axis, bit))
    return whole[0]


def total(value, bits):
    for axis, bit in bits:
        value = value + swap(value, axis, bit)
    return value


def dot_nt(left, right):
    return lax.dot_general(left, right, (((1,), (1,)), ((), ())), preferred_element_type=jnp.float32)


def pool_kernel(cols_ref, filt_ref, lse_ref, *, group):
    letters = cols_ref.shape[0]
    filt = filt_ref[...]
    peak = None
    for first in range(0, letters, group):
        scores = [dot_nt(cols_ref[p], filt) for p in range(first, min(first + group, letters))]
        top = functools.reduce(jnp.maximum, scores)
        if peak is None:
            peak = top
            mass = functools.reduce(jnp.add, [jnp.exp(s - peak) for s in scores])
        else:
            later = jnp.maximum(peak, top)
            fresh = functools.reduce(jnp.add, [jnp.exp(s - later) for s in scores])
            mass = mass * jnp.exp(peak - later) + fresh
            peak = later
    lse_ref[...] = peak + jnp.log(mass)


def pool_forward(columns, filt_rows, block=256):
    letters, words, depth = columns.shape
    filters = filt_rows.shape[0]
    return pl.pallas_call(
        functools.partial(pool_kernel, group=5),
        grid=(filters // block,),
        in_specs=[
            pl.BlockSpec(columns.shape, lambda i: (0, 0, 0)),
            pl.BlockSpec((block, depth), lambda i: (i, 0)),
        ],
        out_specs=pl.BlockSpec((words, block), lambda i: (0, i)),
        out_shape=jax.ShapeDtypeStruct((words, filters), jnp.float32),
        compiler_params=pltpu.CompilerParams(vmem_limit_bytes=48 * 2**20),
        cost_estimate=LIGHT,
        name="pool_forward",
    )(columns, filt_rows)


def back_kernel(
    cols_ref, cols_t_ref, hot_ref, filt_ref, lse_ref, grad_ref, dw_ref, table_ref, gcol_ref, *, depth, taps
):
    letters, words, lanes = cols_ref.shape
    step = pl.program_id(0)
    filt = filt_ref[...]
    lse = lse_ref[...]
    grad = grad_ref[...]

    @pl.when(step == 0)
    def _():
        gcol_ref[...] = jnp.zeros_like(gcol_ref)

    half = letters // 2
    weight_sum = jnp.zeros((lanes, filt.shape[0]), jnp.float32)
    for first, last in ((0, half), (half, letters)):
        slots = jnp.concatenate(
            [low(grad * jnp.exp(dot_nt(cols_ref[p], filt) - lse)) for p in range(first, last)], axis=0
        )
        at = slice(first * words, last * words)
        gcol_ref[at, :] += jnp.dot(slots, filt, preferred_element_type=jnp.float32)
        weight_sum += jnp.dot(cols_t_ref[:, at], slots, preferred_element_type=jnp.float32)
    dw_ref[...] = weight_sum.T

    @pl.when(step == pl.num_programs(0) - 1)
    def _():
        tap = lax.broadcasted_iota(jnp.int32, (words, lanes), 1) // depth
        table_ref[...] = jnp.zeros_like(table_ref)
        for c in range(letters):
            moved = jnp.where(tap == 0, gcol_ref[c * words : (c + 1) * words, :], 0.0)
            for t in range(1, min(taps, c + 1)):
                moved = jnp.where(tap == t, gcol_ref[(c - t) * words : (c - t + 1) * words, :], moved)
            table_ref[...] += jnp.dot(
                hot_ref[:, c * words : (c + 1) * words], low(moved), preferred_element_type=jnp.float32
            )


def pool_backward(columns, columns_t, hot, filt_rows, lse, grad, depth, taps, block=256):
    letters, words, lanes = columns.shape
    filters = filt_rows.shape[0]
    whole = lambda item: pl.BlockSpec(item.shape, lambda i: (0,) * item.ndim)
    return pl.pallas_call(
        functools.partial(back_kernel, depth=depth, taps=taps),
        grid=(filters // block,),
        in_specs=[
            whole(columns),
            whole(columns_t),
            whole(hot),
            pl.BlockSpec((block, lanes), lambda i: (i, 0)),
            pl.BlockSpec((words, block), lambda i: (0, i)),
            pl.BlockSpec((words, block), lambda i: (0, i)),
        ],
        out_specs=[
            pl.BlockSpec((block, lanes), lambda i: (i, 0)),
            pl.BlockSpec((hot.shape[0], lanes), lambda i: (0, 0)),
        ],
        out_shape=[
            jax.ShapeDtypeStruct((filters, lanes), jnp.float32),
            jax.ShapeDtypeStruct((hot.shape[0], lanes), jnp.float32),
        ],
        scratch_shapes=[pltpu.VMEM((letters * words, lanes), jnp.float32)],
        compiler_params=pltpu.CompilerParams(vmem_limit_bytes=48 * 2**20),
        cost_estimate=LIGHT,
        name="pool_backward",
    )(columns, columns_t, hot, filt_rows, lse, grad)


def gelu_parts(values):
    spread_part = 0.5 * (1.0 + lax.erf(values * 0.7071067811865476))
    return spread_part, values * spread_part


def opening_of(values):
    return 1.0 / (1.0 + jnp.exp(-values))


def mix_kernel(place_ref, *refs, parts, by_rows, plain, tile):
    part_refs = refs[:parts]
    weight_a, weight_t, bias_ref, joined_ref, hidden_ref, a_ref, t_ref = refs[parts:]
    half, column = pl.program_id(0), pl.program_id(1)
    mine, pair = place_ref[0], place_ref[1]

    @pl.when((half == 0) & (column == 0))
    def _():
        for k, part in enumerate(part_refs):
            extent = part.shape[0 if by_rows else 1]
            at = pl.ds(pl.multiple_of((mine ^ k) * extent, extent), extent)
            if by_rows:
                joined_ref[at, :] = part[...]
            else:
                joined_ref[:, at] = part[...]

    columns = pl.num_programs(1)
    if plain:
        first = ((column * 2 + (pair ^ half)) * parts + mine) * tile
    else:
        first = ((mine * 2 + (pair ^ half)) * columns + column) * tile

    weight = jnp.concatenate([weight_a[0], weight_t[0]], axis=1)
    mixture = jnp.dot(joined_ref[...], weight, preferred_element_type=jnp.float32)
    a = mixture[:, :tile] + bias_ref[0, 0:1, :]
    t = mixture[:, tile:] + bias_ref[0, 1:2, :]
    skip = full(joined_ref[:, pl.ds(pl.multiple_of(first, tile), tile)])
    opening = opening_of(t)
    hidden_ref[...] = low(opening * skip + (1.0 - opening) * gelu_parts(a)[1])
    a_ref[...] = a
    t_ref[...] = t


def mix_forward(place, parts, weights, bias, by_rows, plain):
    blocks, depth, tile = weights.shape
    columns = blocks // 4
    piece = columns * tile
    rows = sum(p.shape[0] for p in parts) if by_rows else parts[0].shape[0]

    def weight_spec(gate):
        return pl.BlockSpec(
            (1, depth, tile),
            lambda half, column, place: (2 * (column + gate * columns) + (place[1] ^ half), 0, 0),
        )

    def placed(half, column, place):
        return (0, (place[1] ^ half) * columns + column)

    out_block = pl.BlockSpec((rows, tile), placed)
    whole = lambda item: pl.BlockSpec(item.shape, lambda half, column, place: (0,) * item.ndim)
    return pl.pallas_call(
        functools.partial(mix_kernel, parts=len(parts), by_rows=by_rows, plain=plain, tile=tile),
        grid_spec=pltpu.PrefetchScalarGridSpec(
            num_scalar_prefetch=1,
            grid=(2, columns),
            in_specs=[whole(p) for p in parts]
            + [weight_spec(0), weight_spec(1)]
            + [pl.BlockSpec((1, 2, tile), lambda half, column, place: (half, 0, column))],
            out_specs=[
                pl.BlockSpec((rows, depth), lambda half, column, place: (0, 0)),
                out_block,
                out_block,
                out_block,
            ],
        ),
        out_shape=[
            jax.ShapeDtypeStruct((rows, depth), jnp.bfloat16),
            jax.ShapeDtypeStruct((rows, 2 * piece), jnp.bfloat16),
            jax.ShapeDtypeStruct((rows, 2 * piece), jnp.float32),
            jax.ShapeDtypeStruct((rows, 2 * piece), jnp.float32),
        ],
        compiler_params=pltpu.CompilerParams(vmem_limit_bytes=40 * 2**20),
        cost_estimate=LIGHT,
        name="mix_forward",
    )(place, *parts, weights, weights, bias)


def mix_back_kernel(place_ref, grad_ref, a_ref, t_ref, *refs):
    mixed_ref, direct_ref, sums_ref = refs[-3:]
    grad = grad_ref[...]
    a = a_ref[...]
    piece = a.shape[1]
    skip = full(jnp.concatenate([ref[...] for ref in refs[:-3]], axis=1))
    opening = opening_of(t_ref[...])
    phi, bent = gelu_parts(a)
    slope = phi + a * (0.3989422804014327 * jnp.exp(-0.5 * a * a))
    grad_a = low((1.0 - opening) * slope * grad)
    grad_t = low((skip - bent) * opening * (1.0 - opening) * grad)
    mixed_ref[0, :, :piece] = grad_a
    mixed_ref[0, :, piece:] = grad_t
    direct_ref[...] = opening * grad
    sums_ref[0, :, :piece] = jnp.sum(full(grad_a), axis=0, keepdims=True)
    sums_ref[0, :, piece:] = jnp.sum(full(grad_t), axis=0, keepdims=True)


def mix_back(place, grad, a, t, joined, parts, plain, tile=LANES):
    rows, own = grad.shape
    piece = own // 2
    placed = pl.BlockSpec((rows, piece), lambda half, place: (0, place[1] ^ half))
    if plain:
        skips = [
            pl.BlockSpec((rows, tile), lambda half, place, z=z: (0, (z * 2 + (place[1] ^ half)) * parts + place[0]))
            for z in range(piece // tile)
        ]
    else:
        skips = [pl.BlockSpec((rows, piece), lambda half, place: (0, place[0] * 2 + (place[1] ^ half)))]
    return pl.pallas_call(
        mix_back_kernel,
        grid_spec=pltpu.PrefetchScalarGridSpec(
            num_scalar_prefetch=1,
            grid=(2,),
            in_specs=[placed, placed, placed] + skips,
            out_specs=[
                pl.BlockSpec((1, rows, own), lambda half, place: (half, 0, 0)),
                placed,
                pl.BlockSpec((1, 1, own), lambda half, place: (half, 0, 0)),
            ],
        ),
        out_shape=[
            jax.ShapeDtypeStruct((2, rows, own), jnp.bfloat16),
            jax.ShapeDtypeStruct((rows, own), jnp.float32),
            jax.ShapeDtypeStruct((2, 1, own), jnp.float32),
        ],
        compiler_params=pltpu.CompilerParams(vmem_limit_bytes=40 * 2**20),
        cost_estimate=LIGHT,
        name="mix_backward",
    )(place, grad, a, t, *[joined] * len(skips))


def inner_product(mixed_ref, weight_refs):
    blocks = len(weight_refs) // 2
    own = jnp.concatenate([ref[0] for ref in weight_refs[:blocks]], axis=1)
    other = jnp.concatenate([ref[0] for ref in weight_refs[blocks:]], axis=1)
    return dot_nt(mixed_ref[0], own) + dot_nt(mixed_ref[1], other)


def inner_specs(blocks, depth, tile, row_block):
    specs = []
    for flip in (0, 1):
        for z in range(blocks):
            specs.append(
                pl.BlockSpec(
                    (1, depth, tile),
                    lambda i, place, z=z, flip=flip: (2 * z + (place[1] ^ flip), row_block(i, place), 0),
                )
            )
    return specs


def inner_columns_kernel(place_ref, mixed_ref, *refs):
    out_ref = refs[-1]
    out_ref[0] = inner_product(mixed_ref, refs[:-1]).astype(out_ref.dtype)


def inner_columns(place, mixed, weights, odd, parts, dtype):
    _, rows, wide_columns = mixed.shape
    blocks, filters, tile = weights.shape
    blocks = blocks // 2
    depth = filters // parts
    return pl.pallas_call(
        inner_columns_kernel,
        grid_spec=pltpu.PrefetchScalarGridSpec(
            num_scalar_prefetch=1,
            grid=(parts // 2,),
            in_specs=[pl.BlockSpec(mixed.shape, lambda i, place: (0, 0, 0))]
            + inner_specs(blocks, depth, tile, lambda i, place: place[0] ^ (2 * i + odd)),
            out_specs=pl.BlockSpec((1, rows, depth), lambda i, place: (i, 0, 0)),
        ),
        out_shape=jax.ShapeDtypeStruct((parts // 2, rows, depth), dtype),
        compiler_params=pltpu.CompilerParams(vmem_limit_bytes=40 * 2**20),
        cost_estimate=LIGHT,
        name="inner_columns",
    )(place, mixed, *[weights] * (2 * blocks))


def inner_rows_kernel(place_ref, mixed_ref, *refs, parts, plain, tile):
    direct_ref, sent_ref, kept_ref, held_ref = refs[-4:]
    mine = place_ref[0]
    held_ref[...] = inner_product(mixed_ref, refs[:-4])

    step = pl.program_id(0)
    if plain:
        at = pl.ds(pl.multiple_of(mine * tile, tile), tile)
        column = (step % 2) * (pl.num_programs(0) // 2) + step // 2
        held_ref[:, at] += direct_ref[:, pl.ds(pl.multiple_of(column * tile, tile), tile)]
    else:

        @pl.when(step == mine)
        def _():
            held_ref[...] += direct_ref[...]

    extent = held_ref.shape[0] // parts
    for k in range(parts):
        got = held_ref[pl.ds(pl.multiple_of((mine ^ k) * extent, extent), extent), :]
        if k % 2:
            sent_ref[k // 2] = low(got)
        else:
            kept_ref[k // 2] = got


def inner_rows(place, mixed, weights, direct, parts, plain):
    _, rows, wide_columns = mixed.shape
    blocks, filters, tile = weights.shape
    blocks = blocks // 2
    depth = filters // parts
    extent = rows // parts
    out = pl.BlockSpec((parts // 2, extent, depth), lambda j, place: (0, 0, j))
    return pl.pallas_call(
        functools.partial(inner_rows_kernel, parts=parts, plain=plain, tile=tile),
        grid_spec=pltpu.PrefetchScalarGridSpec(
            num_scalar_prefetch=1,
            grid=(parts,),
            in_specs=[pl.BlockSpec(mixed.shape, lambda j, place: (0, 0, 0))]
            + inner_specs(blocks, depth, tile, lambda j, place: j)
            + [pl.BlockSpec(direct.shape, lambda j, place: (0, 0))],
            out_specs=[out, out],
            scratch_shapes=[pltpu.VMEM((rows, depth), jnp.float32)],
        ),
        out_shape=[
            jax.ShapeDtypeStruct((parts // 2, extent, filters), jnp.bfloat16),
            jax.ShapeDtypeStruct((parts // 2, extent, filters), jnp.float32),
        ],
        compiler_params=pltpu.CompilerParams(vmem_limit_bytes=40 * 2**20),
        cost_estimate=LIGHT,
        name="inner_rows",
    )(place, mixed, *[weights] * (2 * blocks), direct)


def slope_of(values):
    phi = 0.5 * (1.0 + lax.erf(values * 0.7071067811865476))
    return phi + values * (0.3989422804014327 * jnp.exp(-0.5 * values * values))


def ffn_forward_kernel(x_ref, *refs, tile):
    out_ref, own_ref = refs[-2:]
    step = pl.program_id(0)
    for k, (up_ref, down_ref, bias_ref) in enumerate(zip(refs[:-2:3], refs[1:-2:3], refs[2:-2:3])):

        @pl.when(step == k)
        def _(k=k, up_ref=up_ref, down_ref=down_ref, bias_ref=bias_ref):
            for first in range(0, x_ref.shape[0], tile):
                at = slice(first, first + tile)
                value = jnp.dot(x_ref[at, :], up_ref[...], preferred_element_type=jnp.float32)
                active = low(gelu_parts(value + full(bias_ref[0:1, :]))[1])
                added = jnp.dot(active, down_ref[...], preferred_element_type=jnp.float32)
                if k == 0:
                    out_ref[at, :] = added
                    own_ref[at, :] = active
                else:
                    out_ref[at, :] += added


def ffn_operands(parts, units):
    width = parts[0].shape[1]
    last = (parts[0].shape[0] - 16) // 16
    specs = [
        pl.BlockSpec((units, width), lambda k: (0, 0)),
        pl.BlockSpec((units, width), lambda k: (1, 0)),
        pl.BlockSpec((16, width), lambda k: (last, 0)),
    ]
    return specs * len(parts), [part for part in parts for _ in range(3)]


def ffn_forward(x, parts, units, tile=256):
    rows, width = x.shape
    whole = lambda shape: pl.BlockSpec(shape, lambda k: (0,) * len(shape))
    specs, operands = ffn_operands(parts, units)
    return pl.pallas_call(
        functools.partial(ffn_forward_kernel, tile=tile),
        grid=(len(parts),),
        in_specs=[whole(x.shape)] + specs,
        out_specs=[whole((rows, width)), whole((rows, units))],
        out_shape=[
            jax.ShapeDtypeStruct((rows, width), jnp.float32),
            jax.ShapeDtypeStruct((rows, units), jnp.bfloat16),
        ],
        compiler_params=pltpu.CompilerParams(vmem_limit_bytes=48 * 2**20),
        cost_estimate=LIGHT,
        name="ffn_forward",
    )(x, *operands)


def ffn_backward_kernel(x_ref, grad_ref, *refs, tile):
    out_ref, own_ref, sums_ref = refs[-3:]
    step = pl.program_id(0)
    for k, (up_ref, down_ref, bias_ref) in enumerate(zip(refs[:-3:3], refs[1:-3:3], refs[2:-3:3])):

        @pl.when(step == k)
        def _(k=k, up_ref=up_ref, down_ref=down_ref, bias_ref=bias_ref):
            sums = jnp.zeros(sums_ref.shape, jnp.float32)
            for first in range(0, x_ref.shape[0], tile):
                at = slice(first, first + tile)
                value = jnp.dot(x_ref[at, :], up_ref[...], preferred_element_type=jnp.float32)
                value = value + full(bias_ref[0:1, :])
                inner = low(dot_nt(grad_ref[at, :], down_ref[...]) * slope_of(value))
                added = dot_nt(inner, up_ref[...])
                if k == 0:
                    out_ref[at, :] = added
                    own_ref[at, :] = inner
                    sums = sums + jnp.sum(full(inner), axis=0, keepdims=True)
                else:
                    out_ref[at, :] += added
            if k == 0:
                sums_ref[...] = sums


def ffn_backward(x, parts, units, grad, tile=256):
    rows, width = x.shape
    whole = lambda shape: pl.BlockSpec(shape, lambda k: (0,) * len(shape))
    specs, operands = ffn_operands(parts, units)
    return pl.pallas_call(
        functools.partial(ffn_backward_kernel, tile=tile),
        grid=(len(parts),),
        in_specs=[whole(x.shape), whole(grad.shape)] + specs,
        out_specs=[whole((rows, width)), whole((rows, units)), whole((1, units))],
        out_shape=[
            jax.ShapeDtypeStruct((rows, width), jnp.float32),
            jax.ShapeDtypeStruct((rows, units), jnp.bfloat16),
            jax.ShapeDtypeStruct((1, units), jnp.float32),
        ],
        compiler_params=pltpu.CompilerParams(vmem_limit_bytes=48 * 2**20),
        cost_estimate=LIGHT,
        name="ffn_backward",
    )(x, grad, *operands)


def masked_scores(query_heads, key_heads, keep_mask, score_scale):
    scores = (
        jnp.einsum("qhd,khd->hqk", query_heads, key_heads, preferred_element_type=jnp.float32)
        * score_scale
    )
    return jnp.where(keep_mask[None, None, :] == 1, scores, NEG_FILL)


def attend(query_heads, key_heads, value_heads, keep_mask, score_scale):
    scores = masked_scores(query_heads, key_heads, keep_mask, score_scale)
    row_peak = jnp.max(scores, axis=-1, keepdims=True)
    raised = jnp.exp(scores - row_peak)
    row_total = jnp.sum(raised, axis=-1, keepdims=True)
    attn_weights = (raised / row_total).astype(jnp.bfloat16)
    context = jnp.einsum(
        "hqk,khd->qhd", attn_weights, value_heads, preferred_element_type=jnp.float32
    )
    return (context.astype(jnp.bfloat16), row_peak, row_total)


def attend_back(
    query_heads, key_heads, value_heads, keep_mask, row_peak, row_total, grad_context, score_scale
):
    scores = masked_scores(query_heads, key_heads, keep_mask, score_scale)
    probs_full = jnp.exp(scores - row_peak) / row_total
    attn_weights = probs_full.astype(jnp.bfloat16)
    grad_value = jnp.einsum(
        "hqk,qhd->khd", attn_weights, grad_context, preferred_element_type=jnp.float32
    )
    grad_weights = jnp.einsum(
        "qhd,khd->hqk", grad_context, value_heads, preferred_element_type=jnp.float32
    )
    inner_sum = jnp.sum(grad_weights * probs_full, axis=-1, keepdims=True)
    grad_scores = (probs_full * (grad_weights - inner_sum)).astype(jnp.bfloat16)
    grad_query = (
        jnp.einsum("hqk,khd->qhd", grad_scores, key_heads, preferred_element_type=jnp.float32)
        * score_scale
    )
    grad_key = (
        jnp.einsum("hqk,qhd->khd", grad_scores, query_heads, preferred_element_type=jnp.float32)
        * score_scale
    )
    return (
        grad_query.astype(jnp.bfloat16),
        grad_key.astype(jnp.bfloat16),
        grad_value.astype(jnp.bfloat16),
    )


def per_device(
    char_ids,
    char_mask,
    position_ids,
    type_ids,
    key_mask,
    char_table,
    conv_weight,
    conv_bias,
    highway_weight,
    highway_bias,
    proj_weight,
    proj_bias,
    position_table,
    type_table,
    embed_gain,
    embed_shift,
    qkv_weight,
    qv_bias,
    out_weight,
    out_bias,
    ln1_gain,
    ln1_shift,
    up_weight,
    up_bias,
    down_weight,
    down_bias,
    ln2_gain,
    ln2_shift,
    cotangent,
):
    n_wide, n_narrow = lax.axis_size("wide"), lax.axis_size("narrow")
    half_wide = n_wide // 2
    me_narrow = lax.axis_index("narrow")
    wide_bits, narrow_bits = bits_of("wide"), bits_of("narrow")
    every_bit = narrow_bits + wide_bits
    falling = every_bit[::-1]
    word_total, letters = char_ids.shape
    tap_rows, own_filters = conv_weight.shape
    char_depth = char_table.shape[1]
    tap_count = tap_rows // char_depth
    filters = highway_weight.shape[1]
    own_mix = highway_weight.shape[2]
    own_width = proj_weight.shape[1]
    seq_length = position_table.shape[0]
    group = word_total * n_narrow
    own_hidden = half_wide * own_mix

    outer = n_wide // 2
    quarter = outer // 2
    outer_groups = [[2 * z + y for z in range(outer)] for y in range(2)]
    me_pair = my_bit("wide", 0)

    def grouped(item):
        split = item.reshape((quarter, 2, n_narrow, own_mix) + item.shape[1:])
        return split.transpose((2, 1, 0, 3) + tuple(range(4, split.ndim))).reshape(item.shape)

    def ungrouped(item):
        split = item.reshape((n_narrow, 2, quarter, own_mix) + item.shape[1:])
        return split.transpose((2, 1, 0, 3) + tuple(range(4, split.ndim))).reshape(item.shape)

    tiled = own_mix == LANES
    corner = jnp.stack([me_narrow, me_pair]).astype(jnp.int32)

    def gather_mix(shard):
        blocks = lax.all_gather(shard, "wide", axis=0)
        if tiled:
            return blocks
        blocks = blocks.reshape(-1, LANES // own_mix, 2, filters, own_mix).transpose(0, 2, 3, 1, 4)
        return blocks.reshape(-1, filters, LANES)

    plain = tiled and half_wide == n_narrow
    ordered, unordered = (lambda item: item, lambda item: item) if plain else (grouped, ungrouped)
    mix_weights = [gather_mix(ordered(highway_weight[0]))]
    mix_weights.append(gather_mix(after(grouped(highway_weight[1]), mix_weights[0])))
    conv_block = jnp.zeros((own_filters, LANES), jnp.bfloat16)
    conv_block = conv_block.at[:, :tap_rows].set(conv_weight.T)
    conv_block = conv_block.at[:, tap_rows + tap_count].set(conv_bias)
    bias_block = jnp.pad(highway_bias, ((0, 0), (0, LANES - own_mix)))
    conv_spread = spread(jnp.concatenate([conv_block, bias_block]), falling)
    filt_rows = ordered(conv_spread[:, :own_filters].reshape(filters, LANES))
    mix_bias = conv_spread[:, own_filters:, :own_mix].reshape(outer, 2, n_narrow, 2, own_mix)
    mix_bias = full(lax.dynamic_index_in_dim(mix_bias, me_narrow, 2, keepdims=False))
    mix_bias = [lax.dynamic_index_in_dim(mix_bias, me_pair ^ half, 1, keepdims=False) for half in range(2)]
    mix_bias = jnp.stack(mix_bias).transpose(2, 0, 1, 3).reshape(2, 2, 2, quarter * own_mix)
    vector_block = jnp.stack([proj_bias, type_table[0], type_table[1], embed_gain, embed_shift], axis=1)
    vector_block = jnp.pad(vector_block, ((0, 0), (0, LANES - vector_block.shape[1])))
    rest = jnp.concatenate([grouped(proj_weight).T, position_table.T, vector_block], axis=1)[None]
    rest_bits = wide_bits[::-1]
    rest = doubled(rest, *rest_bits[0], 1).reshape((-1,) + rest.shape[1:])
    widths = ordered(filter_widths(filters))
    lane = jnp.arange(LANES)
    tap_keep = (lane[None, :] // char_depth) < widths[:, None]
    late = lane - tap_rows
    shut = (late == 0)[None, :] | (
        (late >= 1)[None, :] & (late < tap_count)[None, :] & (widths[:, None] > late[None, :])
    )
    is_bias = (late == tap_count)[None, :]
    filt_rows = jnp.where(
        (tap_keep & (late < 0)[None, :]) | is_bias,
        filt_rows,
        jnp.where(shut, jnp.bfloat16(SHUT), jnp.bfloat16(0.0)),
    )
    vocab = char_table.shape[0]
    vocab_rows = -(-vocab // 16) * 16
    id_row = char_ids.T.reshape(1, letters * word_total)
    hot = (jnp.arange(vocab_rows)[:, None] == id_row).astype(jnp.bfloat16)
    table_t = jnp.pad(char_table, ((0, vocab_rows - vocab), (0, 0))).T
    embedded = low(jnp.dot(table_t, hot, preferred_element_type=jnp.float32))
    embedded = jnp.pad(embedded, ((0, 0), (0, tap_count * word_total)))
    span = letters * word_total
    tap_blocks = [embedded[:, t * word_total : t * word_total + span] for t in range(tap_count)]
    place = jnp.arange(letters)
    usable = (char_mask == 1) | (place[None, :] == 0)
    unusable_row = low(~usable).T.reshape(1, span)
    late_rows = low(place[None, :] == letters - jnp.arange(1, tap_count)[:, None])
    late_rows = jnp.repeat(late_rows, word_total, axis=1)
    columns_t = jnp.concatenate(
        tap_blocks
        + [
            unusable_row,
            late_rows,
            jnp.ones((1, span), jnp.bfloat16),
            jnp.zeros((LANES - tap_rows - tap_count - 1, span), jnp.bfloat16),
        ]
    )
    columns = columns_t.T.reshape(letters, word_total, LANES)
    tally = jnp.stack(
        [jnp.sum(full(usable[:, : letters - w + 1]), axis=1) for w in range(1, tap_count + 1)], axis=1
    )
    width_hot = full(jnp.arange(1, tap_count + 1)[:, None] == widths[None, :])
    valid_count = jnp.dot(tally, width_hot)

    def rest_step(rest, which):
        return doubled(rest, *which, 1).reshape((-1,) + rest.shape[1:])

    rest = after(rest, conv_spread)
    for which in rest_bits[1:-1]:
        rest = rest_step(rest, which)
    units = up_weight.shape[1]
    encoder_pack = jnp.concatenate(
        [up_weight, down_weight, out_weight, jnp.broadcast_to(up_bias[None], (16, units))]
    )
    encoder_parts = [encoder_pack, swap(encoder_pack, "narrow", 1)]
    filt_rows, encoder_parts = lax.optimization_barrier((filt_rows, encoder_parts))
    lse = pool_forward(columns, filt_rows)
    rest = rest_step(after(rest, lse), rest_bits[-1])
    pooled = lse - jnp.log(valid_count)
    features = low(smooth_gelu(pooled))

    parts = near_parts(features, "narrow")
    near_order = [0, 2, 1, 3]
    cotangent_rows = lax.all_gather(
        after(cotangent, mix_weights[1]), "narrow", axis=0, tiled=True
    )
    rest = after(rest, parts[-1])

    def narrowed(rest, bit):
        width = own_hidden << bit
        mine = my_bit("narrow", bit)
        tail = rest[..., 2 * width :]
        kept = lax.dynamic_slice_in_dim(rest, mine * width, width, rest.ndim - 1)
        sent = lax.dynamic_slice_in_dim(rest, (1 - mine) * width, width, rest.ndim - 1)
        kept, sent = (jnp.concatenate([item, tail], axis=-1) for item in (kept, sent))
        got = swap(sent, "narrow", bit)
        high = mine == 1
        pair = jnp.stack([jnp.where(high, got, kept), jnp.where(high, kept, got)], axis=1)
        return pair.reshape((-1,) + pair.shape[2:])

    rest = narrowed(rest, 1)
    highway_saved, pair_parts = [], [swap(features, "wide", 0)]
    for layer_index in range(2):
        joined, hidden, kept_a, kept_t = mix_forward(
            corner, parts, mix_weights[layer_index], mix_bias[layer_index], layer_index == 0, plain and layer_index == 0
        )
        highway_saved.append((joined, kept_a, kept_t))
        if layer_index == 0:
            parts = near_parts(hidden, "narrow")
            pair_parts.append(swap(hidden, "wide", 0))
            rest = narrowed(after(rest, hidden), 0)
            encoder_parts = encoder_parts + [
                swap(item, "narrow", 0) for item in after(encoder_parts, hidden)
            ]
            parts, encoder_parts = lax.optimization_barrier((parts, encoder_parts))
    rest, proj_input = lax.optimization_barrier((rest, hidden))
    rest = rest.reshape(n_wide * n_narrow * own_width, -1)
    model_width = rest.shape[0]
    proj_own = rest[:, :own_hidden]
    position_rows = rest[:, own_hidden : own_hidden + seq_length]
    vectors = full(rest[:, own_hidden + seq_length :].T)
    proj_shift, type_low, type_high, first_gain, first_shift = (vectors[i] for i in range(5))
    projected = fold(dot_nt(proj_input, proj_own).reshape(n_narrow, word_total, model_width), narrow_bits)
    projected, cotangent_rows = lax.optimization_barrier((projected, cotangent_rows))
    position_hot = (position_ids[:, None] == jnp.arange(seq_length)[None, :]).astype(jnp.bfloat16)
    type_rows = jnp.where(type_ids[:, None] == 1, type_high, type_low)
    summed = projected + proj_shift + dot_nt(position_hot, position_rows) + type_rows
    first_state, first_pull = jax.vjp(layer_norm, summed, first_gain, first_shift)

    gathered = lax.all_gather(low(first_state), "narrow", axis=0, tiled=True)
    group_rows = gathered.shape[0]
    qkv_out = jnp.einsum("gd,kdc->kgc", gathered, qkv_weight, preferred_element_type=jnp.float32)
    local_width = qkv_out.shape[2]
    head_count = local_width // HEAD_DIM
    seq_shape = (group_rows, head_count, HEAD_DIM)
    query_heads = low(qkv_out[0] + full(qv_bias[0])).reshape(seq_shape)
    key_heads = low(qkv_out[1]).reshape(seq_shape)
    value_heads = low(qkv_out[2] + full(qv_bias[1])).reshape(seq_shape)
    score_scale = HEAD_DIM ** (-0.5)
    keep_mask = key_mask[0]
    context, row_peak, row_total = attend(query_heads, key_heads, value_heads, keep_mask, score_scale)
    context_rows = context.reshape(group_rows, local_width)

    def by_owner(partial):
        return fold(partial.reshape(n_narrow, word_total, model_width), narrow_bits)

    def own_words(rows):
        return lax.dynamic_slice_in_dim(rows, me_narrow * word_total, word_total, 0)

    attn_branch = full(out_bias)
    for k, part in zip(near_order, near_parts(context_rows, "narrow")):
        weight = encoder_parts[k][2 * units : 2 * units + local_width]
        attn_branch = attn_branch + jnp.dot(part, weight, preferred_element_type=jnp.float32)
    second_state, second_pull = jax.vjp(
        layer_norm, full(gathered) + attn_branch, full(ln1_gain), full(ln1_shift)
    )
    pair_parts, ffn_input = lax.optimization_barrier((pair_parts, low(second_state)))
    ffn_branch, activated = ffn_forward(ffn_input, encoder_parts, units)
    layer_out, third_pull = jax.vjp(
        layer_norm, second_state + (ffn_branch + full(down_bias)), full(ln2_gain), full(ln2_shift)
    )
    layer_out = own_words(layer_out)

    def pair_start(halves):
        kept = lax.dynamic_index_in_dim(halves, me_pair, 0, keepdims=False)
        sent = lax.dynamic_index_in_dim(halves, 1 - me_pair, 0, keepdims=False)
        return kept, swap(sent, "wide", 0)

    def pair_end(mine, back):
        first = me_pair == 0
        return jnp.stack([full(jnp.where(first, mine, back)), full(jnp.where(first, back, mine))])

    grad_third, grad_ln2_gain, grad_ln2_shift = third_pull(cotangent_rows)
    grad_ffn = low(grad_third)
    grad_down_bias = jnp.sum(full(grad_ffn), axis=0)
    grad_down_weight = jnp.einsum("gf,gd->fd", activated, grad_ffn, preferred_element_type=jnp.float32)
    grad_inner, grad_up, grad_up_bias = ffn_backward(ffn_input, encoder_parts, units, grad_ffn)
    grad_up_weight = jnp.einsum("gd,gf->df", ffn_input, grad_up, preferred_element_type=jnp.float32)
    grad_second = grad_third + grad_inner
    ffn_kept, ffn_received = pair_start(jnp.stack([low(grad_up_weight), low(grad_down_weight)]))
    grad_first_branch, grad_ln1_gain, grad_ln1_shift = second_pull(grad_second)
    pair_parts = [near_parts(after(item, ffn_branch), "narrow") for item in pair_parts]
    pair_parts, grad_attn = lax.optimization_barrier((pair_parts, low(grad_first_branch)))
    pair_joined = [
        in_order(item, "narrow", layer_index) for layer_index, item in enumerate(pair_parts)
    ]
    grad_out_bias = jnp.sum(full(grad_attn), axis=0)
    grad_attn_rows = grad_attn
    grad_out_weight = jnp.einsum(
        "gc,gd->cd", context_rows, grad_attn_rows, preferred_element_type=jnp.float32
    )
    grad_context = low(dot_nt(grad_attn_rows, out_weight)).reshape(seq_shape)
    grad_query, grad_key, grad_value = attend_back(
        query_heads, key_heads, value_heads, keep_mask, row_peak, row_total, grad_context, score_scale
    )
    grad_joined = jnp.stack(
        [item.reshape(group_rows, local_width) for item in (grad_query, grad_key, grad_value)]
    )
    grad_qv_bias = jnp.stack(
        [jnp.sum(full(grad_joined[0]), axis=0), jnp.sum(full(grad_joined[2]), axis=0)]
    )
    grad_qkv_weight = jnp.einsum(
        "kgc,gd->kcd", grad_joined, gathered, preferred_element_type=jnp.float32
    )
    attn_kept, attn_received = pair_start(
        jnp.concatenate([low(grad_qkv_weight), low(grad_out_weight)[None]]).reshape(2, -1, model_width)
    )
    grad_first = own_words(grad_first_branch) + by_owner(
        jnp.einsum("kgc,kdc->gd", grad_joined, qkv_weight, preferred_element_type=jnp.float32)
    )
    grad_summed, grad_embed_gain, grad_embed_shift = first_pull(grad_first)

    grad_proj_low = low(grad_summed)
    grad_position = jnp.einsum(
        "td,tl->dl", grad_proj_low, position_hot, preferred_element_type=jnp.float32
    )
    is_high = type_ids[:, None] == 1
    vector_grads = jnp.stack(
        [
            jnp.sum(full(grad_proj_low), axis=0),
            jnp.sum(jnp.where(is_high, 0.0, grad_summed), axis=0),
            jnp.sum(jnp.where(is_high, grad_summed, 0.0), axis=0),
            grad_embed_gain,
            grad_embed_shift,
        ],
        axis=1,
    )
    vector_grads = jnp.pad(vector_grads, ((0, 0), (0, LANES - vector_grads.shape[1])))
    table_grads = jnp.concatenate([grad_position, vector_grads], axis=1)
    grad_proj_rows = lax.all_gather(grad_proj_low, "narrow", axis=0, tiled=True)
    grad_proj_weight = jnp.einsum(
        "gd,gh->dh", grad_proj_rows, proj_input, preferred_element_type=jnp.float32
    )
    table_grads = jnp.concatenate([low(table_grads), low(grad_proj_weight)], axis=1)
    table_grads = table_grads.reshape(n_wide, n_narrow, own_width, -1).transpose(1, 0, 2, 3)
    table_grads = lax.all_to_all(table_grads, "narrow", 0, 0, tiled=True)
    table_width = seq_length + LANES
    table_sums = jnp.sum(full(table_grads[..., :table_width]), axis=0)
    proj_parts = table_grads[..., table_width:].transpose(1, 0, 2, 3)
    rest_grads = [item.reshape(n_wide, -1, LANES) for item in (low(table_sums), proj_parts)]
    table_rows = rest_grads[0].shape[1]
    rest_grads = jnp.concatenate(rest_grads, axis=1)
    grad_hidden = jnp.dot(grad_proj_rows, proj_own, preferred_element_type=jnp.float32)

    mix_bias_grads = [None, None]

    def weight_part(joined, mixed):
        return jnp.einsum(
            "tk,tzc->zkc",
            joined,
            mixed.reshape(group, outer, own_mix),
            preferred_element_type=jnp.float32,
        )

    def pair_weight(layer_index, mixed, met):
        joined = highway_saved[layer_index][0]
        return low(weight_part(joined, mixed[0]) + weight_part(pair_joined[layer_index], met))

    ffn_received, attn_received = after((ffn_received, attn_received), grad_hidden)
    pair_sums = lax.psum(
        (low(full(ffn_kept) + full(ffn_received)), low(full(attn_kept) + full(attn_received))),
        "wide",
        axis_index_groups=outer_groups,
    )
    joined, kept_a, kept_t = highway_saved[1]
    mixed, direct, mix_bias_grads[1] = mix_back(corner, grad_hidden, kept_a, kept_t, joined, n_narrow, False)
    met = swap(mixed[1], "wide", 0)
    sent = inner_columns(corner, mixed, mix_weights[1], 1, n_narrow, jnp.bfloat16)
    kept = inner_columns(corner, mixed, mix_weights[1], 0, n_narrow, jnp.float32)
    grad_hidden = direct + fold_near(sent, kept, "narrow")
    weight_second = pair_weight(1, mixed, after(met, grad_hidden))
    joined, kept_a, kept_t = highway_saved[0]
    mixed, direct, mix_bias_grads[0] = mix_back(corner, grad_hidden, kept_a, kept_t, joined, n_narrow, plain)
    met = swap(mixed[1], "wide", 0)
    sent, kept = inner_rows(corner, mixed, mix_weights[0], direct, n_narrow, plain)
    grad_features = fold_near(sent, kept, "narrow")

    rest_grads = low(halved(after(rest_grads, direct), *wide_bits[0]))
    weight_first = pair_weight(0, mixed, met)
    both = [item.reshape(outer, -1, LANES) for item in (weight_first, weight_second)]
    weight_rows = both[0].shape[1]
    both = jnp.concatenate(both + [rest_grads], axis=1)
    grad_features, both, pair_sums = lax.optimization_barrier((grad_features, both, pair_sums))
    pair_backs = [swap(item, "wide", 0) for item in pair_sums]

    grad_pooled = jax.vjp(smooth_gelu, pooled)[1](grad_features)[0]
    filt_grads, hot_grads = pool_backward(
        columns, columns_t, hot, filt_rows, lse, grad_pooled, char_depth, tap_count
    )
    both = lax.psum_scatter(both, "wide", scatter_dimension=0, axis_index_groups=outer_groups)
    both = full(both)
    owned_highway = jnp.stack(
        [
            unordered(both[:weight_rows].reshape(filters, own_mix)),
            ungrouped(both[weight_rows : 2 * weight_rows].reshape(filters, own_mix)),
        ]
    )
    owned_rest = both[2 * weight_rows :]
    table_grads = owned_rest[:table_rows].reshape(own_width, table_width)
    owned_proj = owned_rest[table_rows:].reshape(n_narrow, own_width, own_hidden).transpose(0, 2, 1)
    owned_proj = ungrouped(owned_proj.reshape(filters, own_width))
    filt_grads = unordered(low(jnp.where(tap_keep | is_bias, filt_grads, 0.0)))
    filt_grads = fold(filt_grads.reshape(n_wide, -1, LANES), wide_bits)
    owned_filt = lax.all_to_all(
        low(filt_grads).reshape(n_narrow, own_filters, LANES), "narrow", 0, 0, tiled=True
    )
    owned_filt = jnp.sum(full(owned_filt), axis=0)
    owned_conv = owned_filt[:, :tap_rows].T
    owned_conv_bias = owned_filt[:, tap_rows + tap_count]
    grad_table = hot_grads[:vocab, :tap_rows].reshape(vocab, tap_count, char_depth).sum(axis=1)

    mix_bias_grads = jnp.stack(mix_bias_grads).reshape(2, 2, outer, own_mix)
    swapped = jnp.stack([jnp.where(me_pair == 0, mix_bias_grads[:, y], mix_bias_grads[:, 1 - y]) for y in range(2)], axis=2)
    mix_bias_grads = swapped.reshape(2, n_wide, own_mix)
    wide_parts = [
        mix_bias_grads,
        grad_up_bias[0],
        grad_qv_bias,
        grad_out_bias,
        grad_ln1_gain,
        grad_ln1_shift,
        grad_down_bias,
        grad_ln2_gain,
        grad_ln2_shift,
    ]
    all_parts = [grad_table]

    def joined_rows(parts):
        flat = jnp.concatenate([item.reshape(-1) for item in parts])
        return jnp.pad(flat, (0, -flat.shape[0] % LANES)).reshape(-1, LANES)

    def parted(flat, parts):
        flat, done, start = flat.reshape(-1), [], 0
        for item in parts:
            done.append(flat[start : start + item.size].reshape(item.shape))
            start += item.size
        return done

    wide_flat, all_flat = joined_rows(wide_parts), joined_rows(all_parts)
    flat, pair_backs = lax.optimization_barrier((jnp.concatenate([wide_flat, all_flat]), pair_backs))
    flat = total(flat, wide_bits)
    (
        mix_sums,
        sum_up_bias,
        sum_qv_bias,
        sum_out_bias,
        sum_ln1_gain,
        sum_ln1_shift,
        sum_down_bias,
        sum_ln2_gain,
        sum_ln2_shift,
    ) = parted(flat[: wide_flat.shape[0]], wide_parts)
    owned_mix_bias = lax.dynamic_index_in_dim(mix_sums, lax.axis_index("wide"), 1, keepdims=False)
    sum_table = parted(total(flat[wide_flat.shape[0] :], narrow_bits), all_parts)[0]
    ffn_sums, attn_sums = (pair_end(mine, back) for mine, back in zip(pair_sums, pair_backs))
    attn_sums = attn_sums.reshape(n_narrow, local_width, model_width)
    owned_vectors = table_grads[:, seq_length : seq_length + 5].T
    return (
        layer_out,
        sum_table,
        owned_conv,
        owned_conv_bias,
        owned_highway,
        owned_mix_bias,
        owned_proj,
        owned_vectors[0],
        table_grads[:, :seq_length].T,
        owned_vectors[1:3],
        owned_vectors[3],
        owned_vectors[4],
        attn_sums[:3].transpose(0, 2, 1),
        sum_qv_bias,
        attn_sums[3],
        sum_out_bias,
        sum_ln1_gain,
        sum_ln1_shift,
        ffn_sums[0],
        sum_up_bias,
        ffn_sums[1],
        sum_down_bias,
        sum_ln2_gain,
        sum_ln2_shift,
    )


def solution(mesh):
    return jax.shard_map(
        per_device,
        mesh=mesh,
        in_specs=(
            P(("wide", "narrow"), None),
            P(("wide", "narrow"), None),
            P(("wide", "narrow")),
            P(("wide", "narrow")),
            P("wide", None),
            P(),
            P(None, ("wide", "narrow")),
            P(("wide", "narrow")),
            P(None, None, ("wide", "narrow")),
            P(None, ("wide", "narrow")),
            P(None, ("wide", "narrow")),
            P(("wide", "narrow")),
            P(None, ("wide", "narrow")),
            P(None, ("wide", "narrow")),
            P(("wide", "narrow")),
            P(("wide", "narrow")),
            P(None, None, "narrow"),
            P(None, "narrow"),
            P("narrow", None),
            P(),
            P(),
            P(),
            P(None, "narrow"),
            P("narrow"),
            P("narrow", None),
            P(),
            P(),
            P(),
            P(("wide", "narrow"), None),
        ),
        out_specs=(
            P(("wide", "narrow"), None),
            P(),
            P(None, ("wide", "narrow")),
            P(("wide", "narrow")),
            P(None, None, ("wide", "narrow")),
            P(None, ("wide", "narrow")),
            P(None, ("wide", "narrow")),
            P(("wide", "narrow")),
            P(None, ("wide", "narrow")),
            P(None, ("wide", "narrow")),
            P(("wide", "narrow")),
            P(("wide", "narrow")),
            P(None, None, "narrow"),
            P(None, "narrow"),
            P("narrow", None),
            P(),
            P(),
            P(),
            P(None, "narrow"),
            P("narrow"),
            P("narrow", None),
            P(),
            P(),
            P(),
        ),
        check_vma=False,
    )
```

```python
import functools

import jax
import jax.numpy as jnp
from jax import lax
from jax.experimental import pallas as pl
from jax.experimental.pallas import tpu as pltpu
from jax.sharding import PartitionSpec as P

HEAD_DIM = 64
EPSILON = 1e-05
NEG_FILL = -1000000000.0
SHUT = -1e30
LANES = 128
LIGHT = pl.CostEstimate(flops=1000, bytes_accessed=1000, transcendentals=0)


def layer_norm(values, gain, shift):
    centre = values - jnp.mean(values, axis=-1, keepdims=True)
    spread = jnp.mean(centre * centre, axis=-1, keepdims=True)
    return centre * lax.rsqrt(spread + EPSILON) * gain + shift


def smooth_gelu(values):
    return jax.nn.gelu(values, approximate=False)


def low(values):
    return values.astype(jnp.bfloat16)


def full(values):
    return values.astype(jnp.float32)


def filter_widths(filter_total):
    index = jnp.arange(filter_total)
    widths = jnp.ones((filter_total,), jnp.int32)
    for level in range(6):
        widths = widths + (index >= filter_total * 2**level // 64).astype(jnp.int32)
    return widths


def swap(block, axis, bit):
    size = lax.axis_size(axis)
    return lax.ppermute(block, axis, [(i, i ^ (1 << bit)) for i in range(size)])


def after(value, *others):
    return lax.optimization_barrier((value,) + others)[0]


def my_bit(axis, bit):
    return (lax.axis_index(axis) >> bit) & 1


def bits_of(axis):
    return [(axis, bit) for bit in range(lax.axis_size(axis).bit_length() - 1)]


def spread(block, bits):
    shape = block.shape
    held = block[None]
    for axis, bit in bits:
        other = swap(held, axis, bit)
        high = my_bit(axis, bit) == 1
        held = jnp.stack([jnp.where(high, other, held), jnp.where(high, held, other)], axis=1)
        held = held.reshape((-1,) + shape)
    return held


def doubled(block, axis, bit, depth):
    other = swap(block, axis, bit)
    high = my_bit(axis, bit) == 1
    return jnp.stack([jnp.where(high, other, block), jnp.where(high, block, other)], axis=depth)


def halved(parts, axis, bit):
    pairs = parts.reshape((-1, 2) + parts.shape[1:])
    mine = my_bit(axis, bit)
    kept = lax.dynamic_index_in_dim(pairs, mine, 1, keepdims=False)
    sent = low(lax.dynamic_index_in_dim(pairs, 1 - mine, 1, keepdims=False))
    return full(kept) + full(swap(sent, axis, bit))


def fold(parts, bits):
    for axis, bit in bits:
        parts = halved(parts, axis, bit)
    return parts[0]


def near_parts(block, axis):
    parts = [block]
    for bit in reversed(range(lax.axis_size(axis).bit_length() - 1)):
        parts = [item for part in parts for item in (part, swap(part, axis, bit))]
    return parts


def in_order(parts, axis, dim):
    mine = lax.axis_index(axis)
    blocks = []
    for m in range(len(parts)):
        held, count = parts, len(parts)
        for bit in range(count.bit_length() - 1):
            here = ((mine >> bit) & 1) == ((m >> bit) & 1)
            held = [jnp.where(here, even, odd) for even, odd in zip(held[::2], held[1::2])]
        blocks.append(held[0])
    return jnp.concatenate(blocks, axis=dim)


def fold_near(sent, kept, axis):
    whole = full(kept) + full(swap(sent, axis, 0))
    for bit in range(1, lax.axis_size(axis).bit_length() - 1):
        pairs = whole.reshape((-1, 2) + whole.shape[1:])
        whole = pairs[:, 0] + full(swap(low(pairs[:, 1]), axis, bit))
    return whole[0]


def total(value, bits):
    for axis, bit in bits:
        value = value + swap(value, axis, bit)
    return value


def dot_nt(left, right):
    return lax.dot_general(left, right, (((1,), (1,)), ((), ())), preferred_element_type=jnp.float32)


def pool_kernel(cols_ref, filt_ref, lse_ref, *, group):
    letters = cols_ref.shape[0]
    filt = filt_ref[...]
    peak = None
    for first in range(0, letters, group):
        scores = [dot_nt(cols_ref[p], filt) for p in range(first, min(first + group, letters))]
        top = functools.reduce(jnp.maximum, scores)
        if peak is None:
            peak = top
            mass = functools.reduce(jnp.add, [jnp.exp(s - peak) for s in scores])
        else:
            later = jnp.maximum(peak, top)
            fresh = functools.reduce(jnp.add, [jnp.exp(s - later) for s in scores])
            mass = mass * jnp.exp(peak - later) + fresh
            peak = later
    lse_ref[...] = peak + jnp.log(mass)


def pool_forward(columns, filt_rows, block=256):
    letters, words, depth = columns.shape
    filters = filt_rows.shape[0]
    return pl.pallas_call(
        functools.partial(pool_kernel, group=5),
        grid=(filters // block,),
        in_specs=[
            pl.BlockSpec(columns.shape, lambda i: (0, 0, 0)),
            pl.BlockSpec((block, depth), lambda i: (i, 0)),
        ],
        out_specs=pl.BlockSpec((words, block), lambda i: (0, i)),
        out_shape=jax.ShapeDtypeStruct((words, filters), jnp.float32),
        compiler_params=pltpu.CompilerParams(vmem_limit_bytes=48 * 2**20),
        cost_estimate=LIGHT,
        name="pool_forward",
    )(columns, filt_rows)


def back_kernel(
    cols_ref, cols_t_ref, hot_ref, filt_ref, lse_ref, grad_ref, dw_ref, table_ref, gcol_ref, *, depth, taps
):
    letters, words, lanes = cols_ref.shape
    step = pl.program_id(0)
    filt = filt_ref[...]
    lse = lse_ref[...]
    grad = grad_ref[...]

    @pl.when(step == 0)
    def _():
        gcol_ref[...] = jnp.zeros_like(gcol_ref)

    half = letters // 2
    weight_sum = jnp.zeros((lanes, filt.shape[0]), jnp.float32)
    for first, last in ((0, half), (half, letters)):
        slots = jnp.concatenate(
            [low(grad * jnp.exp(dot_nt(cols_ref[p], filt) - lse)) for p in range(first, last)], axis=0
        )
        at = slice(first * words, last * words)
        gcol_ref[at, :] += jnp.dot(slots, filt, preferred_element_type=jnp.float32)
        weight_sum += jnp.dot(cols_t_ref[:, at], slots, preferred_element_type=jnp.float32)
    dw_ref[...] = weight_sum.T

    @pl.when(step == pl.num_programs(0) - 1)
    def _():
        tap = lax.broadcasted_iota(jnp.int32, (words, lanes), 1) // depth
        table_ref[...] = jnp.zeros_like(table_ref)
        for c in range(letters):
            moved = jnp.where(tap == 0, gcol_ref[c * words : (c + 1) * words, :], 0.0)
            for t in range(1, min(taps, c + 1)):
                moved = jnp.where(tap == t, gcol_ref[(c - t) * words : (c - t + 1) * words, :], moved)
            table_ref[...] += jnp.dot(
                hot_ref[:, c * words : (c + 1) * words], low(moved), preferred_element_type=jnp.float32
            )


def pool_backward(columns, columns_t, hot, filt_rows, lse, grad, depth, taps, block=256):
    letters, words, lanes = columns.shape
    filters = filt_rows.shape[0]
    whole = lambda item: pl.BlockSpec(item.shape, lambda i: (0,) * item.ndim)
    return pl.pallas_call(
        functools.partial(back_kernel, depth=depth, taps=taps),
        grid=(filters // block,),
        in_specs=[
            whole(columns),
            whole(columns_t),
            whole(hot),
            pl.BlockSpec((block, lanes), lambda i: (i, 0)),
            pl.BlockSpec((words, block), lambda i: (0, i)),
            pl.BlockSpec((words, block), lambda i: (0, i)),
        ],
        out_specs=[
            pl.BlockSpec((block, lanes), lambda i: (i, 0)),
            pl.BlockSpec((hot.shape[0], lanes), lambda i: (0, 0)),
        ],
        out_shape=[
            jax.ShapeDtypeStruct((filters, lanes), jnp.float32),
            jax.ShapeDtypeStruct((hot.shape[0], lanes), jnp.float32),
        ],
        scratch_shapes=[pltpu.VMEM((letters * words, lanes), jnp.float32)],
        compiler_params=pltpu.CompilerParams(vmem_limit_bytes=48 * 2**20),
        cost_estimate=LIGHT,
        name="pool_backward",
    )(columns, columns_t, hot, filt_rows, lse, grad)


def gelu_parts(values):
    spread_part = 0.5 * (1.0 + lax.erf(values * 0.7071067811865476))
    return spread_part, values * spread_part


def opening_of(values):
    return 1.0 / (1.0 + jnp.exp(-values))


def mix_kernel(place_ref, *refs, parts, by_rows, plain, tile):
    part_refs = refs[:parts]
    weight_a, weight_t, bias_ref, joined_ref, hidden_ref, a_ref, t_ref = refs[parts:]
    half, column = pl.program_id(0), pl.program_id(1)
    mine, pair = place_ref[0], place_ref[1]

    @pl.when((half == 0) & (column == 0))
    def _():
        for k, part in enumerate(part_refs):
            extent = part.shape[0 if by_rows else 1]
            at = pl.ds(pl.multiple_of((mine ^ k) * extent, extent), extent)
            if by_rows:
                joined_ref[at, :] = part[...]
            else:
                joined_ref[:, at] = part[...]

    columns = pl.num_programs(1)
    if plain:
        first = ((column * 2 + (pair ^ half)) * parts + mine) * tile
    else:
        first = ((mine * 2 + (pair ^ half)) * columns + column) * tile

    weight = jnp.concatenate([weight_a[0], weight_t[0]], axis=1)
    mixture = jnp.dot(joined_ref[...], weight, preferred_element_type=jnp.float32)
    a = mixture[:, :tile] + bias_ref[0, 0:1, :]
    t = mixture[:, tile:] + bias_ref[0, 1:2, :]
    skip = full(joined_ref[:, pl.ds(pl.multiple_of(first, tile), tile)])
    opening = opening_of(t)
    hidden_ref[...] = low(opening * skip + (1.0 - opening) * gelu_parts(a)[1])
    a_ref[...] = a
    t_ref[...] = t


def mix_forward(place, parts, weights, bias, by_rows, plain):
    blocks, depth, tile = weights.shape
    columns = blocks // 4
    piece = columns * tile
    rows = sum(p.shape[0] for p in parts) if by_rows else parts[0].shape[0]

    def weight_spec(gate):
        return pl.BlockSpec(
            (1, depth, tile),
            lambda half, column, place: (2 * (column + gate * columns) + (place[1] ^ half), 0, 0),
        )

    def placed(half, column, place):
        return (0, (place[1] ^ half) * columns + column)

    out_block = pl.BlockSpec((rows, tile), placed)
    whole = lambda item: pl.BlockSpec(item.shape, lambda half, column, place: (0,) * item.ndim)
    return pl.pallas_call(
        functools.partial(mix_kernel, parts=len(parts), by_rows=by_rows, plain=plain, tile=tile),
        grid_spec=pltpu.PrefetchScalarGridSpec(
            num_scalar_prefetch=1,
            grid=(2, columns),
            in_specs=[whole(p) for p in parts]
            + [weight_spec(0), weight_spec(1)]
            + [pl.BlockSpec((1, 2, tile), lambda half, column, place: (half, 0, column))],
            out_specs=[
                pl.BlockSpec((rows, depth), lambda half, column, place: (0, 0)),
                out_block,
                out_block,
                out_block,
            ],
        ),
        out_shape=[
            jax.ShapeDtypeStruct((rows, depth), jnp.bfloat16),
            jax.ShapeDtypeStruct((rows, 2 * piece), jnp.bfloat16),
            jax.ShapeDtypeStruct((rows, 2 * piece), jnp.float32),
            jax.ShapeDtypeStruct((rows, 2 * piece), jnp.float32),
        ],
        compiler_params=pltpu.CompilerParams(vmem_limit_bytes=40 * 2**20),
        cost_estimate=LIGHT,
        name="mix_forward",
    )(place, *parts, weights, weights, bias)


def mix_back_kernel(place_ref, grad_ref, a_ref, t_ref, *refs):
    mixed_ref, direct_ref, sums_ref = refs[-3:]
    grad = grad_ref[...]
    a = a_ref[...]
    piece = a.shape[1]
    skip = full(jnp.concatenate([ref[...] for ref in refs[:-3]], axis=1))
    opening = opening_of(t_ref[...])
    phi, bent = gelu_parts(a)
    slope = phi + a * (0.3989422804014327 * jnp.exp(-0.5 * a * a))
    grad_a = low((1.0 - opening) * slope * grad)
    grad_t = low((skip - bent) * opening * (1.0 - opening) * grad)
    mixed_ref[0, :, :piece] = grad_a
    mixed_ref[0, :, piece:] = grad_t
    direct_ref[...] = opening * grad
    sums_ref[0, :, :piece] = jnp.sum(full(grad_a), axis=0, keepdims=True)
    sums_ref[0, :, piece:] = jnp.sum(full(grad_t), axis=0, keepdims=True)


def mix_back(place, grad, a, t, joined, parts, plain, tile=LANES):
    rows, own = grad.shape
    piece = own // 2
    placed = pl.BlockSpec((rows, piece), lambda half, place: (0, place[1] ^ half))
    if plain:
        skips = [
            pl.BlockSpec((rows, tile), lambda half, place, z=z: (0, (z * 2 + (place[1] ^ half)) * parts + place[0]))
            for z in range(piece // tile)
        ]
    else:
        skips = [pl.BlockSpec((rows, piece), lambda half, place: (0, place[0] * 2 + (place[1] ^ half)))]
    return pl.pallas_call(
        mix_back_kernel,
        grid_spec=pltpu.PrefetchScalarGridSpec(
            num_scalar_prefetch=1,
            grid=(2,),
            in_specs=[placed, placed, placed] + skips,
            out_specs=[
                pl.BlockSpec((1, rows, own), lambda half, place: (half, 0, 0)),
                placed,
                pl.BlockSpec((1, 1, own), lambda half, place: (half, 0, 0)),
            ],
        ),
        out_shape=[
            jax.ShapeDtypeStruct((2, rows, own), jnp.bfloat16),
            jax.ShapeDtypeStruct((rows, own), jnp.float32),
            jax.ShapeDtypeStruct((2, 1, own), jnp.float32),
        ],
        compiler_params=pltpu.CompilerParams(vmem_limit_bytes=40 * 2**20),
        cost_estimate=LIGHT,
        name="mix_backward",
    )(place, grad, a, t, *[joined] * len(skips))


def inner_product(mixed_ref, weight_refs):
    blocks = len(weight_refs) // 2
    own = jnp.concatenate([ref[0] for ref in weight_refs[:blocks]], axis=1)
    other = jnp.concatenate([ref[0] for ref in weight_refs[blocks:]], axis=1)
    return dot_nt(mixed_ref[0], own) + dot_nt(mixed_ref[1], other)


def inner_specs(blocks, depth, tile, row_block):
    specs = []
    for flip in (0, 1):
        for z in range(blocks):
            specs.append(
                pl.BlockSpec(
                    (1, depth, tile),
                    lambda i, place, z=z, flip=flip: (2 * z + (place[1] ^ flip), row_block(i, place), 0),
                )
            )
    return specs


def inner_columns_kernel(place_ref, mixed_ref, *refs):
    out_ref = refs[-1]
    out_ref[0] = inner_product(mixed_ref, refs[:-1]).astype(out_ref.dtype)


def inner_columns(place, mixed, weights, odd, parts, dtype):
    _, rows, wide_columns = mixed.shape
    blocks, filters, tile = weights.shape
    blocks = blocks // 2
    depth = filters // parts
    return pl.pallas_call(
        inner_columns_kernel,
        grid_spec=pltpu.PrefetchScalarGridSpec(
            num_scalar_prefetch=1,
            grid=(parts // 2,),
            in_specs=[pl.BlockSpec(mixed.shape, lambda i, place: (0, 0, 0))]
            + inner_specs(blocks, depth, tile, lambda i, place: place[0] ^ (2 * i + odd)),
            out_specs=pl.BlockSpec((1, rows, depth), lambda i, place: (i, 0, 0)),
        ),
        out_shape=jax.ShapeDtypeStruct((parts // 2, rows, depth), dtype),
        compiler_params=pltpu.CompilerParams(vmem_limit_bytes=40 * 2**20),
        cost_estimate=LIGHT,
        name="inner_columns",
    )(place, mixed, *[weights] * (2 * blocks))


def inner_rows_kernel(place_ref, mixed_ref, *refs, parts, plain, tile):
    direct_ref, sent_ref, kept_ref, held_ref = refs[-4:]
    mine = place_ref[0]
    held_ref[...] = inner_product(mixed_ref, refs[:-4])

    step = pl.program_id(0)
    if plain:
        at = pl.ds(pl.multiple_of(mine * tile, tile), tile)
        column = (step % 2) * (pl.num_programs(0) // 2) + step // 2
        held_ref[:, at] += direct_ref[:, pl.ds(pl.multiple_of(column * tile, tile), tile)]
    else:

        @pl.when(step == mine)
        def _():
            held_ref[...] += direct_ref[...]

    extent = held_ref.shape[0] // parts
    for k in range(parts):
        got = held_ref[pl.ds(pl.multiple_of((mine ^ k) * extent, extent), extent), :]
        if k % 2:
            sent_ref[k // 2] = low(got)
        else:
            kept_ref[k // 2] = got


def inner_rows(place, mixed, weights, direct, parts, plain):
    _, rows, wide_columns = mixed.shape
    blocks, filters, tile = weights.shape
    blocks = blocks // 2
    depth = filters // parts
    extent = rows // parts
    out = pl.BlockSpec((parts // 2, extent, depth), lambda j, place: (0, 0, j))
    return pl.pallas_call(
        functools.partial(inner_rows_kernel, parts=parts, plain=plain, tile=tile),
        grid_spec=pltpu.PrefetchScalarGridSpec(
            num_scalar_prefetch=1,
            grid=(parts,),
            in_specs=[pl.BlockSpec(mixed.shape, lambda j, place: (0, 0, 0))]
            + inner_specs(blocks, depth, tile, lambda j, place: j)
            + [pl.BlockSpec(direct.shape, lambda j, place: (0, 0))],
            out_specs=[out, out],
            scratch_shapes=[pltpu.VMEM((rows, depth), jnp.float32)],
        ),
        out_shape=[
            jax.ShapeDtypeStruct((parts // 2, extent, filters), jnp.bfloat16),
            jax.ShapeDtypeStruct((parts // 2, extent, filters), jnp.float32),
        ],
        compiler_params=pltpu.CompilerParams(vmem_limit_bytes=40 * 2**20),
        cost_estimate=LIGHT,
        name="inner_rows",
    )(place, mixed, *[weights] * (2 * blocks), direct)


def widen_kernel(sums_ref, out_ref, *, parts):
    filters, tile = out_ref.shape[1:]
    outer = filters // (2 * parts * tile)
    for z in range(outer):
        for pair in range(2):
            for m in range(parts):
                at = ((z * 2 + pair) * parts + m) * tile
                source = filters + ((m * 2 + pair) * outer + z) * tile
                out_ref[0, at : at + tile, :] = sums_ref[:, at : at + tile].T
                out_ref[1, at : at + tile, :] = sums_ref[:, source : source + tile].T


def widen(sums, filters, parts):
    return pl.pallas_call(
        functools.partial(widen_kernel, parts=parts),
        out_shape=jax.ShapeDtypeStruct((2, filters, sums.shape[0]), jnp.float32),
        compiler_params=pltpu.CompilerParams(vmem_limit_bytes=16 * 2**20),
        cost_estimate=LIGHT,
        name="widen",
    )(sums)


def slope_of(values):
    phi = 0.5 * (1.0 + lax.erf(values * 0.7071067811865476))
    return phi + values * (0.3989422804014327 * jnp.exp(-0.5 * values * values))


def ffn_forward_kernel(x_ref, *refs, tile):
    out_ref, own_ref = refs[-2:]
    step = pl.program_id(0)
    for k, (up_ref, down_ref, bias_ref) in enumerate(zip(refs[:-2:3], refs[1:-2:3], refs[2:-2:3])):

        @pl.when(step == k)
        def _(k=k, up_ref=up_ref, down_ref=down_ref, bias_ref=bias_ref):
            for first in range(0, x_ref.shape[0], tile):
                at = slice(first, first + tile)
                value = jnp.dot(x_ref[at, :], up_ref[...], preferred_element_type=jnp.float32)
                active = low(gelu_parts(value + full(bias_ref[0:1, :]))[1])
                added = jnp.dot(active, down_ref[...], preferred_element_type=jnp.float32)
                if k == 0:
                    out_ref[at, :] = added
                    own_ref[at, :] = active
                else:
                    out_ref[at, :] += added


def ffn_operands(parts, units):
    width = parts[0].shape[1]
    last = (parts[0].shape[0] - 16) // 16
    specs = [
        pl.BlockSpec((units, width), lambda k: (0, 0)),
        pl.BlockSpec((units, width), lambda k: (1, 0)),
        pl.BlockSpec((16, width), lambda k: (last, 0)),
    ]
    return specs * len(parts), [part for part in parts for _ in range(3)]


def ffn_forward(x, parts, units, tile=256):
    rows, width = x.shape
    whole = lambda shape: pl.BlockSpec(shape, lambda k: (0,) * len(shape))
    specs, operands = ffn_operands(parts, units)
    return pl.pallas_call(
        functools.partial(ffn_forward_kernel, tile=tile),
        grid=(len(parts),),
        in_specs=[whole(x.shape)] + specs,
        out_specs=[whole((rows, width)), whole((rows, units))],
        out_shape=[
            jax.ShapeDtypeStruct((rows, width), jnp.float32),
            jax.ShapeDtypeStruct((rows, units), jnp.bfloat16),
        ],
        compiler_params=pltpu.CompilerParams(vmem_limit_bytes=48 * 2**20),
        cost_estimate=LIGHT,
        name="ffn_forward",
    )(x, *operands)


def ffn_backward_kernel(x_ref, grad_ref, *refs, tile):
    out_ref, own_ref, sums_ref = refs[-3:]
    step = pl.program_id(0)
    for k, (up_ref, down_ref, bias_ref) in enumerate(zip(refs[:-3:3], refs[1:-3:3], refs[2:-3:3])):

        @pl.when(step == k)
        def _(k=k, up_ref=up_ref, down_ref=down_ref, bias_ref=bias_ref):
            sums = jnp.zeros(sums_ref.shape, jnp.float32)
            for first in range(0, x_ref.shape[0], tile):
                at = slice(first, first + tile)
                value = jnp.dot(x_ref[at, :], up_ref[...], preferred_element_type=jnp.float32)
                value = value + full(bias_ref[0:1, :])
                inner = low(dot_nt(grad_ref[at, :], down_ref[...]) * slope_of(value))
                added = dot_nt(inner, up_ref[...])
                if k == 0:
                    out_ref[at, :] = added
                    own_ref[at, :] = inner
                    sums = sums + jnp.sum(full(inner), axis=0, keepdims=True)
                else:
                    out_ref[at, :] += added
            if k == 0:
                sums_ref[...] = sums


def ffn_backward(x, parts, units, grad, tile=256):
    rows, width = x.shape
    whole = lambda shape: pl.BlockSpec(shape, lambda k: (0,) * len(shape))
    specs, operands = ffn_operands(parts, units)
    return pl.pallas_call(
        functools.partial(ffn_backward_kernel, tile=tile),
        grid=(len(parts),),
        in_specs=[whole(x.shape), whole(grad.shape)] + specs,
        out_specs=[whole((rows, width)), whole((rows, units)), whole((1, units))],
        out_shape=[
            jax.ShapeDtypeStruct((rows, width), jnp.float32),
            jax.ShapeDtypeStruct((rows, units), jnp.bfloat16),
            jax.ShapeDtypeStruct((1, units), jnp.float32),
        ],
        compiler_params=pltpu.CompilerParams(vmem_limit_bytes=48 * 2**20),
        cost_estimate=LIGHT,
        name="ffn_backward",
    )(x, grad, *operands)


def masked_scores(query_heads, key_heads, keep_mask, score_scale):
    scores = (
        jnp.einsum("qhd,khd->hqk", query_heads, key_heads, preferred_element_type=jnp.float32)
        * score_scale
    )
    return jnp.where(keep_mask[None, None, :] == 1, scores, NEG_FILL)


def attend(query_heads, key_heads, value_heads, keep_mask, score_scale):
    scores = masked_scores(query_heads, key_heads, keep_mask, score_scale)
    row_peak = jnp.max(scores, axis=-1, keepdims=True)
    raised = jnp.exp(scores - row_peak)
    row_total = jnp.sum(raised, axis=-1, keepdims=True)
    attn_weights = (raised / row_total).astype(jnp.bfloat16)
    context = jnp.einsum(
        "hqk,khd->qhd", attn_weights, value_heads, preferred_element_type=jnp.float32
    )
    return (context.astype(jnp.bfloat16), row_peak, row_total)


def attend_back(
    query_heads, key_heads, value_heads, keep_mask, row_peak, row_total, grad_context, score_scale
):
    scores = masked_scores(query_heads, key_heads, keep_mask, score_scale)
    probs_full = jnp.exp(scores - row_peak) / row_total
    attn_weights = probs_full.astype(jnp.bfloat16)
    grad_value = jnp.einsum(
        "hqk,qhd->khd", attn_weights, grad_context, preferred_element_type=jnp.float32
    )
    grad_weights = jnp.einsum(
        "qhd,khd->hqk", grad_context, value_heads, preferred_element_type=jnp.float32
    )
    inner_sum = jnp.sum(grad_weights * probs_full, axis=-1, keepdims=True)
    grad_scores = (probs_full * (grad_weights - inner_sum)).astype(jnp.bfloat16)
    grad_query = (
        jnp.einsum("hqk,khd->qhd", grad_scores, key_heads, preferred_element_type=jnp.float32)
        * score_scale
    )
    grad_key = (
        jnp.einsum("hqk,qhd->khd", grad_scores, query_heads, preferred_element_type=jnp.float32)
        * score_scale
    )
    return (
        grad_query.astype(jnp.bfloat16),
        grad_key.astype(jnp.bfloat16),
        grad_value.astype(jnp.bfloat16),
    )


def per_device(
    char_ids,
    char_mask,
    position_ids,
    type_ids,
    key_mask,
    char_table,
    conv_weight,
    conv_bias,
    highway_weight,
    highway_bias,
    proj_weight,
    proj_bias,
    position_table,
    type_table,
    embed_gain,
    embed_shift,
    qkv_weight,
    qv_bias,
    out_weight,
    out_bias,
    ln1_gain,
    ln1_shift,
    up_weight,
    up_bias,
    down_weight,
    down_bias,
    ln2_gain,
    ln2_shift,
    cotangent,
):
    n_wide, n_narrow = lax.axis_size("wide"), lax.axis_size("narrow")
    half_wide = n_wide // 2
    me_narrow = lax.axis_index("narrow")
    wide_bits, narrow_bits = bits_of("wide"), bits_of("narrow")
    every_bit = narrow_bits + wide_bits
    falling = every_bit[::-1]
    word_total, letters = char_ids.shape
    tap_rows, own_filters = conv_weight.shape
    char_depth = char_table.shape[1]
    tap_count = tap_rows // char_depth
    filters = highway_weight.shape[1]
    own_mix = highway_weight.shape[2]
    own_width = proj_weight.shape[1]
    seq_length = position_table.shape[0]
    group = word_total * n_narrow
    own_hidden = half_wide * own_mix

    outer = n_wide // 2
    quarter = outer // 2
    outer_groups = [[2 * z + y for z in range(outer)] for y in range(2)]
    me_pair = my_bit("wide", 0)

    def grouped(item):
        split = item.reshape((quarter, 2, n_narrow, own_mix) + item.shape[1:])
        return split.transpose((2, 1, 0, 3) + tuple(range(4, split.ndim))).reshape(item.shape)

    def ungrouped(item):
        split = item.reshape((n_narrow, 2, quarter, own_mix) + item.shape[1:])
        return split.transpose((2, 1, 0, 3) + tuple(range(4, split.ndim))).reshape(item.shape)

    tiled = own_mix == LANES
    corner = jnp.stack([me_narrow, me_pair]).astype(jnp.int32)

    def gather_mix(shard):
        blocks = lax.all_gather(shard, "wide", axis=0)
        if tiled:
            return blocks
        blocks = blocks.reshape(-1, LANES // own_mix, 2, filters, own_mix).transpose(0, 2, 3, 1, 4)
        return blocks.reshape(-1, filters, LANES)

    plain = tiled and half_wide == n_narrow
    ordered, unordered = (lambda item: item, lambda item: item) if plain else (grouped, ungrouped)
    mix_weights = [gather_mix(ordered(highway_weight[0]))]
    mix_weights.append(gather_mix(after(grouped(highway_weight[1]), mix_weights[0])))
    conv_block = jnp.zeros((own_filters, LANES), jnp.bfloat16)
    conv_block = conv_block.at[:, :tap_rows].set(conv_weight.T)
    conv_block = conv_block.at[:, tap_rows + tap_count].set(conv_bias)
    bias_block = jnp.pad(highway_bias, ((0, 0), (0, LANES - own_mix)))
    conv_spread = spread(jnp.concatenate([conv_block, bias_block]), falling)
    filt_rows = ordered(conv_spread[:, :own_filters].reshape(filters, LANES))
    mix_bias = conv_spread[:, own_filters:, :own_mix].reshape(outer, 2, n_narrow, 2, own_mix)
    mix_bias = full(lax.dynamic_index_in_dim(mix_bias, me_narrow, 2, keepdims=False))
    mix_bias = [lax.dynamic_index_in_dim(mix_bias, me_pair ^ half, 1, keepdims=False) for half in range(2)]
    mix_bias = jnp.stack(mix_bias).transpose(2, 0, 1, 3).reshape(2, 2, 2, quarter * own_mix)
    vector_block = jnp.stack([proj_bias, type_table[0], type_table[1], embed_gain, embed_shift], axis=1)
    vector_block = jnp.pad(vector_block, ((0, 0), (0, LANES - vector_block.shape[1])))
    rest = jnp.concatenate([grouped(proj_weight).T, position_table.T, vector_block], axis=1)[None]
    rest_bits = wide_bits[::-1]
    rest = doubled(rest, *rest_bits[0], 1).reshape((-1,) + rest.shape[1:])
    widths = ordered(filter_widths(filters))
    lane = jnp.arange(LANES)
    tap_keep = (lane[None, :] // char_depth) < widths[:, None]
    late = lane - tap_rows
    shut = (late == 0)[None, :] | (
        (late >= 1)[None, :] & (late < tap_count)[None, :] & (widths[:, None] > late[None, :])
    )
    is_bias = (late == tap_count)[None, :]
    filt_rows = jnp.where(
        (tap_keep & (late < 0)[None, :]) | is_bias,
        filt_rows,
        jnp.where(shut, jnp.bfloat16(SHUT), jnp.bfloat16(0.0)),
    )
    vocab = char_table.shape[0]
    vocab_rows = -(-vocab // 16) * 16
    id_row = char_ids.T.reshape(1, letters * word_total)
    hot = (jnp.arange(vocab_rows)[:, None] == id_row).astype(jnp.bfloat16)
    table_t = jnp.pad(char_table, ((0, vocab_rows - vocab), (0, 0))).T
    embedded = low(jnp.dot(table_t, hot, preferred_element_type=jnp.float32))
    embedded = jnp.pad(embedded, ((0, 0), (0, tap_count * word_total)))
    span = letters * word_total
    tap_blocks = [embedded[:, t * word_total : t * word_total + span] for t in range(tap_count)]
    place = jnp.arange(letters)
    usable = (char_mask == 1) | (place[None, :] == 0)
    unusable_row = low(~usable).T.reshape(1, span)
    late_rows = low(place[None, :] == letters - jnp.arange(1, tap_count)[:, None])
    late_rows = jnp.repeat(late_rows, word_total, axis=1)
    columns_t = jnp.concatenate(
        tap_blocks
        + [
            unusable_row,
            late_rows,
            jnp.ones((1, span), jnp.bfloat16),
            jnp.zeros((LANES - tap_rows - tap_count - 1, span), jnp.bfloat16),
        ]
    )
    columns = columns_t.T.reshape(letters, word_total, LANES)
    tally = jnp.stack(
        [jnp.sum(full(usable[:, : letters - w + 1]), axis=1) for w in range(1, tap_count + 1)], axis=1
    )
    width_hot = full(jnp.arange(1, tap_count + 1)[:, None] == widths[None, :])
    valid_count = jnp.dot(tally, width_hot)

    def rest_step(rest, which):
        return doubled(rest, *which, 1).reshape((-1,) + rest.shape[1:])

    rest = after(rest, conv_spread)
    for which in rest_bits[1:-1]:
        rest = rest_step(rest, which)
    units = up_weight.shape[1]
    encoder_pack = jnp.concatenate(
        [up_weight, down_weight, out_weight, jnp.broadcast_to(up_bias[None], (16, units))]
    )
    encoder_parts = [encoder_pack, swap(encoder_pack, "narrow", 1)]
    filt_rows, encoder_parts = lax.optimization_barrier((filt_rows, encoder_parts))
    lse = pool_forward(columns, filt_rows)
    rest = rest_step(after(rest, lse), rest_bits[-1])
    pooled = lse - jnp.log(valid_count)
    features = low(smooth_gelu(pooled))

    parts = near_parts(features, "narrow")
    near_order = [0, 2, 1, 3]
    cotangent_rows = lax.all_gather(
        after(cotangent, mix_weights[1]), "narrow", axis=0, tiled=True
    )
    rest = after(rest, parts[-1])

    def narrowed(rest, bit):
        width = own_hidden << bit
        mine = my_bit("narrow", bit)
        tail = rest[..., 2 * width :]
        kept = lax.dynamic_slice_in_dim(rest, mine * width, width, rest.ndim - 1)
        sent = lax.dynamic_slice_in_dim(rest, (1 - mine) * width, width, rest.ndim - 1)
        kept, sent = (jnp.concatenate([item, tail], axis=-1) for item in (kept, sent))
        got = swap(sent, "narrow", bit)
        high = mine == 1
        pair = jnp.stack([jnp.where(high, got, kept), jnp.where(high, kept, got)], axis=1)
        return pair.reshape((-1,) + pair.shape[2:])

    rest = narrowed(rest, 1)
    highway_saved, pair_parts = [], [swap(features, "wide", 0)]
    for layer_index in range(2):
        joined, hidden, kept_a, kept_t = mix_forward(
            corner, parts, mix_weights[layer_index], mix_bias[layer_index], layer_index == 0, plain and layer_index == 0
        )
        highway_saved.append((joined, kept_a, kept_t))
        if layer_index == 0:
            parts = near_parts(hidden, "narrow")
            pair_parts.append(swap(hidden, "wide", 0))
            rest = narrowed(after(rest, hidden), 0)
            encoder_parts = encoder_parts + [
                swap(item, "narrow", 0) for item in after(encoder_parts, hidden)
            ]
            parts, encoder_parts = lax.optimization_barrier((parts, encoder_parts))
    rest, proj_input = lax.optimization_barrier((rest, hidden))
    rest = rest.reshape(n_wide * n_narrow * own_width, -1)
    model_width = rest.shape[0]
    proj_own = rest[:, :own_hidden]
    position_rows = rest[:, own_hidden : own_hidden + seq_length]
    vectors = full(rest[:, own_hidden + seq_length :].T)
    proj_shift, type_low, type_high, first_gain, first_shift = (vectors[i] for i in range(5))
    projected = fold(dot_nt(proj_input, proj_own).reshape(n_narrow, word_total, model_width), narrow_bits)
    projected, cotangent_rows = lax.optimization_barrier((projected, cotangent_rows))
    position_hot = (position_ids[:, None] == jnp.arange(seq_length)[None, :]).astype(jnp.bfloat16)
    type_rows = jnp.where(type_ids[:, None] == 1, type_high, type_low)
    summed = projected + proj_shift + dot_nt(position_hot, position_rows) + type_rows
    first_state, first_pull = jax.vjp(layer_norm, summed, first_gain, first_shift)

    gathered = lax.all_gather(low(first_state), "narrow", axis=0, tiled=True)
    group_rows = gathered.shape[0]
    qkv_out = jnp.einsum("gd,kdc->kgc", gathered, qkv_weight, preferred_element_type=jnp.float32)
    local_width = qkv_out.shape[2]
    head_count = local_width // HEAD_DIM
    seq_shape = (group_rows, head_count, HEAD_DIM)
    query_heads = low(qkv_out[0] + full(qv_bias[0])).reshape(seq_shape)
    key_heads = low(qkv_out[1]).reshape(seq_shape)
    value_heads = low(qkv_out[2] + full(qv_bias[1])).reshape(seq_shape)
    score_scale = HEAD_DIM ** (-0.5)
    keep_mask = key_mask[0]
    context, row_peak, row_total = attend(query_heads, key_heads, value_heads, keep_mask, score_scale)
    context_rows = context.reshape(group_rows, local_width)

    def by_owner(partial):
        return fold(partial.reshape(n_narrow, word_total, model_width), narrow_bits)

    def own_words(rows):
        return lax.dynamic_slice_in_dim(rows, me_narrow * word_total, word_total, 0)

    attn_branch = full(out_bias)
    for k, part in zip(near_order, near_parts(context_rows, "narrow")):
        weight = encoder_parts[k][2 * units : 2 * units + local_width]
        attn_branch = attn_branch + jnp.dot(part, weight, preferred_element_type=jnp.float32)
    second_state, second_pull = jax.vjp(
        layer_norm, full(gathered) + attn_branch, full(ln1_gain), full(ln1_shift)
    )
    pair_parts, ffn_input = lax.optimization_barrier((pair_parts, low(second_state)))
    ffn_branch, activated = ffn_forward(ffn_input, encoder_parts, units)
    layer_out, third_pull = jax.vjp(
        layer_norm, second_state + (ffn_branch + full(down_bias)), full(ln2_gain), full(ln2_shift)
    )
    layer_out = own_words(layer_out)

    def pair_start(halves):
        kept = lax.dynamic_index_in_dim(halves, me_pair, 0, keepdims=False)
        sent = lax.dynamic_index_in_dim(halves, 1 - me_pair, 0, keepdims=False)
        return kept, swap(sent, "wide", 0)

    def pair_end(mine, back):
        first = me_pair == 0
        return jnp.stack([full(jnp.where(first, mine, back)), full(jnp.where(first, back, mine))])

    grad_third, grad_ln2_gain, grad_ln2_shift = third_pull(cotangent_rows)
    grad_ffn = low(grad_third)
    grad_down_bias = jnp.sum(full(grad_ffn), axis=0)
    grad_down_weight = jnp.einsum("gf,gd->fd", activated, grad_ffn, preferred_element_type=jnp.float32)
    grad_inner, grad_up, grad_up_bias = ffn_backward(ffn_input, encoder_parts, units, grad_ffn)
    grad_up_weight = jnp.einsum("gd,gf->df", ffn_input, grad_up, preferred_element_type=jnp.float32)
    grad_second = grad_third + grad_inner
    ffn_kept, ffn_received = pair_start(jnp.stack([low(grad_up_weight), low(grad_down_weight)]))
    grad_first_branch, grad_ln1_gain, grad_ln1_shift = second_pull(grad_second)
    pair_parts = [near_parts(after(item, ffn_branch), "narrow") for item in pair_parts]
    pair_parts, grad_attn = lax.optimization_barrier((pair_parts, low(grad_first_branch)))
    pair_joined = [
        in_order(item, "narrow", layer_index) for layer_index, item in enumerate(pair_parts)
    ]
    grad_out_bias = jnp.sum(full(grad_attn), axis=0)
    grad_attn_rows = grad_attn
    grad_out_weight = jnp.einsum(
        "gc,gd->cd", context_rows, grad_attn_rows, preferred_element_type=jnp.float32
    )
    grad_context = low(dot_nt(grad_attn_rows, out_weight)).reshape(seq_shape)
    grad_query, grad_key, grad_value = attend_back(
        query_heads, key_heads, value_heads, keep_mask, row_peak, row_total, grad_context, score_scale
    )
    grad_joined = jnp.stack(
        [item.reshape(group_rows, local_width) for item in (grad_query, grad_key, grad_value)]
    )
    grad_qv_bias = jnp.stack(
        [jnp.sum(full(grad_joined[0]), axis=0), jnp.sum(full(grad_joined[2]), axis=0)]
    )
    grad_qkv_weight = jnp.einsum(
        "kgc,gd->kcd", grad_joined, gathered, preferred_element_type=jnp.float32
    )
    attn_kept, attn_received = pair_start(
        jnp.concatenate([low(grad_qkv_weight), low(grad_out_weight)[None]]).reshape(2, -1, model_width)
    )
    grad_first = own_words(grad_first_branch) + by_owner(
        jnp.einsum("kgc,kdc->gd", grad_joined, qkv_weight, preferred_element_type=jnp.float32)
    )
    grad_summed, grad_embed_gain, grad_embed_shift = first_pull(grad_first)

    grad_proj_low = low(grad_summed)
    grad_position = jnp.einsum(
        "td,tl->dl", grad_proj_low, position_hot, preferred_element_type=jnp.float32
    )
    is_high = type_ids[:, None] == 1
    vector_grads = jnp.stack(
        [
            jnp.sum(full(grad_proj_low), axis=0),
            jnp.sum(jnp.where(is_high, 0.0, grad_summed), axis=0),
            jnp.sum(jnp.where(is_high, grad_summed, 0.0), axis=0),
            grad_embed_gain,
            grad_embed_shift,
        ],
        axis=1,
    )
    vector_grads = jnp.pad(low(vector_grads), ((0, 0), (0, LANES - vector_grads.shape[1])))
    grad_proj_rows = lax.all_gather(grad_proj_low, "narrow", axis=0, tiled=True)
    grad_proj_weight = jnp.einsum(
        "gd,gh->dh", grad_proj_rows, proj_input, preferred_element_type=jnp.float32
    )
    table_grads = [
        item.reshape(n_wide, n_narrow, own_width, -1).transpose(1, 0, 2, 3)
        for item in (low(grad_position), vector_grads, low(grad_proj_weight))
    ]
    table_grads = jnp.concatenate(table_grads, axis=3)
    table_grads = lax.all_to_all(table_grads, "narrow", 0, 0, tiled=True)
    table_width = seq_length + LANES
    table_sums = jnp.sum(full(table_grads[..., :table_width]), axis=0)
    proj_parts = table_grads[..., table_width:].transpose(1, 0, 2, 3)
    rest_grads = [item.reshape(n_wide, LANES, -1) for item in (low(table_sums), proj_parts)]
    table_columns = rest_grads[0].shape[2]
    rest_grads = jnp.concatenate(rest_grads, axis=2)
    grad_hidden = jnp.dot(grad_proj_rows, proj_own, preferred_element_type=jnp.float32)

    mix_bias_grads = [None, None]

    def weight_part(joined, mixed):
        return jnp.einsum(
            "tk,tzc->zck",
            joined,
            mixed.reshape(group, outer, own_mix),
            preferred_element_type=jnp.float32,
        )

    def pair_weight(layer_index, mixed, met):
        joined = highway_saved[layer_index][0]
        return low(weight_part(joined, mixed[0]) + weight_part(pair_joined[layer_index], met))

    ffn_received, attn_received = after((ffn_received, attn_received), grad_hidden)
    pair_sums = lax.psum(
        (low(full(ffn_kept) + full(ffn_received)), low(full(attn_kept) + full(attn_received))),
        "wide",
        axis_index_groups=outer_groups,
    )
    joined, kept_a, kept_t = highway_saved[1]
    mixed, direct, mix_bias_grads[1] = mix_back(corner, grad_hidden, kept_a, kept_t, joined, n_narrow, False)
    met = swap(mixed[1], "wide", 0)
    sent = inner_columns(corner, mixed, mix_weights[1], 1, n_narrow, jnp.bfloat16)
    kept = inner_columns(corner, mixed, mix_weights[1], 0, n_narrow, jnp.float32)
    grad_hidden = direct + fold_near(sent, kept, "narrow")
    weight_second = pair_weight(1, mixed, after(met, grad_hidden))
    joined, kept_a, kept_t = highway_saved[0]
    mixed, direct, mix_bias_grads[0] = mix_back(corner, grad_hidden, kept_a, kept_t, joined, n_narrow, plain)
    met = swap(mixed[1], "wide", 0)
    sent, kept = inner_rows(corner, mixed, mix_weights[0], direct, n_narrow, plain)
    grad_features = fold_near(sent, kept, "narrow")

    rest_grads = low(halved(after(rest_grads, direct), *wide_bits[0]))
    weight_first = pair_weight(0, mixed, met)
    both = [item.reshape(outer, LANES, -1) for item in (weight_first, weight_second)]
    weight_columns = both[0].shape[2]
    both = jnp.concatenate(both + [rest_grads], axis=2)
    grad_features, both, pair_sums = lax.optimization_barrier((grad_features, both, pair_sums))

    grad_pooled = jax.vjp(smooth_gelu, pooled)[1](grad_features)[0]
    filt_grads, hot_grads = pool_backward(
        columns, columns_t, hot, filt_rows, lse, grad_pooled, char_depth, tap_count
    )
    both = lax.psum_scatter(both, "wide", scatter_dimension=0, axis_index_groups=outer_groups)
    both = full(both)
    if plain:
        owned_highway = widen(both, filters, n_narrow)
    else:
        owned_highway = [
            both[:, at * weight_columns : (at + 1) * weight_columns].reshape(own_mix, filters).T
            for at in range(2)
        ]
        owned_highway = jnp.stack([unordered(owned_highway[0]), ungrouped(owned_highway[1])])
    owned_rest = both[:, 2 * weight_columns :]
    table_grads = owned_rest[:, :table_columns].reshape(own_width, table_width)
    owned_proj = owned_rest[:, table_columns:].reshape(n_narrow, own_width, own_hidden).transpose(0, 2, 1)
    owned_proj = ungrouped(owned_proj.reshape(filters, own_width))
    filt_grads = unordered(low(jnp.where(tap_keep | is_bias, filt_grads, 0.0)))
    grad_table = hot_grads[:vocab, :tap_rows].reshape(vocab, tap_count, char_depth).sum(axis=1)
    mix_bias_grads = jnp.stack(mix_bias_grads).reshape(2, 2, outer, own_mix)
    swapped = jnp.stack([jnp.where(me_pair == 0, mix_bias_grads[:, y], mix_bias_grads[:, 1 - y]) for y in range(2)], axis=2)
    mix_bias_grads = swapped.reshape(2, n_wide, own_mix)
    wide_parts = [
        mix_bias_grads,
        grad_up_bias[0],
        grad_qv_bias,
        grad_out_bias,
        grad_ln1_gain,
        grad_ln1_shift,
        grad_down_bias,
        grad_ln2_gain,
        grad_ln2_shift,
    ]
    all_parts = [grad_table]

    def joined_rows(parts):
        flat = jnp.concatenate([item.reshape(-1) for item in parts])
        return jnp.pad(flat, (0, -flat.shape[0] % LANES)).reshape(-1, LANES)

    def parted(flat, parts):
        flat, done, start = flat.reshape(-1), [], 0
        for item in parts:
            done.append(flat[start : start + item.size].reshape(item.shape))
            start += item.size
        return done

    wide_flat, all_flat = joined_rows(wide_parts), joined_rows(all_parts)
    flat = total(jnp.concatenate([wide_flat, all_flat]), wide_bits[:1])
    filt_grads = halved(filt_grads.reshape(n_wide, -1, LANES), *wide_bits[0])
    flat, filt_grads = lax.optimization_barrier((flat, filt_grads))
    filt_grads = fold(filt_grads, wide_bits[1:])
    owned_filt = lax.all_to_all(
        low(filt_grads).reshape(n_narrow, own_filters, LANES), "narrow", 0, 0, tiled=True
    )
    owned_filt = jnp.sum(full(owned_filt), axis=0)
    owned_conv = owned_filt[:, :tap_rows].T
    owned_conv_bias = owned_filt[:, tap_rows + tap_count]

    flat, pair_backs = lax.optimization_barrier(
        (total(flat, wide_bits[1:]), [swap(item, "wide", 0) for item in pair_sums])
    )
    (
        mix_sums,
        sum_up_bias,
        sum_qv_bias,
        sum_out_bias,
        sum_ln1_gain,
        sum_ln1_shift,
        sum_down_bias,
        sum_ln2_gain,
        sum_ln2_shift,
    ) = parted(flat[: wide_flat.shape[0]], wide_parts)
    owned_mix_bias = lax.dynamic_index_in_dim(mix_sums, lax.axis_index("wide"), 1, keepdims=False)
    sum_table = parted(total(flat[wide_flat.shape[0] :], narrow_bits), all_parts)[0]
    ffn_sums, attn_sums = (pair_end(mine, back) for mine, back in zip(pair_sums, pair_backs))
    attn_sums = attn_sums.reshape(n_narrow, local_width, model_width)
    owned_vectors = table_grads[:, seq_length : seq_length + 5].T
    return (
        layer_out,
        sum_table,
        owned_conv,
        owned_conv_bias,
        owned_highway,
        owned_mix_bias,
        owned_proj,
        owned_vectors[0],
        table_grads[:, :seq_length].T,
        owned_vectors[1:3],
        owned_vectors[3],
        owned_vectors[4],
        attn_sums[:3].transpose(0, 2, 1),
        sum_qv_bias,
        attn_sums[3],
        sum_out_bias,
        sum_ln1_gain,
        sum_ln1_shift,
        ffn_sums[0],
        sum_up_bias,
        ffn_sums[1],
        sum_down_bias,
        sum_ln2_gain,
        sum_ln2_shift,
    )


def solution(mesh):
    return jax.shard_map(
        per_device,
        mesh=mesh,
        in_specs=(
            P(("wide", "narrow"), None),
            P(("wide", "narrow"), None),
            P(("wide", "narrow")),
            P(("wide", "narrow")),
            P("wide", None),
            P(),
            P(None, ("wide", "narrow")),
            P(("wide", "narrow")),
            P(None, None, ("wide", "narrow")),
            P(None, ("wide", "narrow")),
            P(None, ("wide", "narrow")),
            P(("wide", "narrow")),
            P(None, ("wide", "narrow")),
            P(None, ("wide", "narrow")),
            P(("wide", "narrow")),
            P(("wide", "narrow")),
            P(None, None, "narrow"),
            P(None, "narrow"),
            P("narrow", None),
            P(),
            P(),
            P(),
            P(None, "narrow"),
            P("narrow"),
            P("narrow", None),
            P(),
            P(),
            P(),
            P(("wide", "narrow"), None),
        ),
        out_specs=(
            P(("wide", "narrow"), None),
            P(),
            P(None, ("wide", "narrow")),
            P(("wide", "narrow")),
            P(None, None, ("wide", "narrow")),
            P(None, ("wide", "narrow")),
            P(None, ("wide", "narrow")),
            P(("wide", "narrow")),
            P(None, ("wide", "narrow")),
            P(None, ("wide", "narrow")),
            P(("wide", "narrow")),
            P(("wide", "narrow")),
            P(None, None, "narrow"),
            P(None, "narrow"),
            P("narrow", None),
            P(),
            P(),
            P(),
            P(None, "narrow"),
            P("narrow"),
            P("narrow", None),
            P(),
            P(),
            P(),
        ),
        check_vma=False,
    )
```

```python
import functools

import jax
import jax.numpy as jnp
from jax import lax
from jax.experimental import pallas as pl
from jax.experimental.pallas import tpu as pltpu
from jax.sharding import PartitionSpec as P

HEAD_DIM = 64
EPSILON = 1e-05
NEG_FILL = -1000000000.0
SHUT = -1e30
LANES = 128
LIGHT = pl.CostEstimate(flops=1000, bytes_accessed=1000, transcendentals=0)


def layer_norm(values, gain, shift):
    centre = values - jnp.mean(values, axis=-1, keepdims=True)
    spread = jnp.mean(centre * centre, axis=-1, keepdims=True)
    return centre * lax.rsqrt(spread + EPSILON) * gain + shift


def smooth_gelu(values):
    return jax.nn.gelu(values, approximate=False)


def low(values):
    return values.astype(jnp.bfloat16)


def full(values):
    return values.astype(jnp.float32)


def filter_widths(filter_total):
    index = jnp.arange(filter_total)
    widths = jnp.ones((filter_total,), jnp.int32)
    for level in range(6):
        widths = widths + (index >= filter_total * 2**level // 64).astype(jnp.int32)
    return widths


def swap(block, axis, bit):
    size = lax.axis_size(axis)
    return lax.ppermute(block, axis, [(i, i ^ (1 << bit)) for i in range(size)])


def after(value, *others):
    return lax.optimization_barrier((value,) + others)[0]


def my_bit(axis, bit):
    return (lax.axis_index(axis) >> bit) & 1


def bits_of(axis):
    return [(axis, bit) for bit in range(lax.axis_size(axis).bit_length() - 1)]


def spread(block, bits):
    shape = block.shape
    held = block[None]
    for axis, bit in bits:
        other = swap(held, axis, bit)
        high = my_bit(axis, bit) == 1
        held = jnp.stack([jnp.where(high, other, held), jnp.where(high, held, other)], axis=1)
        held = held.reshape((-1,) + shape)
    return held


def doubled(block, axis, bit, depth):
    other = swap(block, axis, bit)
    high = my_bit(axis, bit) == 1
    return jnp.stack([jnp.where(high, other, block), jnp.where(high, block, other)], axis=depth)


def halved(parts, axis, bit):
    pairs = parts.reshape((-1, 2) + parts.shape[1:])
    mine = my_bit(axis, bit)
    kept = lax.dynamic_index_in_dim(pairs, mine, 1, keepdims=False)
    sent = low(lax.dynamic_index_in_dim(pairs, 1 - mine, 1, keepdims=False))
    return full(kept) + full(swap(sent, axis, bit))


def fold(parts, bits):
    for axis, bit in bits:
        parts = halved(parts, axis, bit)
    return parts[0]


def near_parts(block, axis):
    parts = [block]
    for bit in reversed(range(lax.axis_size(axis).bit_length() - 1)):
        parts = [item for part in parts for item in (part, swap(part, axis, bit))]
    return parts


def in_order(parts, axis, dim):
    mine = lax.axis_index(axis)
    blocks = []
    for m in range(len(parts)):
        held, count = parts, len(parts)
        for bit in range(count.bit_length() - 1):
            here = ((mine >> bit) & 1) == ((m >> bit) & 1)
            held = [jnp.where(here, even, odd) for even, odd in zip(held[::2], held[1::2])]
        blocks.append(held[0])
    return jnp.concatenate(blocks, axis=dim)


def fold_near(sent, kept, axis):
    whole = full(kept) + full(swap(sent, axis, 0))
    for bit in range(1, lax.axis_size(axis).bit_length() - 1):
        pairs = whole.reshape((-1, 2) + whole.shape[1:])
        whole = pairs[:, 0] + full(swap(low(pairs[:, 1]), axis, bit))
    return whole[0]


def total(value, bits):
    for axis, bit in bits:
        value = value + swap(value, axis, bit)
    return value


def dot_nt(left, right):
    return lax.dot_general(left, right, (((1,), (1,)), ((), ())), preferred_element_type=jnp.float32)


def pool_kernel(cols_ref, filt_ref, lse_ref, *, group):
    letters = cols_ref.shape[0]
    filt = filt_ref[...]
    peak = None
    for first in range(0, letters, group):
        scores = [dot_nt(cols_ref[p], filt) for p in range(first, min(first + group, letters))]
        top = functools.reduce(jnp.maximum, scores)
        if peak is None:
            peak = top
            mass = functools.reduce(jnp.add, [jnp.exp(s - peak) for s in scores])
        else:
            later = jnp.maximum(peak, top)
            fresh = functools.reduce(jnp.add, [jnp.exp(s - later) for s in scores])
            mass = mass * jnp.exp(peak - later) + fresh
            peak = later
    lse_ref[...] = peak + jnp.log(mass)


def pool_forward(columns, filt_rows, block=256):
    letters, words, depth = columns.shape
    filters = filt_rows.shape[0]
    return pl.pallas_call(
        functools.partial(pool_kernel, group=5),
        grid=(filters // block,),
        in_specs=[
            pl.BlockSpec(columns.shape, lambda i: (0, 0, 0)),
            pl.BlockSpec((block, depth), lambda i: (i, 0)),
        ],
        out_specs=pl.BlockSpec((words, block), lambda i: (0, i)),
        out_shape=jax.ShapeDtypeStruct((words, filters), jnp.float32),
        compiler_params=pltpu.CompilerParams(vmem_limit_bytes=48 * 2**20),
        cost_estimate=LIGHT,
        name="pool_forward",
    )(columns, filt_rows)


def back_kernel(
    cols_ref, cols_t_ref, hot_ref, filt_ref, lse_ref, grad_ref, dw_ref, table_ref, gcol_ref, *, depth, taps
):
    letters, words, lanes = cols_ref.shape
    step = pl.program_id(0)
    filt = filt_ref[...]
    lse = lse_ref[...]
    grad = grad_ref[...]

    @pl.when(step == 0)
    def _():
        gcol_ref[...] = jnp.zeros_like(gcol_ref)

    half = letters // 2
    weight_sum = jnp.zeros((lanes, filt.shape[0]), jnp.float32)
    for first, last in ((0, half), (half, letters)):
        slots = jnp.concatenate(
            [low(grad * jnp.exp(dot_nt(cols_ref[p], filt) - lse)) for p in range(first, last)], axis=0
        )
        at = slice(first * words, last * words)
        gcol_ref[at, :] += jnp.dot(slots, filt, preferred_element_type=jnp.float32)
        weight_sum += jnp.dot(cols_t_ref[:, at], slots, preferred_element_type=jnp.float32)
    dw_ref[...] = weight_sum.T

    @pl.when(step == pl.num_programs(0) - 1)
    def _():
        tap = lax.broadcasted_iota(jnp.int32, (words, lanes), 1) // depth
        table_ref[...] = jnp.zeros_like(table_ref)
        for c in range(letters):
            moved = jnp.where(tap == 0, gcol_ref[c * words : (c + 1) * words, :], 0.0)
            for t in range(1, min(taps, c + 1)):
                moved = jnp.where(tap == t, gcol_ref[(c - t) * words : (c - t + 1) * words, :], moved)
            table_ref[...] += jnp.dot(
                hot_ref[:, c * words : (c + 1) * words], low(moved), preferred_element_type=jnp.float32
            )


def pool_backward(columns, columns_t, hot, filt_rows, lse, grad, depth, taps, block=256):
    letters, words, lanes = columns.shape
    filters = filt_rows.shape[0]
    whole = lambda item: pl.BlockSpec(item.shape, lambda i: (0,) * item.ndim)
    return pl.pallas_call(
        functools.partial(back_kernel, depth=depth, taps=taps),
        grid=(filters // block,),
        in_specs=[
            whole(columns),
            whole(columns_t),
            whole(hot),
            pl.BlockSpec((block, lanes), lambda i: (i, 0)),
            pl.BlockSpec((words, block), lambda i: (0, i)),
            pl.BlockSpec((words, block), lambda i: (0, i)),
        ],
        out_specs=[
            pl.BlockSpec((block, lanes), lambda i: (i, 0)),
            pl.BlockSpec((hot.shape[0], lanes), lambda i: (0, 0)),
        ],
        out_shape=[
            jax.ShapeDtypeStruct((filters, lanes), jnp.float32),
            jax.ShapeDtypeStruct((hot.shape[0], lanes), jnp.float32),
        ],
        scratch_shapes=[pltpu.VMEM((letters * words, lanes), jnp.float32)],
        compiler_params=pltpu.CompilerParams(vmem_limit_bytes=48 * 2**20),
        cost_estimate=LIGHT,
        name="pool_backward",
    )(columns, columns_t, hot, filt_rows, lse, grad)


def gelu_parts(values):
    spread_part = 0.5 * (1.0 + lax.erf(values * 0.7071067811865476))
    return spread_part, values * spread_part


def opening_of(values):
    return 1.0 / (1.0 + jnp.exp(-values))


def mix_kernel(place_ref, *refs, parts, by_rows, plain, tile):
    part_refs = refs[:parts]
    weight_a, weight_t, bias_ref, joined_ref, hidden_ref, a_ref, t_ref = refs[parts:]
    half, column = pl.program_id(0), pl.program_id(1)
    mine, pair = place_ref[0], place_ref[1]

    @pl.when((half == 0) & (column == 0))
    def _():
        for k, part in enumerate(part_refs):
            extent = part.shape[0 if by_rows else 1]
            at = pl.ds(pl.multiple_of((mine ^ k) * extent, extent), extent)
            if by_rows:
                joined_ref[at, :] = part[...]
            else:
                joined_ref[:, at] = part[...]

    columns = pl.num_programs(1)
    if plain:
        first = ((column * 2 + (pair ^ half)) * parts + mine) * tile
    else:
        first = ((mine * 2 + (pair ^ half)) * columns + column) * tile

    weight = jnp.concatenate([weight_a[0], weight_t[0]], axis=1)
    mixture = jnp.dot(joined_ref[...], weight, preferred_element_type=jnp.float32)
    a = mixture[:, :tile] + bias_ref[0, 0:1, :]
    t = mixture[:, tile:] + bias_ref[0, 1:2, :]
    skip = full(joined_ref[:, pl.ds(pl.multiple_of(first, tile), tile)])
    opening = opening_of(t)
    hidden_ref[...] = low(opening * skip + (1.0 - opening) * gelu_parts(a)[1])
    a_ref[...] = a
    t_ref[...] = t


def mix_forward(place, parts, weights, bias, by_rows, plain):
    blocks, depth, tile = weights.shape
    columns = blocks // 4
    piece = columns * tile
    rows = sum(p.shape[0] for p in parts) if by_rows else parts[0].shape[0]

    def weight_spec(gate):
        return pl.BlockSpec(
            (1, depth, tile),
            lambda half, column, place: (2 * (column + gate * columns) + (place[1] ^ half), 0, 0),
        )

    def placed(half, column, place):
        return (0, (place[1] ^ half) * columns + column)

    out_block = pl.BlockSpec((rows, tile), placed)
    whole = lambda item: pl.BlockSpec(item.shape, lambda half, column, place: (0,) * item.ndim)
    return pl.pallas_call(
        functools.partial(mix_kernel, parts=len(parts), by_rows=by_rows, plain=plain, tile=tile),
        grid_spec=pltpu.PrefetchScalarGridSpec(
            num_scalar_prefetch=1,
            grid=(2, columns),
            in_specs=[whole(p) for p in parts]
            + [weight_spec(0), weight_spec(1)]
            + [pl.BlockSpec((1, 2, tile), lambda half, column, place: (half, 0, column))],
            out_specs=[
                pl.BlockSpec((rows, depth), lambda half, column, place: (0, 0)),
                out_block,
                out_block,
                out_block,
            ],
        ),
        out_shape=[
            jax.ShapeDtypeStruct((rows, depth), jnp.bfloat16),
            jax.ShapeDtypeStruct((rows, 2 * piece), jnp.bfloat16),
            jax.ShapeDtypeStruct((rows, 2 * piece), jnp.float32),
            jax.ShapeDtypeStruct((rows, 2 * piece), jnp.float32),
        ],
        compiler_params=pltpu.CompilerParams(vmem_limit_bytes=60 * 2**20),
        cost_estimate=LIGHT,
        name="mix_forward",
    )(place, *parts, weights, weights, bias)


def mix_back_kernel(place_ref, grad_ref, a_ref, t_ref, *refs):
    mixed_ref, direct_ref, sums_ref = refs[-3:]
    grad = grad_ref[...]
    a = a_ref[...]
    piece = a.shape[1]
    skip = full(jnp.concatenate([ref[...] for ref in refs[:-3]], axis=1))
    opening = opening_of(t_ref[...])
    phi, bent = gelu_parts(a)
    slope = phi + a * (0.3989422804014327 * jnp.exp(-0.5 * a * a))
    grad_a = low((1.0 - opening) * slope * grad)
    grad_t = low((skip - bent) * opening * (1.0 - opening) * grad)
    mixed_ref[0, :, :piece] = grad_a
    mixed_ref[0, :, piece:] = grad_t
    direct_ref[...] = opening * grad
    sums_ref[0, :, :piece] = jnp.sum(full(grad_a), axis=0, keepdims=True)
    sums_ref[0, :, piece:] = jnp.sum(full(grad_t), axis=0, keepdims=True)


def mix_back(place, grad, a, t, joined, parts, plain, tile=LANES):
    rows, own = grad.shape
    piece = own // 2
    placed = pl.BlockSpec((rows, piece), lambda half, place: (0, place[1] ^ half))
    if plain:
        skips = [
            pl.BlockSpec((rows, tile), lambda half, place, z=z: (0, (z * 2 + (place[1] ^ half)) * parts + place[0]))
            for z in range(piece // tile)
        ]
    else:
        skips = [pl.BlockSpec((rows, piece), lambda half, place: (0, place[0] * 2 + (place[1] ^ half)))]
    return pl.pallas_call(
        mix_back_kernel,
        grid_spec=pltpu.PrefetchScalarGridSpec(
            num_scalar_prefetch=1,
            grid=(2,),
            in_specs=[placed, placed, placed] + skips,
            out_specs=[
                pl.BlockSpec((1, rows, own), lambda half, place: (half, 0, 0)),
                placed,
                pl.BlockSpec((1, 1, own), lambda half, place: (half, 0, 0)),
            ],
        ),
        out_shape=[
            jax.ShapeDtypeStruct((2, rows, own), jnp.bfloat16),
            jax.ShapeDtypeStruct((rows, own), jnp.float32),
            jax.ShapeDtypeStruct((2, 1, own), jnp.float32),
        ],
        compiler_params=pltpu.CompilerParams(vmem_limit_bytes=40 * 2**20),
        cost_estimate=LIGHT,
        name="mix_backward",
    )(place, grad, a, t, *[joined] * len(skips))


def inner_product(mixed_ref, weight_refs):
    blocks = len(weight_refs) // 2
    own = jnp.concatenate([ref[0] for ref in weight_refs[:blocks]], axis=1)
    other = jnp.concatenate([ref[0] for ref in weight_refs[blocks:]], axis=1)
    return dot_nt(mixed_ref[0], own) + dot_nt(mixed_ref[1], other)


def inner_specs(blocks, depth, tile, row_block):
    specs = []
    for flip in (0, 1):
        for z in range(blocks):
            specs.append(
                pl.BlockSpec(
                    (1, depth, tile),
                    lambda i, place, z=z, flip=flip: (2 * z + (place[1] ^ flip), row_block(i, place), 0),
                )
            )
    return specs


def inner_columns_kernel(place_ref, mixed_ref, *refs):
    out_ref = refs[-1]
    out_ref[0] = inner_product(mixed_ref, refs[:-1]).astype(out_ref.dtype)


def inner_columns(place, mixed, weights, odd, parts, dtype):
    _, rows, wide_columns = mixed.shape
    blocks, filters, tile = weights.shape
    blocks = blocks // 2
    depth = filters // parts
    return pl.pallas_call(
        inner_columns_kernel,
        grid_spec=pltpu.PrefetchScalarGridSpec(
            num_scalar_prefetch=1,
            grid=(parts // 2,),
            in_specs=[pl.BlockSpec(mixed.shape, lambda i, place: (0, 0, 0))]
            + inner_specs(blocks, depth, tile, lambda i, place: place[0] ^ (2 * i + odd)),
            out_specs=pl.BlockSpec((1, rows, depth), lambda i, place: (i, 0, 0)),
        ),
        out_shape=jax.ShapeDtypeStruct((parts // 2, rows, depth), dtype),
        compiler_params=pltpu.CompilerParams(vmem_limit_bytes=40 * 2**20),
        cost_estimate=LIGHT,
        name="inner_columns",
    )(place, mixed, *[weights] * (2 * blocks))


def inner_rows_kernel(place_ref, mixed_ref, *refs, parts, plain, tile):
    direct_ref, sent_ref, kept_ref, held_ref = refs[-4:]
    mine = place_ref[0]
    held_ref[...] = inner_product(mixed_ref, refs[:-4])

    step = pl.program_id(0)
    if plain:
        at = pl.ds(pl.multiple_of(mine * tile, tile), tile)
        column = (step % 2) * (pl.num_programs(0) // 2) + step // 2
        held_ref[:, at] += direct_ref[:, pl.ds(pl.multiple_of(column * tile, tile), tile)]
    else:

        @pl.when(step == mine)
        def _():
            held_ref[...] += direct_ref[...]

    extent = held_ref.shape[0] // parts
    for k in range(parts):
        got = held_ref[pl.ds(pl.multiple_of((mine ^ k) * extent, extent), extent), :]
        if k % 2:
            sent_ref[k // 2] = low(got)
        else:
            kept_ref[k // 2] = got


def inner_rows(place, mixed, weights, direct, parts, plain):
    _, rows, wide_columns = mixed.shape
    blocks, filters, tile = weights.shape
    blocks = blocks // 2
    depth = filters // parts
    extent = rows // parts
    out = pl.BlockSpec((parts // 2, extent, depth), lambda j, place: (0, 0, j))
    return pl.pallas_call(
        functools.partial(inner_rows_kernel, parts=parts, plain=plain, tile=tile),
        grid_spec=pltpu.PrefetchScalarGridSpec(
            num_scalar_prefetch=1,
            grid=(parts,),
            in_specs=[pl.BlockSpec(mixed.shape, lambda j, place: (0, 0, 0))]
            + inner_specs(blocks, depth, tile, lambda j, place: j)
            + [pl.BlockSpec(direct.shape, lambda j, place: (0, 0))],
            out_specs=[out, out],
            scratch_shapes=[pltpu.VMEM((rows, depth), jnp.float32)],
        ),
        out_shape=[
            jax.ShapeDtypeStruct((parts // 2, extent, filters), jnp.bfloat16),
            jax.ShapeDtypeStruct((parts // 2, extent, filters), jnp.float32),
        ],
        compiler_params=pltpu.CompilerParams(vmem_limit_bytes=40 * 2**20),
        cost_estimate=LIGHT,
        name="inner_rows",
    )(place, mixed, *[weights] * (2 * blocks), direct)


def widen_kernel(sums_ref, out_ref, *, parts):
    filters, tile = out_ref.shape[1:]
    outer = filters // (2 * parts * tile)
    for z in range(outer):
        for pair in range(2):
            for m in range(parts):
                at = ((z * 2 + pair) * parts + m) * tile
                source = filters + ((m * 2 + pair) * outer + z) * tile
                out_ref[0, at : at + tile, :] = sums_ref[:, at : at + tile].T
                out_ref[1, at : at + tile, :] = sums_ref[:, source : source + tile].T


def widen(sums, filters, parts):
    return pl.pallas_call(
        functools.partial(widen_kernel, parts=parts),
        out_shape=jax.ShapeDtypeStruct((2, filters, sums.shape[0]), jnp.float32),
        compiler_params=pltpu.CompilerParams(vmem_limit_bytes=16 * 2**20),
        cost_estimate=LIGHT,
        name="widen",
    )(sums)


def slope_of(values):
    phi = 0.5 * (1.0 + lax.erf(values * 0.7071067811865476))
    return phi + values * (0.3989422804014327 * jnp.exp(-0.5 * values * values))


def weight_copies(part_refs, up_ref, down_ref, bias_ref, sems):
    units = up_ref.shape[1]
    copies = []
    for k, part in enumerate(part_refs):
        last = part.shape[0] - 16
        copies.append(
            (
                pltpu.make_async_copy(part.at[pl.ds(0, units)], up_ref.at[k], sems.at[3 * k]),
                pltpu.make_async_copy(part.at[pl.ds(units, units)], down_ref.at[k], sems.at[3 * k + 1]),
                pltpu.make_async_copy(part.at[pl.ds(last, 16)], bias_ref.at[k], sems.at[3 * k + 2]),
            )
        )
    for part_copies in copies:
        for copy in part_copies:
            copy.start()
    return copies


def ffn_forward_kernel(x_ref, *refs, tile):
    part_refs, (out_ref, own_ref, up_ref, down_ref, bias_ref, sems) = refs[:-6], refs[-6:]
    copies = weight_copies(part_refs, up_ref, down_ref, bias_ref, sems)
    for k, part_copies in enumerate(copies):
        for copy in part_copies:
            copy.wait()
        for first in range(0, x_ref.shape[0], tile):
            at = slice(first, first + tile)
            value = jnp.dot(x_ref[at, :], up_ref[k], preferred_element_type=jnp.float32)
            active = low(gelu_parts(value + full(bias_ref[k, 0:1, :]))[1])
            added = jnp.dot(active, down_ref[k], preferred_element_type=jnp.float32)
            if k == 0:
                out_ref[at, :] = added
                own_ref[at, :] = active
            else:
                out_ref[at, :] += added


def ffn_call(kernel, operands, parts, units, outs, name):
    width = parts[0].shape[1]
    vmem = pl.BlockSpec(memory_space=pltpu.VMEM)
    return pl.pallas_call(
        kernel,
        in_specs=[vmem] * len(operands) + [pl.BlockSpec(memory_space=pl.ANY)] * len(parts),
        out_specs=[vmem] * len(outs),
        out_shape=outs,
        scratch_shapes=[
            pltpu.VMEM((len(parts), units, width), jnp.bfloat16),
            pltpu.VMEM((len(parts), units, width), jnp.bfloat16),
            pltpu.VMEM((len(parts), 16, width), jnp.bfloat16),
            pltpu.SemaphoreType.DMA((3 * len(parts),)),
        ],
        compiler_params=pltpu.CompilerParams(vmem_limit_bytes=40 * 2**20),
        cost_estimate=LIGHT,
        name=name,
    )(*operands, *parts)


def ffn_forward(x, parts, units, tile=256):
    rows, width = x.shape
    outs = [
        jax.ShapeDtypeStruct((rows, width), jnp.float32),
        jax.ShapeDtypeStruct((rows, units), jnp.bfloat16),
    ]
    kernel = functools.partial(ffn_forward_kernel, tile=tile)
    return ffn_call(kernel, [x], parts, units, outs, "ffn_forward")


def ffn_backward_kernel(x_ref, grad_ref, *refs, tile):
    part_refs, (out_ref, own_ref, sums_ref, up_ref, down_ref, bias_ref, sems) = refs[:-7], refs[-7:]
    copies = weight_copies(part_refs, up_ref, down_ref, bias_ref, sems)
    sums = jnp.zeros(sums_ref.shape, jnp.float32)
    for k, part_copies in enumerate(copies):
        for copy in part_copies:
            copy.wait()
        for first in range(0, x_ref.shape[0], tile):
            at = slice(first, first + tile)
            value = jnp.dot(x_ref[at, :], up_ref[k], preferred_element_type=jnp.float32)
            value = value + full(bias_ref[k, 0:1, :])
            inner = low(dot_nt(grad_ref[at, :], down_ref[k]) * slope_of(value))
            added = dot_nt(inner, up_ref[k])
            if k == 0:
                out_ref[at, :] = added
                own_ref[at, :] = inner
                sums = sums + jnp.sum(full(inner), axis=0, keepdims=True)
            else:
                out_ref[at, :] += added
    sums_ref[...] = sums


def ffn_backward(x, parts, units, grad, tile=256):
    rows, width = x.shape
    outs = [
        jax.ShapeDtypeStruct((rows, width), jnp.float32),
        jax.ShapeDtypeStruct((rows, units), jnp.bfloat16),
        jax.ShapeDtypeStruct((1, units), jnp.float32),
    ]
    kernel = functools.partial(ffn_backward_kernel, tile=tile)
    return ffn_call(kernel, [x, grad], parts, units, outs, "ffn_backward")


def masked_scores(query_heads, key_heads, keep_mask, score_scale):
    scores = (
        jnp.einsum("qhd,khd->hqk", query_heads, key_heads, preferred_element_type=jnp.float32)
        * score_scale
    )
    return jnp.where(keep_mask[None, None, :] == 1, scores, NEG_FILL)


def attend(query_heads, key_heads, value_heads, keep_mask, score_scale):
    scores = masked_scores(query_heads, key_heads, keep_mask, score_scale)
    row_peak = jnp.max(scores, axis=-1, keepdims=True)
    raised = jnp.exp(scores - row_peak)
    row_total = jnp.sum(raised, axis=-1, keepdims=True)
    attn_weights = (raised / row_total).astype(jnp.bfloat16)
    context = jnp.einsum(
        "hqk,khd->qhd", attn_weights, value_heads, preferred_element_type=jnp.float32
    )
    return (context.astype(jnp.bfloat16), row_peak, row_total)


def attend_back(
    query_heads, key_heads, value_heads, keep_mask, row_peak, row_total, grad_context, score_scale
):
    scores = masked_scores(query_heads, key_heads, keep_mask, score_scale)
    probs_full = jnp.exp(scores - row_peak) / row_total
    attn_weights = probs_full.astype(jnp.bfloat16)
    grad_value = jnp.einsum(
        "hqk,qhd->khd", attn_weights, grad_context, preferred_element_type=jnp.float32
    )
    grad_weights = jnp.einsum(
        "qhd,khd->hqk", grad_context, value_heads, preferred_element_type=jnp.float32
    )
    inner_sum = jnp.sum(grad_weights * probs_full, axis=-1, keepdims=True)
    grad_scores = (probs_full * (grad_weights - inner_sum)).astype(jnp.bfloat16)
    grad_query = (
        jnp.einsum("hqk,khd->qhd", grad_scores, key_heads, preferred_element_type=jnp.float32)
        * score_scale
    )
    grad_key = (
        jnp.einsum("hqk,qhd->khd", grad_scores, query_heads, preferred_element_type=jnp.float32)
        * score_scale
    )
    return (
        grad_query.astype(jnp.bfloat16),
        grad_key.astype(jnp.bfloat16),
        grad_value.astype(jnp.bfloat16),
    )


def per_device(
    char_ids,
    char_mask,
    position_ids,
    type_ids,
    key_mask,
    char_table,
    conv_weight,
    conv_bias,
    highway_weight,
    highway_bias,
    proj_weight,
    proj_bias,
    position_table,
    type_table,
    embed_gain,
    embed_shift,
    qkv_weight,
    qv_bias,
    out_weight,
    out_bias,
    ln1_gain,
    ln1_shift,
    up_weight,
    up_bias,
    down_weight,
    down_bias,
    ln2_gain,
    ln2_shift,
    cotangent,
):
    n_wide, n_narrow = lax.axis_size("wide"), lax.axis_size("narrow")
    half_wide = n_wide // 2
    me_narrow = lax.axis_index("narrow")
    wide_bits, narrow_bits = bits_of("wide"), bits_of("narrow")
    every_bit = narrow_bits + wide_bits
    falling = every_bit[::-1]
    word_total, letters = char_ids.shape
    tap_rows, own_filters = conv_weight.shape
    char_depth = char_table.shape[1]
    tap_count = tap_rows // char_depth
    filters = highway_weight.shape[1]
    own_mix = highway_weight.shape[2]
    own_width = proj_weight.shape[1]
    seq_length = position_table.shape[0]
    group = word_total * n_narrow
    own_hidden = half_wide * own_mix

    outer = n_wide // 2
    quarter = outer // 2
    outer_groups = [[2 * z + y for z in range(outer)] for y in range(2)]
    me_pair = my_bit("wide", 0)

    def grouped(item):
        split = item.reshape((quarter, 2, n_narrow, own_mix) + item.shape[1:])
        return split.transpose((2, 1, 0, 3) + tuple(range(4, split.ndim))).reshape(item.shape)

    def ungrouped(item):
        split = item.reshape((n_narrow, 2, quarter, own_mix) + item.shape[1:])
        return split.transpose((2, 1, 0, 3) + tuple(range(4, split.ndim))).reshape(item.shape)

    tiled = own_mix == LANES
    corner = jnp.stack([me_narrow, me_pair]).astype(jnp.int32)

    def gather_mix(shard):
        blocks = lax.all_gather(shard, "wide", axis=0)
        if tiled:
            return blocks
        blocks = blocks.reshape(-1, LANES // own_mix, 2, filters, own_mix).transpose(0, 2, 3, 1, 4)
        return blocks.reshape(-1, filters, LANES)

    plain = tiled and half_wide == n_narrow
    ordered, unordered = (lambda item: item, lambda item: item) if plain else (grouped, ungrouped)
    mix_weights = [gather_mix(ordered(highway_weight[0]))]
    mix_weights.append(gather_mix(after(grouped(highway_weight[1]), mix_weights[0])))
    conv_block = jnp.zeros((own_filters, LANES), jnp.bfloat16)
    conv_block = conv_block.at[:, :tap_rows].set(conv_weight.T)
    conv_block = conv_block.at[:, tap_rows + tap_count].set(conv_bias)
    bias_block = jnp.pad(highway_bias, ((0, 0), (0, LANES - own_mix)))
    conv_spread = spread(jnp.concatenate([conv_block, bias_block]), falling)
    filt_rows = ordered(conv_spread[:, :own_filters].reshape(filters, LANES))
    mix_bias = conv_spread[:, own_filters:, :own_mix].reshape(outer, 2, n_narrow, 2, own_mix)
    mix_bias = full(lax.dynamic_index_in_dim(mix_bias, me_narrow, 2, keepdims=False))
    mix_bias = [lax.dynamic_index_in_dim(mix_bias, me_pair ^ half, 1, keepdims=False) for half in range(2)]
    mix_bias = jnp.stack(mix_bias).transpose(2, 0, 1, 3).reshape(2, 2, 2, quarter * own_mix)
    vector_block = jnp.stack([proj_bias, type_table[0], type_table[1], embed_gain, embed_shift], axis=1)
    vector_block = jnp.pad(vector_block, ((0, 0), (0, LANES - vector_block.shape[1])))
    rest = jnp.concatenate([grouped(proj_weight).T, position_table.T, vector_block], axis=1)[None]
    rest_bits = wide_bits[::-1]
    rest = doubled(rest, *rest_bits[0], 1).reshape((-1,) + rest.shape[1:])
    widths = ordered(filter_widths(filters))
    lane = jnp.arange(LANES)
    tap_keep = (lane[None, :] // char_depth) < widths[:, None]
    late = lane - tap_rows
    shut = (late == 0)[None, :] | (
        (late >= 1)[None, :] & (late < tap_count)[None, :] & (widths[:, None] > late[None, :])
    )
    is_bias = (late == tap_count)[None, :]
    filt_rows = jnp.where(
        (tap_keep & (late < 0)[None, :]) | is_bias,
        filt_rows,
        jnp.where(shut, jnp.bfloat16(SHUT), jnp.bfloat16(0.0)),
    )
    vocab = char_table.shape[0]
    vocab_rows = -(-vocab // 16) * 16
    id_row = char_ids.T.reshape(1, letters * word_total)
    hot = (jnp.arange(vocab_rows)[:, None] == id_row).astype(jnp.bfloat16)
    table_t = jnp.pad(char_table, ((0, vocab_rows - vocab), (0, 0))).T
    embedded = low(jnp.dot(table_t, hot, preferred_element_type=jnp.float32))
    embedded = jnp.pad(embedded, ((0, 0), (0, tap_count * word_total)))
    span = letters * word_total
    tap_blocks = [embedded[:, t * word_total : t * word_total + span] for t in range(tap_count)]
    place = jnp.arange(letters)
    usable = (char_mask == 1) | (place[None, :] == 0)
    unusable_row = low(~usable).T.reshape(1, span)
    late_rows = low(place[None, :] == letters - jnp.arange(1, tap_count)[:, None])
    late_rows = jnp.repeat(late_rows, word_total, axis=1)
    columns_t = jnp.concatenate(
        tap_blocks
        + [
            unusable_row,
            late_rows,
            jnp.ones((1, span), jnp.bfloat16),
            jnp.zeros((LANES - tap_rows - tap_count - 1, span), jnp.bfloat16),
        ]
    )
    columns = columns_t.T.reshape(letters, word_total, LANES)
    tally = jnp.stack(
        [jnp.sum(full(usable[:, : letters - w + 1]), axis=1) for w in range(1, tap_count + 1)], axis=1
    )
    width_hot = full(jnp.arange(1, tap_count + 1)[:, None] == widths[None, :])
    valid_count = jnp.dot(tally, width_hot)

    def rest_step(rest, which):
        return doubled(rest, *which, 1).reshape((-1,) + rest.shape[1:])

    rest = after(rest, conv_spread)
    for which in rest_bits[1:-1]:
        rest = rest_step(rest, which)
    units = up_weight.shape[1]
    encoder_pack = jnp.concatenate(
        [up_weight, down_weight, out_weight, jnp.broadcast_to(up_bias[None], (16, units))]
    )
    encoder_parts = [encoder_pack, swap(encoder_pack, "narrow", 1)]
    filt_rows, encoder_parts = lax.optimization_barrier((filt_rows, encoder_parts))
    lse = pool_forward(columns, filt_rows)
    rest = rest_step(after(rest, lse), rest_bits[-1])
    pooled = lse - jnp.log(valid_count)
    features = low(smooth_gelu(pooled))

    parts = near_parts(features, "narrow")
    near_order = [0, 2, 1, 3]
    cotangent_rows = lax.all_gather(
        after(cotangent, mix_weights[1]), "narrow", axis=0, tiled=True
    )
    rest = after(rest, parts[-1])

    def narrowed(rest, bit):
        width = own_hidden << bit
        mine = my_bit("narrow", bit)
        tail = rest[..., 2 * width :]
        kept = lax.dynamic_slice_in_dim(rest, mine * width, width, rest.ndim - 1)
        sent = lax.dynamic_slice_in_dim(rest, (1 - mine) * width, width, rest.ndim - 1)
        kept, sent = (jnp.concatenate([item, tail], axis=-1) for item in (kept, sent))
        got = swap(sent, "narrow", bit)
        high = mine == 1
        pair = jnp.stack([jnp.where(high, got, kept), jnp.where(high, kept, got)], axis=1)
        return pair.reshape((-1,) + pair.shape[2:])

    rest = narrowed(rest, 1)
    highway_saved, pair_parts = [], [swap(features, "wide", 0)]
    for layer_index in range(2):
        joined, hidden, kept_a, kept_t = mix_forward(
            corner, parts, mix_weights[layer_index], mix_bias[layer_index], layer_index == 0, plain and layer_index == 0
        )
        highway_saved.append((joined, kept_a, kept_t))
        if layer_index == 0:
            parts = near_parts(hidden, "narrow")
            pair_parts.append(swap(hidden, "wide", 0))
            rest = narrowed(after(rest, hidden), 0)
            encoder_parts = encoder_parts + [
                swap(item, "narrow", 0) for item in after(encoder_parts, hidden)
            ]
            parts, encoder_parts, rest = lax.optimization_barrier((parts, encoder_parts, rest))
    proj_input = hidden
    rest = rest.reshape(n_wide * n_narrow * own_width, -1)
    model_width = rest.shape[0]
    proj_own = rest[:, :own_hidden]
    position_rows = rest[:, own_hidden : own_hidden + seq_length]
    vectors = full(rest[:, own_hidden + seq_length :].T)
    proj_shift, type_low, type_high, first_gain, first_shift = (vectors[i] for i in range(5))
    projected = fold(dot_nt(proj_input, proj_own).reshape(n_narrow, word_total, model_width), narrow_bits)
    projected, cotangent_rows = lax.optimization_barrier((projected, cotangent_rows))
    position_hot = (position_ids[:, None] == jnp.arange(seq_length)[None, :]).astype(jnp.bfloat16)
    type_rows = jnp.where(type_ids[:, None] == 1, type_high, type_low)
    summed = projected + proj_shift + dot_nt(position_hot, position_rows) + type_rows
    first_state, first_pull = jax.vjp(layer_norm, summed, first_gain, first_shift)

    gathered = lax.all_gather(low(first_state), "narrow", axis=0, tiled=True)
    group_rows = gathered.shape[0]
    qkv_out = jnp.einsum("gd,kdc->kgc", gathered, qkv_weight, preferred_element_type=jnp.float32)
    local_width = qkv_out.shape[2]
    head_count = local_width // HEAD_DIM
    seq_shape = (group_rows, head_count, HEAD_DIM)
    query_heads = low(qkv_out[0] + full(qv_bias[0])).reshape(seq_shape)
    key_heads = low(qkv_out[1]).reshape(seq_shape)
    value_heads = low(qkv_out[2] + full(qv_bias[1])).reshape(seq_shape)
    score_scale = HEAD_DIM ** (-0.5)
    keep_mask = key_mask[0]
    context, row_peak, row_total = attend(query_heads, key_heads, value_heads, keep_mask, score_scale)
    context_rows = context.reshape(group_rows, local_width)

    def by_owner(partial):
        return fold(partial.reshape(n_narrow, word_total, model_width), narrow_bits)

    def own_words(rows):
        return lax.dynamic_slice_in_dim(rows, me_narrow * word_total, word_total, 0)

    attn_branch = full(out_bias)
    for k, part in zip(near_order, near_parts(context_rows, "narrow")):
        weight = encoder_parts[k][2 * units : 2 * units + local_width]
        attn_branch = attn_branch + jnp.dot(part, weight, preferred_element_type=jnp.float32)
    second_state, second_pull = jax.vjp(
        layer_norm, full(gathered) + attn_branch, full(ln1_gain), full(ln1_shift)
    )
    pair_parts, ffn_input = lax.optimization_barrier((pair_parts, low(second_state)))
    ffn_branch, activated = ffn_forward(ffn_input, encoder_parts, units)
    layer_out, third_pull = jax.vjp(
        layer_norm, second_state + (ffn_branch + full(down_bias)), full(ln2_gain), full(ln2_shift)
    )
    layer_out = own_words(layer_out)

    def pair_start(halves):
        kept = lax.dynamic_index_in_dim(halves, me_pair, 0, keepdims=False)
        sent = lax.dynamic_index_in_dim(halves, 1 - me_pair, 0, keepdims=False)
        return kept, swap(sent, "wide", 0)

    def pair_end(mine, back):
        first = me_pair == 0
        return jnp.stack([full(jnp.where(first, mine, back)), full(jnp.where(first, back, mine))])

    grad_third, grad_ln2_gain, grad_ln2_shift = third_pull(cotangent_rows)
    grad_ffn = low(grad_third)
    grad_down_bias = jnp.sum(full(grad_ffn), axis=0)
    grad_down_weight = jnp.einsum("gf,gd->fd", activated, grad_ffn, preferred_element_type=jnp.float32)
    grad_inner, grad_up, grad_up_bias = ffn_backward(ffn_input, encoder_parts, units, grad_ffn)
    grad_up_weight = jnp.einsum("gd,gf->df", ffn_input, grad_up, preferred_element_type=jnp.float32)
    grad_second = grad_third + grad_inner
    ffn_kept, ffn_received = pair_start(jnp.stack([low(grad_up_weight), low(grad_down_weight)]))
    grad_first_branch, grad_ln1_gain, grad_ln1_shift = second_pull(grad_second)
    pair_parts = [near_parts(after(item, ffn_branch), "narrow") for item in pair_parts]
    pair_parts, grad_attn = lax.optimization_barrier((pair_parts, low(grad_first_branch)))
    pair_joined = [
        in_order(item, "narrow", layer_index) for layer_index, item in enumerate(pair_parts)
    ]
    grad_out_bias = jnp.sum(full(grad_attn), axis=0)
    grad_attn_rows = grad_attn
    grad_out_weight = jnp.einsum(
        "gc,gd->cd", context_rows, grad_attn_rows, preferred_element_type=jnp.float32
    )
    grad_context = low(dot_nt(grad_attn_rows, out_weight)).reshape(seq_shape)
    grad_query, grad_key, grad_value = attend_back(
        query_heads, key_heads, value_heads, keep_mask, row_peak, row_total, grad_context, score_scale
    )
    grad_joined = jnp.stack(
        [item.reshape(group_rows, local_width) for item in (grad_query, grad_key, grad_value)]
    )
    grad_qv_bias = jnp.stack(
        [jnp.sum(full(grad_joined[0]), axis=0), jnp.sum(full(grad_joined[2]), axis=0)]
    )
    grad_qkv_weight = jnp.einsum(
        "kgc,gd->kcd", grad_joined, gathered, preferred_element_type=jnp.float32
    )
    attn_kept, attn_received = pair_start(
        jnp.concatenate([low(grad_qkv_weight), low(grad_out_weight)[None]]).reshape(2, -1, model_width)
    )
    grad_first = own_words(grad_first_branch) + by_owner(
        jnp.einsum("kgc,kdc->gd", grad_joined, qkv_weight, preferred_element_type=jnp.float32)
    )
    grad_summed, grad_embed_gain, grad_embed_shift = first_pull(grad_first)

    grad_proj_low = low(grad_summed)
    grad_position = jnp.einsum(
        "td,tl->dl", grad_proj_low, position_hot, preferred_element_type=jnp.float32
    )
    is_high = type_ids[:, None] == 1
    vector_grads = jnp.stack(
        [
            jnp.sum(full(grad_proj_low), axis=0),
            jnp.sum(jnp.where(is_high, 0.0, grad_summed), axis=0),
            jnp.sum(jnp.where(is_high, grad_summed, 0.0), axis=0),
            grad_embed_gain,
            grad_embed_shift,
        ],
        axis=1,
    )
    vector_grads = jnp.pad(low(vector_grads), ((0, 0), (0, LANES - vector_grads.shape[1])))
    grad_proj_rows = lax.all_gather(grad_proj_low, "narrow", axis=0, tiled=True)
    grad_proj_weight = jnp.einsum(
        "gd,gh->dh", grad_proj_rows, proj_input, preferred_element_type=jnp.float32
    )
    table_grads = [
        item.reshape(n_wide, n_narrow, own_width, -1).transpose(1, 0, 2, 3)
        for item in (low(grad_position), vector_grads, low(grad_proj_weight))
    ]
    table_grads = jnp.concatenate(table_grads, axis=3)
    table_grads = lax.all_to_all(table_grads, "narrow", 0, 0, tiled=True)
    table_width = seq_length + LANES
    table_sums = jnp.sum(full(table_grads[..., :table_width]), axis=0)
    proj_parts = table_grads[..., table_width:].transpose(1, 0, 2, 3)
    rest_grads = [item.reshape(n_wide, LANES, -1) for item in (low(table_sums), proj_parts)]
    table_columns = rest_grads[0].shape[2]
    rest_grads = jnp.concatenate(rest_grads, axis=2)
    grad_hidden = jnp.dot(grad_proj_rows, proj_own, preferred_element_type=jnp.float32)

    mix_bias_grads = [None, None]

    def weight_part(joined, mixed):
        return jnp.einsum(
            "tk,tzc->zck",
            joined,
            mixed.reshape(group, outer, own_mix),
            preferred_element_type=jnp.float32,
        )

    def pair_weight(layer_index, mixed, met):
        joined = highway_saved[layer_index][0]
        return low(weight_part(joined, mixed[0]) + weight_part(pair_joined[layer_index], met))

    ffn_received, attn_received = after((ffn_received, attn_received), grad_hidden)
    pair_sums = lax.psum(
        (low(full(ffn_kept) + full(ffn_received)), low(full(attn_kept) + full(attn_received))),
        "wide",
        axis_index_groups=outer_groups,
    )
    joined, kept_a, kept_t = highway_saved[1]
    mixed, direct, mix_bias_grads[1] = mix_back(corner, grad_hidden, kept_a, kept_t, joined, n_narrow, False)
    met = swap(mixed[1], "wide", 0)
    sent = inner_columns(corner, mixed, mix_weights[1], 1, n_narrow, jnp.bfloat16)
    kept = inner_columns(corner, mixed, mix_weights[1], 0, n_narrow, jnp.float32)
    grad_hidden = direct + fold_near(sent, kept, "narrow")
    weight_second = pair_weight(1, mixed, after(met, grad_hidden))
    joined, kept_a, kept_t = highway_saved[0]
    mixed, direct, mix_bias_grads[0] = mix_back(corner, grad_hidden, kept_a, kept_t, joined, n_narrow, plain)
    met = swap(mixed[1], "wide", 0)
    sent, kept = inner_rows(corner, mixed, mix_weights[0], direct, n_narrow, plain)
    grad_features = fold_near(sent, kept, "narrow")

    rest_grads = low(halved(after(rest_grads, direct), *wide_bits[0]))
    weight_first = pair_weight(0, mixed, met)
    both = [item.reshape(outer, LANES, -1) for item in (weight_first, weight_second)]
    weight_columns = both[0].shape[2]
    both = jnp.concatenate(both + [rest_grads], axis=2)
    grad_features, both, pair_sums = lax.optimization_barrier((grad_features, both, pair_sums))

    grad_pooled = jax.vjp(smooth_gelu, pooled)[1](grad_features)[0]
    filt_grads, hot_grads = pool_backward(
        columns, columns_t, hot, filt_rows, lse, grad_pooled, char_depth, tap_count
    )
    both = lax.psum_scatter(both, "wide", scatter_dimension=0, axis_index_groups=outer_groups)
    both = full(both)
    if plain:
        owned_highway = widen(both, filters, n_narrow)
    else:
        owned_highway = [
            both[:, at * weight_columns : (at + 1) * weight_columns].reshape(own_mix, filters).T
            for at in range(2)
        ]
        owned_highway = jnp.stack([unordered(owned_highway[0]), ungrouped(owned_highway[1])])
    owned_rest = both[:, 2 * weight_columns :]
    table_grads = owned_rest[:, :table_columns].reshape(own_width, table_width)
    owned_proj = owned_rest[:, table_columns:].reshape(n_narrow, own_width, own_hidden).transpose(0, 2, 1)
    owned_proj = ungrouped(owned_proj.reshape(filters, own_width))
    filt_grads = unordered(low(jnp.where(tap_keep | is_bias, filt_grads, 0.0)))
    grad_table = hot_grads[:vocab, :tap_rows].reshape(vocab, tap_count, char_depth).sum(axis=1)
    mix_bias_grads = jnp.stack(mix_bias_grads).reshape(2, 2, outer, own_mix)
    swapped = jnp.stack([jnp.where(me_pair == 0, mix_bias_grads[:, y], mix_bias_grads[:, 1 - y]) for y in range(2)], axis=2)
    mix_bias_grads = swapped.reshape(2, n_wide, own_mix)
    wide_parts = [
        mix_bias_grads,
        grad_up_bias[0],
        grad_qv_bias,
        grad_out_bias,
        grad_ln1_gain,
        grad_ln1_shift,
        grad_down_bias,
        grad_ln2_gain,
        grad_ln2_shift,
    ]
    all_parts = [grad_table]

    def joined_rows(parts):
        flat = jnp.concatenate([item.reshape(-1) for item in parts])
        return jnp.pad(flat, (0, -flat.shape[0] % LANES)).reshape(-1, LANES)

    def parted(flat, parts):
        flat, done, start = flat.reshape(-1), [], 0
        for item in parts:
            done.append(flat[start : start + item.size].reshape(item.shape))
            start += item.size
        return done

    wide_flat, all_flat = joined_rows(wide_parts), joined_rows(all_parts)
    flat = total(jnp.concatenate([wide_flat, all_flat]), wide_bits[:1])
    filt_grads = halved(filt_grads.reshape(n_wide, -1, LANES), *wide_bits[0])
    flat, filt_grads = lax.optimization_barrier((flat, filt_grads))
    filt_grads = fold(filt_grads, wide_bits[1:])
    owned_filt = lax.all_to_all(
        low(filt_grads).reshape(n_narrow, own_filters, LANES), "narrow", 0, 0, tiled=True
    )
    owned_filt = jnp.sum(full(owned_filt), axis=0)
    owned_conv = owned_filt[:, :tap_rows].T
    owned_conv_bias = owned_filt[:, tap_rows + tap_count]

    flat, pair_backs = lax.optimization_barrier(
        (total(flat, wide_bits[1:]), [swap(item, "wide", 0) for item in pair_sums])
    )
    (
        mix_sums,
        sum_up_bias,
        sum_qv_bias,
        sum_out_bias,
        sum_ln1_gain,
        sum_ln1_shift,
        sum_down_bias,
        sum_ln2_gain,
        sum_ln2_shift,
    ) = parted(flat[: wide_flat.shape[0]], wide_parts)
    owned_mix_bias = lax.dynamic_index_in_dim(mix_sums, lax.axis_index("wide"), 1, keepdims=False)
    sum_table = parted(total(flat[wide_flat.shape[0] :], narrow_bits), all_parts)[0]
    ffn_sums, attn_sums = (pair_end(mine, back) for mine, back in zip(pair_sums, pair_backs))
    attn_sums = attn_sums.reshape(n_narrow, local_width, model_width)
    owned_vectors = table_grads[:, seq_length : seq_length + 5].T
    return (
        layer_out,
        sum_table,
        owned_conv,
        owned_conv_bias,
        owned_highway,
        owned_mix_bias,
        owned_proj,
        owned_vectors[0],
        table_grads[:, :seq_length].T,
        owned_vectors[1:3],
        owned_vectors[3],
        owned_vectors[4],
        attn_sums[:3].transpose(0, 2, 1),
        sum_qv_bias,
        attn_sums[3],
        sum_out_bias,
        sum_ln1_gain,
        sum_ln1_shift,
        ffn_sums[0],
        sum_up_bias,
        ffn_sums[1],
        sum_down_bias,
        sum_ln2_gain,
        sum_ln2_shift,
    )


def solution(mesh):
    return jax.shard_map(
        per_device,
        mesh=mesh,
        in_specs=(
            P(("wide", "narrow"), None),
            P(("wide", "narrow"), None),
            P(("wide", "narrow")),
            P(("wide", "narrow")),
            P("wide", None),
            P(),
            P(None, ("wide", "narrow")),
            P(("wide", "narrow")),
            P(None, None, ("wide", "narrow")),
            P(None, ("wide", "narrow")),
            P(None, ("wide", "narrow")),
            P(("wide", "narrow")),
            P(None, ("wide", "narrow")),
            P(None, ("wide", "narrow")),
            P(("wide", "narrow")),
            P(("wide", "narrow")),
            P(None, None, "narrow"),
            P(None, "narrow"),
            P("narrow", None),
            P(),
            P(),
            P(),
            P(None, "narrow"),
            P("narrow"),
            P("narrow", None),
            P(),
            P(),
            P(),
            P(("wide", "narrow"), None),
        ),
        out_specs=(
            P(("wide", "narrow"), None),
            P(),
            P(None, ("wide", "narrow")),
            P(("wide", "narrow")),
            P(None, None, ("wide", "narrow")),
            P(None, ("wide", "narrow")),
            P(None, ("wide", "narrow")),
            P(("wide", "narrow")),
            P(None, ("wide", "narrow")),
            P(None, ("wide", "narrow")),
            P(("wide", "narrow")),
            P(("wide", "narrow")),
            P(None, None, "narrow"),
            P(None, "narrow"),
            P("narrow", None),
            P(),
            P(),
            P(),
            P(None, "narrow"),
            P("narrow"),
            P("narrow", None),
            P(),
            P(),
            P(),
        ),
        check_vma=False,
    )
```

```python
import functools

import jax
import jax.numpy as jnp
from jax import lax
from jax.experimental import pallas as pl
from jax.experimental.pallas import tpu as pltpu
from jax.sharding import PartitionSpec as P

HEAD_DIM = 64
EPSILON = 1e-05
NEG_FILL = -1000000000.0
SHUT = -1e30
LANES = 128
LIGHT = pl.CostEstimate(flops=1000, bytes_accessed=1000, transcendentals=0)


def layer_norm(values, gain, shift):
    centre = values - jnp.mean(values, axis=-1, keepdims=True)
    spread = jnp.mean(centre * centre, axis=-1, keepdims=True)
    return centre * lax.rsqrt(spread + EPSILON) * gain + shift


def smooth_gelu(values):
    return jax.nn.gelu(values, approximate=False)


def low(values):
    return values.astype(jnp.bfloat16)


def full(values):
    return values.astype(jnp.float32)


def filter_widths(filter_total):
    index = jnp.arange(filter_total)
    widths = jnp.ones((filter_total,), jnp.int32)
    for level in range(6):
        widths = widths + (index >= filter_total * 2**level // 64).astype(jnp.int32)
    return widths


def swap(block, axis, bit):
    size = lax.axis_size(axis)
    return lax.ppermute(block, axis, [(i, i ^ (1 << bit)) for i in range(size)])


def after(value, *others):
    return lax.optimization_barrier((value,) + others)[0]


def my_bit(axis, bit):
    return (lax.axis_index(axis) >> bit) & 1


def bits_of(axis):
    return [(axis, bit) for bit in range(lax.axis_size(axis).bit_length() - 1)]


def spread(block, bits):
    shape = block.shape
    held = block[None]
    for axis, bit in bits:
        other = swap(held, axis, bit)
        high = my_bit(axis, bit) == 1
        held = jnp.stack([jnp.where(high, other, held), jnp.where(high, held, other)], axis=1)
        held = held.reshape((-1,) + shape)
    return held


def doubled(block, axis, bit, depth):
    other = swap(block, axis, bit)
    high = my_bit(axis, bit) == 1
    return jnp.stack([jnp.where(high, other, block), jnp.where(high, block, other)], axis=depth)


def halved(parts, axis, bit):
    pairs = parts.reshape((-1, 2) + parts.shape[1:])
    mine = my_bit(axis, bit)
    kept = lax.dynamic_index_in_dim(pairs, mine, 1, keepdims=False)
    sent = low(lax.dynamic_index_in_dim(pairs, 1 - mine, 1, keepdims=False))
    return full(kept) + full(swap(sent, axis, bit))


def fold(parts, bits):
    for axis, bit in bits:
        parts = halved(parts, axis, bit)
    return parts[0]


def near_parts(block, axis):
    parts = [block]
    for bit in reversed(range(lax.axis_size(axis).bit_length() - 1)):
        parts = [item for part in parts for item in (part, swap(part, axis, bit))]
    return parts


def in_order(parts, axis, dim):
    mine = lax.axis_index(axis)
    blocks = []
    for m in range(len(parts)):
        held, count = parts, len(parts)
        for bit in range(count.bit_length() - 1):
            here = ((mine >> bit) & 1) == ((m >> bit) & 1)
            held = [jnp.where(here, even, odd) for even, odd in zip(held[::2], held[1::2])]
        blocks.append(held[0])
    return jnp.concatenate(blocks, axis=dim)


def fold_near(sent, kept, axis):
    whole = full(kept) + full(swap(sent, axis, 0))
    for bit in range(1, lax.axis_size(axis).bit_length() - 1):
        pairs = whole.reshape((-1, 2) + whole.shape[1:])
        whole = pairs[:, 0] + full(swap(low(pairs[:, 1]), axis, bit))
    return whole[0]


def total(value, bits):
    for axis, bit in bits:
        value = value + swap(value, axis, bit)
    return value


def dot_nt(left, right):
    return lax.dot_general(left, right, (((1,), (1,)), ((), ())), preferred_element_type=jnp.float32)


def pool_kernel(cols_ref, filt_ref, lse_ref, *, group):
    letters = cols_ref.shape[0]
    filt = filt_ref[...]
    peak = None
    for first in range(0, letters, group):
        scores = [dot_nt(cols_ref[p], filt) for p in range(first, min(first + group, letters))]
        top = functools.reduce(jnp.maximum, scores)
        if peak is None:
            peak = top
            mass = functools.reduce(jnp.add, [jnp.exp(s - peak) for s in scores])
        else:
            later = jnp.maximum(peak, top)
            fresh = functools.reduce(jnp.add, [jnp.exp(s - later) for s in scores])
            mass = mass * jnp.exp(peak - later) + fresh
            peak = later
    lse_ref[...] = peak + jnp.log(mass)


def pool_forward(columns, filt_rows, block=256):
    letters, words, depth = columns.shape
    filters = filt_rows.shape[0]
    return pl.pallas_call(
        functools.partial(pool_kernel, group=5),
        grid=(filters // block,),
        in_specs=[
            pl.BlockSpec(columns.shape, lambda i: (0, 0, 0)),
            pl.BlockSpec((block, depth), lambda i: (i, 0)),
        ],
        out_specs=pl.BlockSpec((words, block), lambda i: (0, i)),
        out_shape=jax.ShapeDtypeStruct((words, filters), jnp.float32),
        compiler_params=pltpu.CompilerParams(vmem_limit_bytes=48 * 2**20),
        cost_estimate=LIGHT,
        name="pool_forward",
    )(columns, filt_rows)


def back_kernel(
    cols_ref, cols_t_ref, hot_ref, filt_ref, lse_ref, grad_ref, dw_ref, table_ref, gcol_ref, *, depth, taps
):
    letters, words, lanes = cols_ref.shape
    step = pl.program_id(0)
    filt = filt_ref[...]
    lse = lse_ref[...]
    grad = grad_ref[...]

    @pl.when(step == 0)
    def _():
        gcol_ref[...] = jnp.zeros_like(gcol_ref)

    half = letters // 2
    weight_sum = jnp.zeros((lanes, filt.shape[0]), jnp.float32)
    for first, last in ((0, half), (half, letters)):
        slots = jnp.concatenate(
            [low(grad * jnp.exp(dot_nt(cols_ref[p], filt) - lse)) for p in range(first, last)], axis=0
        )
        at = slice(first * words, last * words)
        gcol_ref[at, :] += jnp.dot(slots, filt, preferred_element_type=jnp.float32)
        weight_sum += jnp.dot(cols_t_ref[:, at], slots, preferred_element_type=jnp.float32)
    dw_ref[...] = weight_sum.T

    @pl.when(step == pl.num_programs(0) - 1)
    def _():
        tap = lax.broadcasted_iota(jnp.int32, (words, lanes), 1) // depth
        table_ref[...] = jnp.zeros_like(table_ref)
        for c in range(letters):
            moved = jnp.where(tap == 0, gcol_ref[c * words : (c + 1) * words, :], 0.0)
            for t in range(1, min(taps, c + 1)):
                moved = jnp.where(tap == t, gcol_ref[(c - t) * words : (c - t + 1) * words, :], moved)
            table_ref[...] += jnp.dot(
                hot_ref[:, c * words : (c + 1) * words], low(moved), preferred_element_type=jnp.float32
            )


def pool_backward(columns, columns_t, hot, filt_rows, lse, grad, depth, taps, block=256):
    letters, words, lanes = columns.shape
    filters = filt_rows.shape[0]
    whole = lambda item: pl.BlockSpec(item.shape, lambda i: (0,) * item.ndim)
    return pl.pallas_call(
        functools.partial(back_kernel, depth=depth, taps=taps),
        grid=(filters // block,),
        in_specs=[
            whole(columns),
            whole(columns_t),
            whole(hot),
            pl.BlockSpec((block, lanes), lambda i: (i, 0)),
            pl.BlockSpec((words, block), lambda i: (0, i)),
            pl.BlockSpec((words, block), lambda i: (0, i)),
        ],
        out_specs=[
            pl.BlockSpec((block, lanes), lambda i: (i, 0)),
            pl.BlockSpec((hot.shape[0], lanes), lambda i: (0, 0)),
        ],
        out_shape=[
            jax.ShapeDtypeStruct((filters, lanes), jnp.float32),
            jax.ShapeDtypeStruct((hot.shape[0], lanes), jnp.float32),
        ],
        scratch_shapes=[pltpu.VMEM((letters * words, lanes), jnp.float32)],
        compiler_params=pltpu.CompilerParams(vmem_limit_bytes=48 * 2**20),
        cost_estimate=LIGHT,
        name="pool_backward",
    )(columns, columns_t, hot, filt_rows, lse, grad)


def gelu_parts(values):
    spread_part = 0.5 * (1.0 + lax.erf(values * 0.7071067811865476))
    return spread_part, values * spread_part


def opening_of(values):
    return 1.0 / (1.0 + jnp.exp(-values))


def mix_kernel(place_ref, *refs, parts, by_rows, plain, tile):
    part_refs = refs[:parts]
    weight_a, weight_t, bias_ref, joined_ref, hidden_ref, a_ref, t_ref = refs[parts:]
    half, column = pl.program_id(0), pl.program_id(1)
    mine, pair = place_ref[0], place_ref[1]

    @pl.when((half == 0) & (column == 0))
    def _():
        for k, part in enumerate(part_refs):
            extent = part.shape[0 if by_rows else 1]
            at = pl.ds(pl.multiple_of((mine ^ k) * extent, extent), extent)
            if by_rows:
                joined_ref[at, :] = part[...]
            else:
                joined_ref[:, at] = part[...]

    columns = pl.num_programs(1)
    if plain:
        first = ((column * 2 + (pair ^ half)) * parts + mine) * tile
    else:
        first = ((mine * 2 + (pair ^ half)) * columns + column) * tile

    weight = jnp.concatenate([weight_a[0], weight_t[0]], axis=1)
    mixture = jnp.dot(joined_ref[...], weight, preferred_element_type=jnp.float32)
    a = mixture[:, :tile] + bias_ref[0, 0:1, :]
    t = mixture[:, tile:] + bias_ref[0, 1:2, :]
    skip = full(joined_ref[:, pl.ds(pl.multiple_of(first, tile), tile)])
    opening = opening_of(t)
    hidden_ref[...] = low(opening * skip + (1.0 - opening) * gelu_parts(a)[1])
    a_ref[...] = a
    t_ref[...] = t


def mix_forward(place, parts, weights, bias, by_rows, plain):
    blocks, depth, tile = weights.shape
    columns = blocks // 4
    piece = columns * tile
    rows = sum(p.shape[0] for p in parts) if by_rows else parts[0].shape[0]

    def weight_spec(gate):
        return pl.BlockSpec(
            (1, depth, tile),
            lambda half, column, place: (2 * (column + gate * columns) + (place[1] ^ half), 0, 0),
        )

    def placed(half, column, place):
        return (0, (place[1] ^ half) * columns + column)

    out_block = pl.BlockSpec((rows, tile), placed)
    whole = lambda item: pl.BlockSpec(item.shape, lambda half, column, place: (0,) * item.ndim)
    return pl.pallas_call(
        functools.partial(mix_kernel, parts=len(parts), by_rows=by_rows, plain=plain, tile=tile),
        grid_spec=pltpu.PrefetchScalarGridSpec(
            num_scalar_prefetch=1,
            grid=(2, columns),
            in_specs=[whole(p) for p in parts]
            + [weight_spec(0), weight_spec(1)]
            + [pl.BlockSpec((1, 2, tile), lambda half, column, place: (half, 0, column))],
            out_specs=[
                pl.BlockSpec((rows, depth), lambda half, column, place: (0, 0)),
                out_block,
                out_block,
                out_block,
            ],
        ),
        out_shape=[
            jax.ShapeDtypeStruct((rows, depth), jnp.bfloat16),
            jax.ShapeDtypeStruct((rows, 2 * piece), jnp.bfloat16),
            jax.ShapeDtypeStruct((rows, 2 * piece), jnp.float32),
            jax.ShapeDtypeStruct((rows, 2 * piece), jnp.float32),
        ],
        compiler_params=pltpu.CompilerParams(vmem_limit_bytes=60 * 2**20),
        cost_estimate=LIGHT,
        name="mix_forward",
    )(place, *parts, weights, weights, bias)


def mix_back_kernel(place_ref, grad_ref, a_ref, t_ref, *refs):
    mixed_ref, direct_ref, sums_ref = refs[-3:]
    grad = grad_ref[...]
    a = a_ref[...]
    piece = a.shape[1]
    skip = full(jnp.concatenate([ref[...] for ref in refs[:-3]], axis=1))
    opening = opening_of(t_ref[...])
    phi, bent = gelu_parts(a)
    slope = phi + a * (0.3989422804014327 * jnp.exp(-0.5 * a * a))
    grad_a = low((1.0 - opening) * slope * grad)
    grad_t = low((skip - bent) * opening * (1.0 - opening) * grad)
    mixed_ref[0, :, :piece] = grad_a
    mixed_ref[0, :, piece:] = grad_t
    direct_ref[...] = opening * grad
    sums_ref[0, :, :piece] = jnp.sum(full(grad_a), axis=0, keepdims=True)
    sums_ref[0, :, piece:] = jnp.sum(full(grad_t), axis=0, keepdims=True)


def mix_back(place, grad, a, t, joined, parts, plain, tile=LANES):
    rows, own = grad.shape
    piece = own // 2
    placed = pl.BlockSpec((rows, piece), lambda half, place: (0, place[1] ^ half))
    if plain:
        skips = [
            pl.BlockSpec((rows, tile), lambda half, place, z=z: (0, (z * 2 + (place[1] ^ half)) * parts + place[0]))
            for z in range(piece // tile)
        ]
    else:
        skips = [pl.BlockSpec((rows, piece), lambda half, place: (0, place[0] * 2 + (place[1] ^ half)))]
    return pl.pallas_call(
        mix_back_kernel,
        grid_spec=pltpu.PrefetchScalarGridSpec(
            num_scalar_prefetch=1,
            grid=(2,),
            in_specs=[placed, placed, placed] + skips,
            out_specs=[
                pl.BlockSpec((1, rows, own), lambda half, place: (half, 0, 0)),
                placed,
                pl.BlockSpec((1, 1, own), lambda half, place: (half, 0, 0)),
            ],
        ),
        out_shape=[
            jax.ShapeDtypeStruct((2, rows, own), jnp.bfloat16),
            jax.ShapeDtypeStruct((rows, own), jnp.float32),
            jax.ShapeDtypeStruct((2, 1, own), jnp.float32),
        ],
        compiler_params=pltpu.CompilerParams(vmem_limit_bytes=40 * 2**20),
        cost_estimate=LIGHT,
        name="mix_backward",
    )(place, grad, a, t, *[joined] * len(skips))


def inner_product(mixed_ref, weight_refs):
    blocks = len(weight_refs) // 2
    own = jnp.concatenate([ref[0] for ref in weight_refs[:blocks]], axis=1)
    other = jnp.concatenate([ref[0] for ref in weight_refs[blocks:]], axis=1)
    return dot_nt(mixed_ref[0], own) + dot_nt(mixed_ref[1], other)


def inner_specs(blocks, depth, tile, row_block):
    specs = []
    for flip in (0, 1):
        for z in range(blocks):
            specs.append(
                pl.BlockSpec(
                    (1, depth, tile),
                    lambda i, place, z=z, flip=flip: (2 * z + (place[1] ^ flip), row_block(i, place), 0),
                )
            )
    return specs


def inner_columns_kernel(place_ref, mixed_ref, *refs):
    out_ref = refs[-1]
    out_ref[0] = inner_product(mixed_ref, refs[:-1]).astype(out_ref.dtype)


def inner_columns(place, mixed, weights, odd, parts, dtype):
    _, rows, wide_columns = mixed.shape
    blocks, filters, tile = weights.shape
    blocks = blocks // 2
    depth = filters // parts
    return pl.pallas_call(
        inner_columns_kernel,
        grid_spec=pltpu.PrefetchScalarGridSpec(
            num_scalar_prefetch=1,
            grid=(parts // 2,),
            in_specs=[pl.BlockSpec(mixed.shape, lambda i, place: (0, 0, 0))]
            + inner_specs(blocks, depth, tile, lambda i, place: place[0] ^ (2 * i + odd)),
            out_specs=pl.BlockSpec((1, rows, depth), lambda i, place: (i, 0, 0)),
        ),
        out_shape=jax.ShapeDtypeStruct((parts // 2, rows, depth), dtype),
        compiler_params=pltpu.CompilerParams(vmem_limit_bytes=40 * 2**20),
        cost_estimate=LIGHT,
        name="inner_columns",
    )(place, mixed, *[weights] * (2 * blocks))


def inner_rows_kernel(place_ref, mixed_ref, *refs, parts, plain, tile):
    direct_ref, sent_ref, kept_ref, held_ref = refs[-4:]
    mine = place_ref[0]
    held_ref[...] = inner_product(mixed_ref, refs[:-4])

    step = pl.program_id(0)
    if plain:
        at = pl.ds(pl.multiple_of(mine * tile, tile), tile)
        column = (step % 2) * (pl.num_programs(0) // 2) + step // 2
        held_ref[:, at] += direct_ref[:, pl.ds(pl.multiple_of(column * tile, tile), tile)]
    else:

        @pl.when(step == mine)
        def _():
            held_ref[...] += direct_ref[...]

    extent = held_ref.shape[0] // parts
    for k in range(parts):
        got = held_ref[pl.ds(pl.multiple_of((mine ^ k) * extent, extent), extent), :]
        if k % 2:
            sent_ref[k // 2] = low(got)
        else:
            kept_ref[k // 2] = got


def inner_rows(place, mixed, weights, direct, parts, plain):
    _, rows, wide_columns = mixed.shape
    blocks, filters, tile = weights.shape
    blocks = blocks // 2
    depth = filters // parts
    extent = rows // parts
    out = pl.BlockSpec((parts // 2, extent, depth), lambda j, place: (0, 0, j))
    return pl.pallas_call(
        functools.partial(inner_rows_kernel, parts=parts, plain=plain, tile=tile),
        grid_spec=pltpu.PrefetchScalarGridSpec(
            num_scalar_prefetch=1,
            grid=(parts,),
            in_specs=[pl.BlockSpec(mixed.shape, lambda j, place: (0, 0, 0))]
            + inner_specs(blocks, depth, tile, lambda j, place: j)
            + [pl.BlockSpec(direct.shape, lambda j, place: (0, 0))],
            out_specs=[out, out],
            scratch_shapes=[pltpu.VMEM((rows, depth), jnp.float32)],
        ),
        out_shape=[
            jax.ShapeDtypeStruct((parts // 2, extent, filters), jnp.bfloat16),
            jax.ShapeDtypeStruct((parts // 2, extent, filters), jnp.float32),
        ],
        compiler_params=pltpu.CompilerParams(vmem_limit_bytes=40 * 2**20),
        cost_estimate=LIGHT,
        name="inner_rows",
    )(place, mixed, *[weights] * (2 * blocks), direct)


def widen_kernel(sums_ref, out_ref, *, parts):
    filters, tile = out_ref.shape[1:]
    outer = filters // (2 * parts * tile)
    for z in range(outer):
        for pair in range(2):
            for m in range(parts):
                at = ((z * 2 + pair) * parts + m) * tile
                source = filters + ((m * 2 + pair) * outer + z) * tile
                out_ref[0, at : at + tile, :] = sums_ref[:, at : at + tile].T
                out_ref[1, at : at + tile, :] = sums_ref[:, source : source + tile].T


def widen(sums, filters, parts):
    return pl.pallas_call(
        functools.partial(widen_kernel, parts=parts),
        out_shape=jax.ShapeDtypeStruct((2, filters, sums.shape[0]), jnp.float32),
        compiler_params=pltpu.CompilerParams(vmem_limit_bytes=16 * 2**20),
        cost_estimate=LIGHT,
        name="widen",
    )(sums)


def slope_of(values):
    phi = 0.5 * (1.0 + lax.erf(values * 0.7071067811865476))
    return phi + values * (0.3989422804014327 * jnp.exp(-0.5 * values * values))


def weight_copies(part_refs, up_ref, down_ref, bias_ref, sems):
    units = up_ref.shape[1]
    copies = []
    for k, part in enumerate(part_refs):
        last = part.shape[0] - 16
        copies.append(
            (
                pltpu.make_async_copy(part.at[pl.ds(0, units)], up_ref.at[k], sems.at[3 * k]),
                pltpu.make_async_copy(part.at[pl.ds(units, units)], down_ref.at[k], sems.at[3 * k + 1]),
                pltpu.make_async_copy(part.at[pl.ds(last, 16)], bias_ref.at[k], sems.at[3 * k + 2]),
            )
        )
    for part_copies in copies:
        for copy in part_copies:
            copy.start()
    return copies


def ffn_forward_kernel(x_ref, *refs, tile):
    part_refs, (out_ref, own_ref, up_ref, down_ref, bias_ref, sems) = refs[:-6], refs[-6:]
    copies = weight_copies(part_refs, up_ref, down_ref, bias_ref, sems)
    for k, part_copies in enumerate(copies):
        for copy in part_copies:
            copy.wait()
        for first in range(0, x_ref.shape[0], tile):
            at = slice(first, first + tile)
            value = jnp.dot(x_ref[at, :], up_ref[k], preferred_element_type=jnp.float32)
            active = low(gelu_parts(value + full(bias_ref[k, 0:1, :]))[1])
            added = jnp.dot(active, down_ref[k], preferred_element_type=jnp.float32)
            if k == 0:
                out_ref[at, :] = added
                own_ref[at, :] = active
            else:
                out_ref[at, :] += added


def ffn_call(kernel, operands, parts, units, outs, name):
    width = parts[0].shape[1]
    vmem = pl.BlockSpec(memory_space=pltpu.VMEM)
    return pl.pallas_call(
        kernel,
        in_specs=[vmem] * len(operands) + [pl.BlockSpec(memory_space=pl.ANY)] * len(parts),
        out_specs=[vmem] * len(outs),
        out_shape=outs,
        scratch_shapes=[
            pltpu.VMEM((len(parts), units, width), jnp.bfloat16),
            pltpu.VMEM((len(parts), units, width), jnp.bfloat16),
            pltpu.VMEM((len(parts), 16, width), jnp.bfloat16),
            pltpu.SemaphoreType.DMA((3 * len(parts),)),
        ],
        compiler_params=pltpu.CompilerParams(vmem_limit_bytes=40 * 2**20),
        cost_estimate=LIGHT,
        name=name,
    )(*operands, *parts)


def ffn_forward(x, parts, units, tile=256):
    rows, width = x.shape
    outs = [
        jax.ShapeDtypeStruct((rows, width), jnp.float32),
        jax.ShapeDtypeStruct((rows, units), jnp.bfloat16),
    ]
    kernel = functools.partial(ffn_forward_kernel, tile=tile)
    return ffn_call(kernel, [x], parts, units, outs, "ffn_forward")


def ffn_backward_kernel(x_ref, grad_ref, *refs, tile):
    part_refs, (out_ref, own_ref, sums_ref, up_ref, down_ref, bias_ref, sems) = refs[:-7], refs[-7:]
    copies = weight_copies(part_refs, up_ref, down_ref, bias_ref, sems)
    sums = jnp.zeros(sums_ref.shape, jnp.float32)
    for k, part_copies in enumerate(copies):
        for copy in part_copies:
            copy.wait()
        for first in range(0, x_ref.shape[0], tile):
            at = slice(first, first + tile)
            value = jnp.dot(x_ref[at, :], up_ref[k], preferred_element_type=jnp.float32)
            value = value + full(bias_ref[k, 0:1, :])
            inner = low(dot_nt(grad_ref[at, :], down_ref[k]) * slope_of(value))
            added = dot_nt(inner, up_ref[k])
            if k == 0:
                out_ref[at, :] = added
                own_ref[at, :] = inner
                sums = sums + jnp.sum(full(inner), axis=0, keepdims=True)
            else:
                out_ref[at, :] += added
    sums_ref[...] = sums


def ffn_backward(x, parts, units, grad, tile=256):
    rows, width = x.shape
    outs = [
        jax.ShapeDtypeStruct((rows, width), jnp.float32),
        jax.ShapeDtypeStruct((rows, units), jnp.bfloat16),
        jax.ShapeDtypeStruct((1, units), jnp.float32),
    ]
    kernel = functools.partial(ffn_backward_kernel, tile=tile)
    return ffn_call(kernel, [x, grad], parts, units, outs, "ffn_backward")


def masked_scores(query_heads, key_heads, keep_mask, score_scale):
    scores = (
        jnp.einsum("qhd,khd->hqk", query_heads, key_heads, preferred_element_type=jnp.float32)
        * score_scale
    )
    return jnp.where(keep_mask[None, None, :] == 1, scores, NEG_FILL)


def attend(query_heads, key_heads, value_heads, keep_mask, score_scale):
    scores = masked_scores(query_heads, key_heads, keep_mask, score_scale)
    row_peak = jnp.max(scores, axis=-1, keepdims=True)
    raised = jnp.exp(scores - row_peak)
    row_total = jnp.sum(raised, axis=-1, keepdims=True)
    attn_weights = (raised / row_total).astype(jnp.bfloat16)
    context = jnp.einsum(
        "hqk,khd->qhd", attn_weights, value_heads, preferred_element_type=jnp.float32
    )
    return (context.astype(jnp.bfloat16), row_peak, row_total)


def attend_back(
    query_heads, key_heads, value_heads, keep_mask, row_peak, row_total, grad_context, score_scale
):
    scores = masked_scores(query_heads, key_heads, keep_mask, score_scale)
    probs_full = jnp.exp(scores - row_peak) / row_total
    attn_weights = probs_full.astype(jnp.bfloat16)
    grad_value = jnp.einsum(
        "hqk,qhd->khd", attn_weights, grad_context, preferred_element_type=jnp.float32
    )
    grad_weights = jnp.einsum(
        "qhd,khd->hqk", grad_context, value_heads, preferred_element_type=jnp.float32
    )
    inner_sum = jnp.sum(grad_weights * probs_full, axis=-1, keepdims=True)
    grad_scores = (probs_full * (grad_weights - inner_sum)).astype(jnp.bfloat16)
    grad_query = (
        jnp.einsum("hqk,khd->qhd", grad_scores, key_heads, preferred_element_type=jnp.float32)
        * score_scale
    )
    grad_key = (
        jnp.einsum("hqk,qhd->khd", grad_scores, query_heads, preferred_element_type=jnp.float32)
        * score_scale
    )
    return (
        grad_query.astype(jnp.bfloat16),
        grad_key.astype(jnp.bfloat16),
        grad_value.astype(jnp.bfloat16),
    )


def per_device(
    char_ids,
    char_mask,
    position_ids,
    type_ids,
    key_mask,
    char_table,
    conv_weight,
    conv_bias,
    highway_weight,
    highway_bias,
    proj_weight,
    proj_bias,
    position_table,
    type_table,
    embed_gain,
    embed_shift,
    qkv_weight,
    qv_bias,
    out_weight,
    out_bias,
    ln1_gain,
    ln1_shift,
    up_weight,
    up_bias,
    down_weight,
    down_bias,
    ln2_gain,
    ln2_shift,
    cotangent,
):
    n_wide, n_narrow = lax.axis_size("wide"), lax.axis_size("narrow")
    half_wide = n_wide // 2
    me_narrow = lax.axis_index("narrow")
    wide_bits, narrow_bits = bits_of("wide"), bits_of("narrow")
    every_bit = narrow_bits + wide_bits
    falling = every_bit[::-1]
    word_total, letters = char_ids.shape
    tap_rows, own_filters = conv_weight.shape
    char_depth = char_table.shape[1]
    tap_count = tap_rows // char_depth
    filters = highway_weight.shape[1]
    own_mix = highway_weight.shape[2]
    own_width = proj_weight.shape[1]
    seq_length = position_table.shape[0]
    group = word_total * n_narrow
    own_hidden = half_wide * own_mix

    outer = n_wide // 2
    quarter = outer // 2
    outer_groups = [[2 * z + y for z in range(outer)] for y in range(2)]
    me_pair = my_bit("wide", 0)

    def grouped(item):
        split = item.reshape((quarter, 2, n_narrow, own_mix) + item.shape[1:])
        return split.transpose((2, 1, 0, 3) + tuple(range(4, split.ndim))).reshape(item.shape)

    def ungrouped(item):
        split = item.reshape((n_narrow, 2, quarter, own_mix) + item.shape[1:])
        return split.transpose((2, 1, 0, 3) + tuple(range(4, split.ndim))).reshape(item.shape)

    tiled = own_mix == LANES
    corner = jnp.stack([me_narrow, me_pair]).astype(jnp.int32)

    def gather_mix(shard):
        blocks = lax.all_gather(shard, "wide", axis=0)
        if tiled:
            return blocks
        blocks = blocks.reshape(-1, LANES // own_mix, 2, filters, own_mix).transpose(0, 2, 3, 1, 4)
        return blocks.reshape(-1, filters, LANES)

    plain = tiled and half_wide == n_narrow
    ordered, unordered = (lambda item: item, lambda item: item) if plain else (grouped, ungrouped)
    mix_weights = [gather_mix(ordered(highway_weight[0]))]
    mix_weights.append(gather_mix(after(grouped(highway_weight[1]), mix_weights[0])))
    conv_block = jnp.zeros((own_filters, LANES), jnp.bfloat16)
    conv_block = conv_block.at[:, :tap_rows].set(conv_weight.T)
    conv_block = conv_block.at[:, tap_rows + tap_count].set(conv_bias)
    bias_block = jnp.pad(highway_bias, ((0, 0), (0, LANES - own_mix)))
    conv_spread = spread(jnp.concatenate([conv_block, bias_block]), falling)
    filt_rows = ordered(conv_spread[:, :own_filters].reshape(filters, LANES))
    mix_bias = conv_spread[:, own_filters:, :own_mix].reshape(outer, 2, n_narrow, 2, own_mix)
    mix_bias = full(lax.dynamic_index_in_dim(mix_bias, me_narrow, 2, keepdims=False))
    mix_bias = [lax.dynamic_index_in_dim(mix_bias, me_pair ^ half, 1, keepdims=False) for half in range(2)]
    mix_bias = jnp.stack(mix_bias).transpose(2, 0, 1, 3).reshape(2, 2, 2, quarter * own_mix)
    vector_block = jnp.stack([proj_bias, type_table[0], type_table[1], embed_gain, embed_shift], axis=1)
    vector_block = jnp.pad(vector_block, ((0, 0), (0, LANES - vector_block.shape[1])))
    rest = jnp.concatenate([grouped(proj_weight).T, position_table.T, vector_block], axis=1)[None]
    rest_bits = wide_bits[::-1]
    rest = doubled(rest, *rest_bits[0], 1).reshape((-1,) + rest.shape[1:])
    widths = ordered(filter_widths(filters))
    lane = jnp.arange(LANES)
    tap_keep = (lane[None, :] // char_depth) < widths[:, None]
    late = lane - tap_rows
    shut = (late == 0)[None, :] | (
        (late >= 1)[None, :] & (late < tap_count)[None, :] & (widths[:, None] > late[None, :])
    )
    is_bias = (late == tap_count)[None, :]
    filt_rows = jnp.where(
        (tap_keep & (late < 0)[None, :]) | is_bias,
        filt_rows,
        jnp.where(shut, jnp.bfloat16(SHUT), jnp.bfloat16(0.0)),
    )
    vocab = char_table.shape[0]
    vocab_rows = -(-vocab // 16) * 16
    id_row = char_ids.T.reshape(1, letters * word_total)
    hot = (jnp.arange(vocab_rows)[:, None] == id_row).astype(jnp.bfloat16)
    table_t = jnp.pad(char_table, ((0, vocab_rows - vocab), (0, 0))).T
    embedded = low(jnp.dot(table_t, hot, preferred_element_type=jnp.float32))
    embedded = jnp.pad(embedded, ((0, 0), (0, tap_count * word_total)))
    span = letters * word_total
    tap_blocks = [embedded[:, t * word_total : t * word_total + span] for t in range(tap_count)]
    place = jnp.arange(letters)
    usable = (char_mask == 1) | (place[None, :] == 0)
    unusable_row = low(~usable).T.reshape(1, span)
    late_rows = low(place[None, :] == letters - jnp.arange(1, tap_count)[:, None])
    late_rows = jnp.repeat(late_rows, word_total, axis=1)
    columns_t = jnp.concatenate(
        tap_blocks
        + [
            unusable_row,
            late_rows,
            jnp.ones((1, span), jnp.bfloat16),
            jnp.zeros((LANES - tap_rows - tap_count - 1, span), jnp.bfloat16),
        ]
    )
    columns = columns_t.T.reshape(letters, word_total, LANES)
    tally = jnp.stack(
        [jnp.sum(full(usable[:, : letters - w + 1]), axis=1) for w in range(1, tap_count + 1)], axis=1
    )
    width_hot = full(jnp.arange(1, tap_count + 1)[:, None] == widths[None, :])
    valid_count = jnp.dot(tally, width_hot)

    def rest_step(rest, which):
        return doubled(rest, *which, 1).reshape((-1,) + rest.shape[1:])

    rest = after(rest, conv_spread)
    for which in rest_bits[1:-1]:
        rest = rest_step(rest, which)
    units = up_weight.shape[1]
    encoder_pack = jnp.concatenate(
        [up_weight, down_weight, out_weight, jnp.broadcast_to(up_bias[None], (16, units))]
    )
    encoder_parts = [encoder_pack, swap(encoder_pack, "narrow", 1)]
    filt_rows, encoder_parts = lax.optimization_barrier((filt_rows, encoder_parts))
    lse = pool_forward(columns, filt_rows)
    rest = rest_step(after(rest, lse), rest_bits[-1])
    pooled = lse - jnp.log(valid_count)
    features = low(smooth_gelu(pooled))

    parts = near_parts(features, "narrow")
    near_order = [0, 2, 1, 3]
    cotangent_rows = lax.all_gather(
        after(cotangent, mix_weights[1]), "narrow", axis=0, tiled=True
    )
    rest = after(rest, parts[-1])

    def narrowed(rest, bit):
        width = own_hidden << bit
        mine = my_bit("narrow", bit)
        tail = rest[..., 2 * width :]
        kept = lax.dynamic_slice_in_dim(rest, mine * width, width, rest.ndim - 1)
        sent = lax.dynamic_slice_in_dim(rest, (1 - mine) * width, width, rest.ndim - 1)
        kept, sent = (jnp.concatenate([item, tail], axis=-1) for item in (kept, sent))
        got = swap(sent, "narrow", bit)
        high = mine == 1
        pair = jnp.stack([jnp.where(high, got, kept), jnp.where(high, kept, got)], axis=1)
        return pair.reshape((-1,) + pair.shape[2:])

    rest = narrowed(rest, 1)
    highway_saved, pair_parts = [], [swap(features, "wide", 0)]
    for layer_index in range(2):
        joined, hidden, kept_a, kept_t = mix_forward(
            corner, parts, mix_weights[layer_index], mix_bias[layer_index], layer_index == 0, plain and layer_index == 0
        )
        highway_saved.append((joined, kept_a, kept_t))
        if layer_index == 0:
            parts = near_parts(hidden, "narrow")
            pair_parts.append(swap(hidden, "wide", 0))
            rest = narrowed(after(rest, hidden), 0)
            encoder_parts = encoder_parts + [
                swap(item, "narrow", 0) for item in after(encoder_parts, hidden)
            ]
            encoder_vectors = [
                full(item) for item in (out_bias, ln1_gain, ln1_shift, down_bias, ln2_gain, ln2_shift, qv_bias)
            ]
            parts, encoder_parts, rest, encoder_vectors = lax.optimization_barrier(
                (parts, encoder_parts, rest, encoder_vectors)
            )
    proj_input = hidden
    rest = rest.reshape(n_wide * n_narrow * own_width, -1)
    model_width = rest.shape[0]
    proj_own = rest[:, :own_hidden]
    position_rows = rest[:, own_hidden : own_hidden + seq_length]
    vectors = full(rest[:, own_hidden + seq_length :].T)
    proj_shift, type_low, type_high, first_gain, first_shift = (vectors[i] for i in range(5))
    projected = fold(dot_nt(proj_input, proj_own).reshape(n_narrow, word_total, model_width), narrow_bits)
    projected, cotangent_rows = lax.optimization_barrier((projected, cotangent_rows))
    position_hot = (position_ids[:, None] == jnp.arange(seq_length)[None, :]).astype(jnp.bfloat16)
    type_rows = jnp.where(type_ids[:, None] == 1, type_high, type_low)
    summed = projected + proj_shift + dot_nt(position_hot, position_rows) + type_rows
    first_state, first_pull = jax.vjp(layer_norm, summed, first_gain, first_shift)

    out_bias, ln1_gain, ln1_shift, down_bias, ln2_gain, ln2_shift, qv_bias = encoder_vectors
    gathered = lax.all_gather(low(first_state), "narrow", axis=0, tiled=True)
    group_rows = gathered.shape[0]
    qkv_out = jnp.einsum("gd,kdc->kgc", gathered, qkv_weight, preferred_element_type=jnp.float32)
    local_width = qkv_out.shape[2]
    head_count = local_width // HEAD_DIM
    seq_shape = (group_rows, head_count, HEAD_DIM)
    query_heads = low(qkv_out[0] + qv_bias[0]).reshape(seq_shape)
    key_heads = low(qkv_out[1]).reshape(seq_shape)
    value_heads = low(qkv_out[2] + qv_bias[1]).reshape(seq_shape)
    score_scale = HEAD_DIM ** (-0.5)
    keep_mask = key_mask[0]
    context, row_peak, row_total = attend(query_heads, key_heads, value_heads, keep_mask, score_scale)
    context_rows = context.reshape(group_rows, local_width)

    def by_owner(partial):
        return fold(partial.reshape(n_narrow, word_total, model_width), narrow_bits)

    def own_words(rows):
        return lax.dynamic_slice_in_dim(rows, me_narrow * word_total, word_total, 0)

    attn_branch = out_bias
    for k, part in zip(near_order, near_parts(context_rows, "narrow")):
        weight = encoder_parts[k][2 * units : 2 * units + local_width]
        attn_branch = attn_branch + jnp.dot(part, weight, preferred_element_type=jnp.float32)
    second_state, second_pull = jax.vjp(
        layer_norm, full(gathered) + attn_branch, ln1_gain, ln1_shift
    )
    pair_parts, ffn_input = lax.optimization_barrier((pair_parts, low(second_state)))
    ffn_branch, activated = ffn_forward(ffn_input, encoder_parts, units)
    layer_out, third_pull = jax.vjp(
        layer_norm, second_state + (ffn_branch + down_bias), ln2_gain, ln2_shift
    )
    layer_out = own_words(layer_out)

    def pair_start(halves):
        kept = lax.dynamic_index_in_dim(halves, me_pair, 0, keepdims=False)
        sent = lax.dynamic_index_in_dim(halves, 1 - me_pair, 0, keepdims=False)
        return kept, swap(sent, "wide", 0)

    def pair_end(mine, back):
        first = me_pair == 0
        return jnp.stack([full(jnp.where(first, mine, back)), full(jnp.where(first, back, mine))])

    grad_third, grad_ln2_gain, grad_ln2_shift = third_pull(cotangent_rows)
    grad_ffn = low(grad_third)
    grad_down_bias = jnp.sum(full(grad_ffn), axis=0)
    grad_down_weight = jnp.einsum("gf,gd->fd", activated, grad_ffn, preferred_element_type=jnp.float32)
    grad_inner, grad_up, grad_up_bias = ffn_backward(ffn_input, encoder_parts, units, grad_ffn)
    grad_up_weight = jnp.einsum("gd,gf->df", ffn_input, grad_up, preferred_element_type=jnp.float32)
    grad_second = grad_third + grad_inner
    ffn_kept, ffn_received = pair_start(jnp.stack([low(grad_up_weight), low(grad_down_weight)]))
    grad_first_branch, grad_ln1_gain, grad_ln1_shift = second_pull(grad_second)
    pair_parts = [near_parts(after(item, ffn_branch), "narrow") for item in pair_parts]
    pair_parts, grad_attn = lax.optimization_barrier((pair_parts, low(grad_first_branch)))
    pair_joined = [
        in_order(item, "narrow", layer_index) for layer_index, item in enumerate(pair_parts)
    ]
    grad_out_bias = jnp.sum(full(grad_attn), axis=0)
    grad_attn_rows = grad_attn
    grad_out_weight = jnp.einsum(
        "gc,gd->cd", context_rows, grad_attn_rows, preferred_element_type=jnp.float32
    )
    grad_context = low(dot_nt(grad_attn_rows, out_weight)).reshape(seq_shape)
    grad_query, grad_key, grad_value = attend_back(
        query_heads, key_heads, value_heads, keep_mask, row_peak, row_total, grad_context, score_scale
    )
    grad_joined = jnp.stack(
        [item.reshape(group_rows, local_width) for item in (grad_query, grad_key, grad_value)]
    )
    grad_qv_bias = jnp.stack(
        [jnp.sum(full(grad_joined[0]), axis=0), jnp.sum(full(grad_joined[2]), axis=0)]
    )
    grad_qkv_weight = jnp.einsum(
        "kgc,gd->kcd", grad_joined, gathered, preferred_element_type=jnp.float32
    )
    attn_kept, attn_received = pair_start(
        jnp.concatenate([low(grad_qkv_weight), low(grad_out_weight)[None]]).reshape(2, -1, model_width)
    )
    grad_first = own_words(grad_first_branch) + by_owner(
        jnp.einsum("kgc,kdc->gd", grad_joined, qkv_weight, preferred_element_type=jnp.float32)
    )
    grad_summed, grad_embed_gain, grad_embed_shift = first_pull(grad_first)

    grad_proj_low = low(grad_summed)
    grad_position = jnp.einsum(
        "td,tl->dl", grad_proj_low, position_hot, preferred_element_type=jnp.float32
    )
    is_high = type_ids[:, None] == 1
    vector_grads = jnp.stack(
        [
            jnp.sum(full(grad_proj_low), axis=0),
            jnp.sum(jnp.where(is_high, 0.0, grad_summed), axis=0),
            jnp.sum(jnp.where(is_high, grad_summed, 0.0), axis=0),
            grad_embed_gain,
            grad_embed_shift,
        ],
        axis=1,
    )
    vector_grads = jnp.pad(low(vector_grads), ((0, 0), (0, LANES - vector_grads.shape[1])))
    grad_proj_rows = lax.all_gather(grad_proj_low, "narrow", axis=0, tiled=True)
    grad_proj_weight = jnp.einsum(
        "gd,gh->dh", grad_proj_rows, proj_input, preferred_element_type=jnp.float32
    )
    grad_hidden = jnp.dot(grad_proj_rows, proj_own, preferred_element_type=jnp.float32)

    mix_bias_grads = [None, None]

    def weight_part(joined, mixed):
        return jnp.einsum(
            "tk,tzc->zck",
            joined,
            mixed.reshape(group, outer, own_mix),
            preferred_element_type=jnp.float32,
        )

    def pair_weight(layer_index, mixed, met):
        joined = highway_saved[layer_index][0]
        return low(weight_part(joined, mixed[0]) + weight_part(pair_joined[layer_index], met))

    ffn_received, attn_received = after((ffn_received, attn_received), grad_hidden)
    pair_sums = lax.psum(
        (low(full(ffn_kept) + full(ffn_received)), low(full(attn_kept) + full(attn_received))),
        "wide",
        axis_index_groups=outer_groups,
    )
    joined, kept_a, kept_t = highway_saved[1]
    mixed, direct, mix_bias_grads[1] = mix_back(corner, grad_hidden, kept_a, kept_t, joined, n_narrow, False)
    met = swap(mixed[1], "wide", 0)
    sent = inner_columns(corner, mixed, mix_weights[1], 1, n_narrow, jnp.bfloat16)
    kept = inner_columns(corner, mixed, mix_weights[1], 0, n_narrow, jnp.float32)
    table_grads = [
        item.reshape(n_wide, n_narrow, own_width, -1).transpose(1, 0, 2, 3)
        for item in after((low(grad_position), vector_grads, low(grad_proj_weight)), kept)
    ]
    table_grads = jnp.concatenate(table_grads, axis=3)
    table_grads = lax.all_to_all(table_grads, "narrow", 0, 0, tiled=True)
    table_width = seq_length + LANES
    table_sums = jnp.sum(full(table_grads[..., :table_width]), axis=0)
    proj_parts = table_grads[..., table_width:].transpose(1, 0, 2, 3)
    rest_grads = [item.reshape(n_wide, LANES, -1) for item in (low(table_sums), proj_parts)]
    table_columns = rest_grads[0].shape[2]
    rest_grads = jnp.concatenate(rest_grads, axis=2)
    grad_hidden = direct + fold_near(sent, kept, "narrow")
    weight_second = pair_weight(1, mixed, after(met, grad_hidden))
    joined, kept_a, kept_t = highway_saved[0]
    mixed, direct, mix_bias_grads[0] = mix_back(corner, grad_hidden, kept_a, kept_t, joined, n_narrow, plain)
    met = swap(mixed[1], "wide", 0)
    sent, kept = inner_rows(corner, mixed, mix_weights[0], direct, n_narrow, plain)
    grad_features = fold_near(sent, kept, "narrow")

    rest_grads = low(halved(rest_grads, *wide_bits[0]))
    weight_first = pair_weight(0, mixed, met)
    both = [item.reshape(outer, LANES, -1) for item in (weight_first, weight_second)]
    weight_columns = both[0].shape[2]
    both = jnp.concatenate(both + [rest_grads], axis=2)
    grad_features, both, pair_sums = lax.optimization_barrier((grad_features, both, pair_sums))

    grad_pooled = jax.vjp(smooth_gelu, pooled)[1](grad_features)[0]
    filt_grads, hot_grads = pool_backward(
        columns, columns_t, hot, filt_rows, lse, grad_pooled, char_depth, tap_count
    )
    both = lax.psum_scatter(both, "wide", scatter_dimension=0, axis_index_groups=outer_groups)
    both = full(both)
    if plain:
        owned_highway = widen(both, filters, n_narrow)
    else:
        owned_highway = [
            both[:, at * weight_columns : (at + 1) * weight_columns].reshape(own_mix, filters).T
            for at in range(2)
        ]
        owned_highway = jnp.stack([unordered(owned_highway[0]), ungrouped(owned_highway[1])])
    owned_rest = both[:, 2 * weight_columns :]
    table_grads = owned_rest[:, :table_columns].reshape(own_width, table_width)
    owned_proj = owned_rest[:, table_columns:].reshape(n_narrow, own_width, own_hidden).transpose(0, 2, 1)
    owned_proj = ungrouped(owned_proj.reshape(filters, own_width))
    filt_grads = unordered(low(jnp.where(tap_keep | is_bias, filt_grads, 0.0)))
    grad_table = hot_grads[:vocab, :tap_rows].reshape(vocab, tap_count, char_depth).sum(axis=1)
    mix_bias_grads = jnp.stack(mix_bias_grads).reshape(2, 2, outer, own_mix)
    swapped = jnp.stack([jnp.where(me_pair == 0, mix_bias_grads[:, y], mix_bias_grads[:, 1 - y]) for y in range(2)], axis=2)
    mix_bias_grads = swapped.reshape(2, n_wide, own_mix)
    wide_parts = [
        mix_bias_grads,
        grad_up_bias[0],
        grad_qv_bias,
        grad_out_bias,
        grad_ln1_gain,
        grad_ln1_shift,
        grad_down_bias,
        grad_ln2_gain,
        grad_ln2_shift,
    ]
    all_parts = [grad_table]

    def joined_rows(parts):
        flat = jnp.concatenate([item.reshape(-1) for item in parts])
        return jnp.pad(flat, (0, -flat.shape[0] % LANES)).reshape(-1, LANES)

    def parted(flat, parts):
        flat, done, start = flat.reshape(-1), [], 0
        for item in parts:
            done.append(flat[start : start + item.size].reshape(item.shape))
            start += item.size
        return done

    wide_flat, all_flat = joined_rows(wide_parts), joined_rows(all_parts)
    flat = total(jnp.concatenate([wide_flat, all_flat]), wide_bits[:1])
    filt_grads = halved(filt_grads.reshape(n_wide, -1, LANES), *wide_bits[0])
    flat, filt_grads = lax.optimization_barrier((flat, filt_grads))
    filt_grads = fold(filt_grads, wide_bits[1:])
    owned_filt = lax.all_to_all(
        low(filt_grads).reshape(n_narrow, own_filters, LANES), "narrow", 0, 0, tiled=True
    )
    owned_filt = jnp.sum(full(owned_filt), axis=0)
    owned_conv = owned_filt[:, :tap_rows].T
    owned_conv_bias = owned_filt[:, tap_rows + tap_count]

    flat, pair_backs = lax.optimization_barrier(
        (total(flat, wide_bits[1:]), [swap(item, "wide", 0) for item in pair_sums])
    )
    (
        mix_sums,
        sum_up_bias,
        sum_qv_bias,
        sum_out_bias,
        sum_ln1_gain,
        sum_ln1_shift,
        sum_down_bias,
        sum_ln2_gain,
        sum_ln2_shift,
    ) = parted(flat[: wide_flat.shape[0]], wide_parts)
    owned_mix_bias = lax.dynamic_index_in_dim(mix_sums, lax.axis_index("wide"), 1, keepdims=False)
    sum_table = parted(total(flat[wide_flat.shape[0] :], narrow_bits), all_parts)[0]
    ffn_sums, attn_sums = (pair_end(mine, back) for mine, back in zip(pair_sums, pair_backs))
    attn_sums = attn_sums.reshape(n_narrow, local_width, model_width)
    owned_vectors = table_grads[:, seq_length : seq_length + 5].T
    return (
        layer_out,
        sum_table,
        owned_conv,
        owned_conv_bias,
        owned_highway,
        owned_mix_bias,
        owned_proj,
        owned_vectors[0],
        table_grads[:, :seq_length].T,
        owned_vectors[1:3],
        owned_vectors[3],
        owned_vectors[4],
        attn_sums[:3].transpose(0, 2, 1),
        sum_qv_bias,
        attn_sums[3],
        sum_out_bias,
        sum_ln1_gain,
        sum_ln1_shift,
        ffn_sums[0],
        sum_up_bias,
        ffn_sums[1],
        sum_down_bias,
        sum_ln2_gain,
        sum_ln2_shift,
    )


def solution(mesh):
    return jax.shard_map(
        per_device,
        mesh=mesh,
        in_specs=(
            P(("wide", "narrow"), None),
            P(("wide", "narrow"), None),
            P(("wide", "narrow")),
            P(("wide", "narrow")),
            P("wide", None),
            P(),
            P(None, ("wide", "narrow")),
            P(("wide", "narrow")),
            P(None, None, ("wide", "narrow")),
            P(None, ("wide", "narrow")),
            P(None, ("wide", "narrow")),
            P(("wide", "narrow")),
            P(None, ("wide", "narrow")),
            P(None, ("wide", "narrow")),
            P(("wide", "narrow")),
            P(("wide", "narrow")),
            P(None, None, "narrow"),
            P(None, "narrow"),
            P("narrow", None),
            P(),
            P(),
            P(),
            P(None, "narrow"),
            P("narrow"),
            P("narrow", None),
            P(),
            P(),
            P(),
            P(("wide", "narrow"), None),
        ),
        out_specs=(
            P(("wide", "narrow"), None),
            P(),
            P(None, ("wide", "narrow")),
            P(("wide", "narrow")),
            P(None, None, ("wide", "narrow")),
            P(None, ("wide", "narrow")),
            P(None, ("wide", "narrow")),
            P(("wide", "narrow")),
            P(None, ("wide", "narrow")),
            P(None, ("wide", "narrow")),
            P(("wide", "narrow")),
            P(("wide", "narrow")),
            P(None, None, "narrow"),
            P(None, "narrow"),
            P("narrow", None),
            P(),
            P(),
            P(),
            P(None, "narrow"),
            P("narrow"),
            P("narrow", None),
            P(),
            P(),
            P(),
        ),
        check_vma=False,
    )
```
